32 devices in a mesh: fsdp: 32 (over z, y, x, core).
Axes of the slice: x: 2, y: 2, z: 4, core: 2. Of those that a mesh axis runs over, the one named last changes fastest.
Arguments:
- layer_in: bfloat16 [20480, 1280], P('fsdp'), may hold values from -6 to 6
- out_grad: bfloat16 [20480, 1280], P('fsdp'), may hold values from -6 to 6
- segment_ids: int32 [20480], P('fsdp'), may hold values from 0 to 51, as said below
- segment_parents: int32 [52], replicated, may hold values from 0 to 43, as said below
- norm_gain1: bfloat16 [1280], P('fsdp'), may hold values from 0.5 to 1.5
- w_query: bfloat16 [1280, 1280], P('fsdp'), may hold values from -0.15625 to 0.15625
- w_key: bfloat16 [1280, 320], P('fsdp'), may hold values from -0.15625 to 0.15625
- w_value: bfloat16 [1280, 320], P('fsdp'), may hold values from -0.15625 to 0.15625
- w_output: bfloat16 [1280, 1280], P(None, 'fsdp'), may hold values from -4 to 4
- norm_gain2: bfloat16 [1280], P('fsdp'), may hold values from 0.5 to 1.5
- w_gate: bfloat16 [1280, 3584], P('fsdp'), may hold values from -0.15625 to 0.15625
- w_up: bfloat16 [1280, 3584], P('fsdp'), may hold values from -0.15625 to 0.15625
- w_down: bfloat16 [3584, 1280], P(None, 'fsdp'), may hold values from -0.09375 to 0.09375
Outputs:
- layer_out: bfloat16 [20480, 1280], P('fsdp')
- input_grad: float32 [20480, 1280], P('fsdp')
- grad_norm_gain1: float32 [1280], P('fsdp')
- grad_w_query: float32 [1280, 1280], P('fsdp')
- grad_w_key: float32 [1280, 320], P('fsdp')
- grad_w_value: float32 [1280, 320], P('fsdp')
- grad_w_output: float32 [1280, 1280], P(None, 'fsdp')
- grad_norm_gain2: float32 [1280], P('fsdp')
- grad_w_gate: float32 [1280, 3584], P('fsdp')
- grad_w_up: float32 [1280, 3584], P('fsdp')
- grad_w_down: float32 [3584, 1280], P(None, 'fsdp')
The draws below stay inside these ranges and needn't reach their ends.
Inputs may be any that keep to these rules, and one draw needn't show every extreme that they name: `segment_ids`: tree k holds rows k * 5120 to (k + 1) * 5120 - 1 and segments k * 13 to (k + 1) * 13 - 1 in rising order: first its trunk, then 4 branches, then 2 * 4 leaves; every segment has at least one token. `segment_parents`: A trunk's parent is itself, each branch's parent is its tree's trunk, each leaf's parent is one of its tree's branches, and every branch is the parent of exactly two leaves.
All inputs are finite; a program needn't handle non-finite values.
Results may differ from the reference program's by a relative error of at most 0.014.
Values may be sent and summed in bfloat16 or wider, within the bound.
No kernel may reach another device: no remote copies, remote signals or barrier semaphores. Data moves between devices by JAX's collectives and lax.ppermute only.
A program may use at most 320 MiB of HBM per device.

```python
import math
import jax
import jax.numpy as jnp
from jax import lax

D = 1280
HEADS = 20
KV_HEADS = 5
HEAD = 64
FF = 3584
TOK_DEV = 640
TREE = 5120
BRANCHES = 4
SEG_TREE = 13
TREES = 4
TOKENS = 20480


def draw_segment_ids(key, part):
    key = jax.random.fold_in(key, 11)
    trunk_key, jitter_key = jax.random.split(key)
    trunk_len = jax.random.randint(trunk_key, (TREES,), 3 * TREE // 10, TREE // 2 + 1)
    others = 3 * BRANCHES
    rest_len = TREE - trunk_len
    base_len = rest_len // others
    reach_len = base_len // 4
    jitter = jax.random.randint(jitter_key, (TREES, others // 2), -reach_len[:, None], reach_len[:, None] + 1)
    paired = jnp.stack([base_len[:, None] + jitter, base_len[:, None] - jitter], axis=2).reshape(TREES, others)
    paired = paired.at[:, others - 1].add(rest_len - others * base_len)
    lengths = jnp.concatenate([trunk_len[:, None], paired], axis=1)
    starts = jnp.cumsum(lengths, axis=1) - lengths
    places = jnp.arange(TREE, dtype=jnp.int32)
    local_ids = jnp.sum((places[None, None, :] >= starts[:, :, None]).astype(jnp.int32), axis=1) - 1
    tree_base = jnp.arange(TREES, dtype=jnp.int32)[:, None] * SEG_TREE
    return (local_ids + tree_base).reshape(TREES * TREE).astype(jnp.int32)


def leaf_permutation(tree_key):
    return jax.random.permutation(tree_key, 2 * BRANCHES)


def draw_segment_parents(key, part):
    key = jax.random.fold_in(key, 29)
    tree_keys = jax.random.split(key, TREES)
    leaf_order = jax.vmap(leaf_permutation)(tree_keys).astype(jnp.int32)
    root_ids = jnp.arange(TREES, dtype=jnp.int32)[:, None] * SEG_TREE
    branch_parent = jnp.zeros((TREES, BRANCHES), jnp.int32) + root_ids
    leaf_parent = root_ids + 1 + leaf_order // 2
    return jnp.concatenate([root_ids, branch_parent, leaf_parent], axis=1).reshape(TREES * SEG_TREE).astype(jnp.int32)


def with_spikes(drawn, own_key, source, target, shards_of, factor):
    def block_of(position):
        return (jnp.arange(drawn.shape[position]) // (drawn.shape[position] // shards_of)).reshape((-1,) + (1,) * (drawn.ndim - 1 - position))

    first = jax.random.permutation(own_key, shards_of)[block_of(target)]
    other_side = (block_of(target) + shards_of // 2) % shards_of
    return jnp.where((block_of(source) == first) | (block_of(source) == other_side), factor * drawn, drawn)


def shard_levels(rng, shape, cuts, low, high):
    gain = 1.0
    for dim, parts in cuts:
        draws = jax.random.uniform(jax.random.fold_in(jax.random.fold_in(rng, 6), dim), (parts,), jnp.float32, low / len(cuts), high / len(cuts))
        gain = gain * jnp.repeat(jnp.exp(draws), shape[dim] // parts).reshape((-1,) + (1,) * (len(shape) - 1 - dim))
    return gain


def gaussian(rng, extent, scale, bound, shards=(), held_as=jnp.bfloat16):
    array = scale * jax.random.normal(rng, extent, jnp.float32)
    if shards:
        array = array * shard_levels(rng, extent, shards, -0.22, 0.18)
    return jnp.clip(array, -bound, bound).astype(held_as)


def bell_draw_with(key, extent, width, limit, shards, heavy, kind=jnp.bfloat16):
    array = width * jax.random.normal(key, extent, jnp.float32)
    if shards:
        array = array * shard_levels(key, extent, shards, -0.22, 0.18)
    return jnp.clip(with_spikes(array, jax.random.fold_in(key, 3), *heavy), -limit, limit).astype(kind)


def setup_inputs(seed: int = 0) -> dict:
    seeds = jax.random.split(jax.random.key(seed), 14)
    return {
        "layer_in": gaussian(seeds[0], (TOKENS, D), 1.0, 6.0, ((0, 32),)),
        "out_grad": bell_draw_with(seeds[1], (TOKENS, D), 1.0, 6.0, ((0, 32),), (0, 1, 32, 2.75)),
        "segment_ids": draw_segment_ids(jax.random.fold_in(seeds[13], 71), 0),
        "segment_parents": draw_segment_parents(jax.random.fold_in(seeds[13], 71), 0),
        "norm_gain1": jnp.clip(1.0 + 0.1 * jax.random.normal(seeds[4], (D,), jnp.float32), 0.5, 1.5).astype(jnp.bfloat16),
        "w_query": gaussian(seeds[5], (D, HEADS * HEAD), D ** -0.5, 0.15625, ((0, 32),)),
        "w_key": gaussian(seeds[6], (D, KV_HEADS * HEAD), D ** -0.5, 0.15625, ((0, 32),)),
        "w_value": gaussian(seeds[7], (D, KV_HEADS * HEAD), D ** -0.5, 0.15625, ((0, 32),)),
        "w_output": gaussian(seeds[8], (HEADS * HEAD, D), (max(1, D // 512)) ** -0.5, 4.0, ((1, 32),)),
        "norm_gain2": jnp.clip(1.0 + 0.1 * jax.random.normal(seeds[9], (D,), jnp.float32), 0.5, 1.5).astype(jnp.bfloat16),
        "w_gate": gaussian(seeds[10], (D, FF), D ** -0.5, 0.15625, ((0, 32),)),
        "w_up": gaussian(seeds[11], (D, FF), D ** -0.5, 0.15625, ((0, 32),)),
        "w_down": gaussian(seeds[12], (FF, D), FF ** -0.5, 0.09375, ((1, 32),)),
    }


@jax.custom_vjp
def low(v):
    return lax.optimization_barrier(v.astype(jnp.bfloat16)).astype(jnp.float32)

@jax.custom_vjp
def low_back(v):
    return v

def low_keep(v):
    return (low(v), None)

def low_pass(kept, grad):
    return (grad,)

def back_keep(v):
    return (v, None)

def back_low(kept, grad):
    return (low(grad),)
low.defvjp(low_keep, low_pass)
low_back.defvjp(back_keep, back_low)
EPSILON = 1e-05
ROPE_BASE = 10000.0
MASKED_SCORE = -1e+30
HIGHEST_PRECISION = lax.Precision.HIGHEST

def matmul_high(left, right):
    return jnp.dot(left, right, precision=HIGHEST_PRECISION, preferred_element_type=jnp.float32)

def rms_norm(inputs, gain_vector):
    norm_scale = lax.rsqrt(lax.optimization_barrier(jnp.mean(inputs * inputs, axis=-1, keepdims=True)) + EPSILON)
    return inputs * norm_scale * gain_vector

def rotate(inputs, cosine, sine_table):
    middle = inputs.shape[-1] // 2
    turned = jnp.concatenate([-inputs[..., middle:], inputs[..., :middle]], axis=-1)
    return inputs * cosine + turned * sine_table

def tree_layer(params, inputs, cosine, sine_table, key_seg, ancestry):
    gain1, query_w, key_w, value_w, output_w, gain2, gate_w, up_w, down_w = params
    row_count = inputs.shape[0]
    group_size = HEADS // KV_HEADS
    normed1 = low(rms_norm(inputs, gain1))
    query_proj = low_back(matmul_high(normed1, query_w)).reshape(row_count, HEADS, HEAD)
    key_proj = low_back(matmul_high(normed1, key_w)).reshape(row_count, KV_HEADS, HEAD)
    values = low(low_back(matmul_high(normed1, value_w))).reshape(row_count, KV_HEADS, HEAD)
    query_rot = low(rotate(query_proj, cosine, sine_table)).reshape(row_count, KV_HEADS, group_size, HEAD)
    keys_rot = low(rotate(key_proj, cosine, sine_table))
    row_ids = jnp.arange(row_count, dtype=jnp.int32)
    block_count = row_count // TOK_DEV

    def query_block(block_item):
        query_part, ancestry_part, query_rows = block_item
        matched = (key_seg[None, :] == ancestry_part[:, 0:1]) | (key_seg[None, :] == ancestry_part[:, 1:2]) | (key_seg[None, :] == ancestry_part[:, 2:3])
        allowed = matched & (row_ids[None, :] <= query_rows[:, None])
        raw_scores = jnp.einsum('qhgd,khd->hgqk', query_part, keys_rot, precision=HIGHEST_PRECISION) * HEAD ** (-0.5)
        scores = jnp.where(allowed[None, None], low_back(raw_scores), MASKED_SCORE)
        prob_values = low(jax.nn.softmax(scores, axis=-1))
        return jnp.einsum('hgqk,khd->qhgd', prob_values, values, precision=HIGHEST_PRECISION)
    attended = lax.map(jax.checkpoint(query_block), (query_rot.reshape(block_count, TOK_DEV, KV_HEADS, group_size, HEAD), ancestry.reshape(block_count, TOK_DEV, 3), row_ids.reshape(block_count, TOK_DEV)))
    attended = low(low_back(attended.reshape(row_count, HEADS * HEAD)))
    mid_stream = inputs + low_back(matmul_high(attended, output_w))
    normed2 = low(rms_norm(mid_stream, gain2))
    gate_act = low_back(matmul_high(normed2, gate_w))
    up_act = low_back(matmul_high(normed2, up_w))
    hidden = low(jax.nn.silu(gate_act) * up_act)
    return mid_stream + low_back(matmul_high(hidden, down_w))

def reference(layer_in, out_grad, segment_ids, segment_parents, norm_gain1, w_query, w_key, w_value, w_output, norm_gain2, w_gate, w_up, w_down):
    seg_total = segment_parents.shape[0]
    lengths = jax.ops.segment_sum(jnp.ones_like(segment_ids), segment_ids, num_segments=seg_total).astype(jnp.int32)
    layout_start = jnp.cumsum(lengths) - lengths
    parent = segment_parents
    grand_ids = parent[parent]
    own_ids = jnp.arange(seg_total, dtype=jnp.int32)
    depth_start = jnp.where(parent != own_ids, lengths[parent], 0) + jnp.where(grand_ids != parent, lengths[grand_ids], 0)
    row_ids = jnp.arange(TOKENS, dtype=jnp.int32)
    positions = (depth_start[segment_ids] + row_ids - layout_start[segment_ids]).astype(jnp.float32)
    middle = HEAD // 2
    inverse = jnp.exp(jnp.arange(middle, dtype=jnp.float32) * (-2.0 * math.log(ROPE_BASE) / HEAD))
    angles = positions[:, None] * inverse[None, :]
    cosine = jnp.concatenate([jnp.cos(angles), jnp.cos(angles)], axis=1)[:, None, :]
    sine_table = jnp.concatenate([jnp.sin(angles), jnp.sin(angles)], axis=1)[:, None, :]
    ancestry = jnp.stack([segment_ids, parent[segment_ids], grand_ids[segment_ids]], axis=1)
    weights = tuple((matrix.astype(jnp.float32) for matrix in (norm_gain1, w_query, w_key, w_value, w_output, norm_gain2, w_gate, w_up, w_down)))

    def forward(inputs, *params):

        def one_tree(tree_item):
            tree_inputs, tree_cos, tree_sin, tree_segs, tree_ancestry = tree_item
            return tree_layer(params, tree_inputs, tree_cos, tree_sin, tree_segs, tree_ancestry)
        stacked = lax.map(jax.checkpoint(one_tree), (inputs.reshape(TREES, TREE, D), cosine.reshape(TREES, TREE, 1, HEAD), sine_table.reshape(TREES, TREE, 1, HEAD), segment_ids.reshape(TREES, TREE), ancestry.reshape(TREES, TREE, 3)))
        return stacked.reshape(TOKENS, D)
    result, pullback = jax.vjp(forward, layer_in.astype(jnp.float32), *weights)
    gradients = pullback(out_grad.astype(jnp.float32))
    return (result.astype(jnp.bfloat16), gradients[0], gradients[1], gradients[2], gradients[3], gradients[4], gradients[5], gradients[6], gradients[7], gradients[8], gradients[9])
```

```python
import functools
import math

import jax
import jax.numpy as jnp
from jax import lax
from jax.experimental import pallas as pl
from jax.experimental.pallas import tpu as pltpu
from jax.sharding import PartitionSpec as P

HEADS = 20
KV_HEADS = 5
GROUP = HEADS // KV_HEADS
HEAD = 64
TREE = 5120
D = 1280
FF = 3584
HALF = FF // 2
LANES = 128
GROUP_COLS = GROUP * HEAD + 2 * HEAD
QKV = KV_HEADS * GROUP_COLS
QKV_PAD = QKV + LANES
BQ = 128
BK = 256
STACK = GROUP * BQ

EPSILON = 1e-05
ROPE_BASE = 10000.0
MASKED = -1e30
SCALE = HEAD**-0.5
SCALE2 = SCALE * math.log2(math.e)
SAFE_EXPONENT = 60.0
FAR = 1 << 20

F32 = jnp.float32
BF16 = jnp.bfloat16
ROWS_BY_ROWS = (((1,), (1,)), ((), ()))
COLS_BY_COLS = (((0,), (0,)), ((), ()))
VMEM_SPACE = pl.BlockSpec(memory_space=pltpu.VMEM)
SMEM_SPACE = pl.BlockSpec(memory_space=pltpu.SMEM)
ANY_SPACE = pl.BlockSpec(memory_space=pl.ANY)


def params(mib):
    return pltpu.CompilerParams(vmem_limit_bytes=mib * 2**20)


def lane_iota(shape):
    return lax.broadcasted_iota(jnp.int32, shape, len(shape) - 1)


def dot(a, b):
    return jnp.dot(a, b, preferred_element_type=F32)


def dot_tr(a, b):
    return lax.dot_general(a, b, ROWS_BY_ROWS, preferred_element_type=F32)


def dot_cc(a, b):
    return lax.dot_general(a, b, COLS_BY_COLS, preferred_element_type=F32)


def half_turn(z, low):
    return jnp.where(low, pltpu.roll(z, LANES - 32, 1), pltpu.roll(z, 32, 1))


def project_kernel(x_ref, w_ref, cos_ref, sin_ref, n_ref, q_ref, kv_ref, gain_ref):
    gains = w_ref[:, QKV:].astype(F32).T
    gain_ref[...] = gains[:8, :]
    gain1 = gains[0:1, :]
    rows = x_ref.shape[0]

    def norm(i, _):
        at = pl.ds(i * BQ, BQ)
        x = x_ref[at, :].astype(F32)
        scale = lax.rsqrt(jnp.mean(x * x, axis=1, keepdims=True) + EPSILON)
        n_ref[at, :] = (x * scale * gain1).astype(BF16)
        return 0

    lax.fori_loop(0, rows // BQ, norm, 0)
    lane = lane_iota((rows, LANES))
    low = (lane % HEAD) < HEAD // 2
    left = lane < HEAD
    cos = cos_ref[...]
    sin = sin_ref[...]
    for g in range(KV_HEADS):
        z = dot(n_ref[...], w_ref[:, g * GROUP_COLS : (g + 1) * GROUP_COLS])
        for pair in range(GROUP // 2):
            zp = z[:, pair * LANES : (pair + 1) * LANES]
            rot = (zp * cos + half_turn(zp, low) * sin).astype(BF16).astype(F32)
            head = g * GROUP + 2 * pair
            q_ref[head] = jnp.where(left, rot, 0.0).astype(BF16)
            q_ref[head + 1] = jnp.where(left, pltpu.roll(rot, HEAD, 1), 0.0).astype(BF16)
        zk = z[:, GROUP * HEAD :]
        rot = zk * cos + half_turn(zk, low) * sin
        kv_ref[g] = jnp.where(left, rot, zk).astype(BF16)


def project(x, w, cos, sin):
    rows = x.shape[0]
    return pl.pallas_call(
        project_kernel,
        out_shape=[
            jax.ShapeDtypeStruct((rows, D), BF16),
            jax.ShapeDtypeStruct((HEADS, rows, LANES), BF16),
            jax.ShapeDtypeStruct((KV_HEADS, rows, LANES), BF16),
            jax.ShapeDtypeStruct((8, D), F32),
        ],
        compiler_params=params(48),
        name="project",
    )(x, w, cos, sin)


def gather_keys(block, kv_refs, kv, sems):
    rows = kv_refs[0].shape[1]
    copies = []
    for e, ref in enumerate(kv_refs):
        at = pl.multiple_of((block ^ e) * rows, LANES)
        copies.append(pltpu.make_async_copy(ref, kv.at[:, pl.ds(at, rows), :], sems.at[e]))
    for copy in copies:
        copy.start()
    for copy in copies:
        copy.wait()


def tile_pair(meta_ref, tiles, i, t):
    spots = []
    count = meta_ref[1 + i]
    for k in (2 * t, 2 * t + 1):
        first = pl.multiple_of(meta_ref[1 + BQ + i * tiles + jnp.minimum(k, count - 1)] * BK, BK)
        spots.append((first, jnp.where(k < count, first, FAR)))
    return spots


def mask_bias(info_ref, seg_ref, i, spots):
    info = info_ref[pl.ds(i * BQ, BQ), :]
    own, parent, grand, row = (info[:, c : c + 1] for c in range(4))
    parts = []
    for first, name in spots:
        seg = seg_ref[:, pl.ds(first, BK)]
        key_row = lane_iota((1, BK)) + name
        ok = ((seg == own) | (seg == parent) | (seg == grand)) & (key_row <= row)
        parts.append(jnp.where(ok, 0.0, MASKED))
    return jnp.concatenate(parts, axis=1)


def key_pair(kv, g, spots):
    return jnp.concatenate([kv[g, pl.ds(first, BK), :] for first, _ in spots], axis=0)


def masked(s, bias):
    return (s.reshape(GROUP, BQ, 2 * BK) * SCALE2 + bias[None]).reshape(STACK, 2 * BK)


def largest_square(ref, rows):
    ones = jnp.where(lax.broadcasted_iota(jnp.int32, (LANES, LANES), 0) < HEAD, 1.0, 0.0)
    ones = ones.astype(BF16)

    def step(n, top):
        for g in range(ref.shape[0]):
            v = ref[g, pl.ds(n * BK, BK), :].astype(F32)
            sums = dot((v * v).astype(BF16), ones)
            top = jnp.maximum(top, jnp.max(sums.reshape(BK // 8, 8, LANES), axis=0))
        return top

    top = lax.fori_loop(0, rows // BK, step, jnp.zeros((8, LANES), F32))
    return jnp.max(top)


def forward_kernel(
    meta_ref, q_ref, *refs, tiles, span
):
    kv_refs = refs[:span]
    info_ref, seg_ref, att_ref, lse_ref, kv, acc, total, top, sems = refs[span:]
    rows = q_ref.shape[1]
    gather_keys(meta_ref[0], kv_refs, kv, sems)

    def q_rows(i, g):
        at = pl.ds(pl.multiple_of(i * BQ, BQ), BQ)
        return q_ref[pl.ds(g * GROUP, GROUP), at, :].reshape(STACK, LANES)

    def fold(i, g, spots, bias, ceiling):
        pair = key_pair(kv, g, spots)
        s = masked(dot_tr(q_rows(i, g), pair), bias)
        if ceiling:
            s = s - top[g, :, 0:1]
        p = jnp.exp2(s)
        total[g] += sum(p[:, k * LANES : (k + 1) * LANES] for k in range(2 * BK // LANES))
        acc[g] += dot(p.astype(BF16), pair)

    def finish(i, ceiling):
        at = pl.ds(pl.multiple_of(i * BQ, BQ), BQ)
        lane = lane_iota((BQ, LANES))
        logs = jnp.zeros((BQ, LANES), F32)
        for g in range(KV_HEADS):
            sums = jnp.sum(total[g], axis=1, keepdims=True)
            out = acc[g] * (1.0 / sums)
            lse = jnp.log2(sums)
            if ceiling:
                lse = lse + top[g, :, 0:1]
            for h in range(GROUP):
                logs = jnp.where(lane == g * GROUP + h, lse[h * BQ : (h + 1) * BQ], logs)
            for pair in range(GROUP // 2):
                first = out[2 * pair * BQ : (2 * pair + 1) * BQ]
                second = out[(2 * pair + 1) * BQ : (2 * pair + 2) * BQ]
                both = jnp.where(lane < HEAD, pltpu.roll(first, HEAD, 1), second)
                column = (g * GROUP // 2 + pair) * LANES
                att_ref[at, column : column + LANES] = both.astype(BF16)
        lse_ref[at, :] = logs

    def run(ceiling):
        def q_loop(i, _):
            acc[...] = jnp.zeros_like(acc)
            total[...] = jnp.zeros_like(total)
            pairs = (meta_ref[1 + i] + 1) // 2
            if ceiling:
                top[...] = jnp.full_like(top, 2 * MASKED)

                def top_loop(t, _):
                    spots = tile_pair(meta_ref, tiles, i, t)
                    bias = mask_bias(info_ref, seg_ref, i, spots)

                    def top_group(g, _):
                        s = masked(dot_tr(q_rows(i, g), key_pair(kv, g, spots)), bias)
                        top[g] = jnp.maximum(top[g], jnp.max(s, axis=1, keepdims=True))
                        return 0

                    lax.fori_loop(0, KV_HEADS, top_group, 0)
                    return 0

                lax.fori_loop(0, pairs, top_loop, 0)

            def k_loop(t, _):
                spots = tile_pair(meta_ref, tiles, i, t)
                bias = mask_bias(info_ref, seg_ref, i, spots)
                if ceiling:

                    def group(g, _):
                        fold(i, g, spots, bias, True)
                        return 0

                    lax.fori_loop(0, KV_HEADS, group, 0)
                else:
                    for g in range(KV_HEADS):
                        fold(i, g, spots, bias, False)
                return 0

            lax.fori_loop(0, pairs, k_loop, 0)
            finish(i, ceiling)
            return 0

        lax.fori_loop(0, rows // BQ, q_loop, 0)

    bound = largest_square(q_ref, rows // BK * BK)
    if rows % BK:
        bound = jnp.maximum(bound, largest_square(q_ref.at[:, rows - BK :, :], BK))
    bound = bound * largest_square(kv, kv.shape[1])
    limit = (SAFE_EXPONENT / SCALE2) ** 2
    safe = bound < limit

    @pl.when(safe)
    def _():
        run(False)

    @pl.when(jnp.logical_not(safe))
    def _():
        run(True)


def attention_forward(meta, q, kvs, info, seg):
    rows = q.shape[1]
    span = len(kvs)
    keys = span * rows
    tiles = keys // BK
    return pl.pallas_call(
        functools.partial(forward_kernel, tiles=tiles, span=span),
        out_shape=[
            jax.ShapeDtypeStruct((rows, D), BF16),
            jax.ShapeDtypeStruct((rows, LANES), F32),
        ],
        in_specs=[SMEM_SPACE, VMEM_SPACE] + [ANY_SPACE] * span + [VMEM_SPACE] * 2,
        out_specs=[VMEM_SPACE] * 2,
        scratch_shapes=[
            pltpu.VMEM((KV_HEADS, keys, LANES), BF16),
            pltpu.VMEM((KV_HEADS, STACK, LANES), F32),
            pltpu.VMEM((KV_HEADS, STACK, LANES), F32),
            pltpu.VMEM((KV_HEADS, STACK, LANES), F32),
            pltpu.SemaphoreType.DMA((span,)),
        ],
        compiler_params=params(52),
        cost_estimate=pl.CostEstimate(
            flops=20 * 10**9, bytes_accessed=15 * 10**6, transcendentals=3 * 10**7
        ),
        name="attention_forward",
    )(meta, q, *kvs, info, seg)


def backward_kernel(meta_ref, q_ref, da_ref, att_ref, lse_ref, cos_ref, sin_ref, *refs, tiles, span):
    kv_refs = refs[:span]
    info_ref, seg_ref, dq_ref, near_ref, far_ref, kv, dkv, dq, qd, stats, sems = refs[span:]
    rows = q_ref.shape[1]
    block = meta_ref[0]
    gather_keys(block, kv_refs, kv, sems)

    def clear(n, _):
        dkv[:, pl.ds(n * BK, BK), :] = jnp.zeros((KV_HEADS, BK, LANES), F32)
        return 0

    lax.fori_loop(0, kv.shape[1] // BK, clear, 0)
    lane = lane_iota((BQ, LANES))
    left = lane < HEAD

    def q_loop(i, _):
        at = pl.ds(pl.multiple_of(i * BQ, BQ), BQ)
        dq[...] = jnp.zeros_like(dq)
        logs = lse_ref[at, :]
        for h in range(HEADS):
            g, r = h // GROUP, h % GROUP
            column = h // 2 * LANES
            da = da_ref[at, column : column + LANES].astype(F32)
            delta = da * att_ref[at, column : column + LANES].astype(F32)
            mine = left if h % 2 == 0 else jnp.logical_not(left)
            delta = jnp.sum(jnp.where(mine, delta, 0.0), axis=1, keepdims=True)
            if h % 2 == 0:
                da = pltpu.roll(da, HEAD, 1)
            da = jnp.where(left, 0.0, da).astype(BF16)
            qd[g, r * BQ : (r + 1) * BQ, :] = q_ref[h, at, :]
            qd[g, STACK + r * BQ : STACK + (r + 1) * BQ, :] = da
            stats[g, r * BQ : (r + 1) * BQ, :] = jnp.where(left, logs[:, h : h + 1], delta)

        def k_loop(t, _):
            spots = tile_pair(meta_ref, tiles, i, t)
            bias = mask_bias(info_ref, seg_ref, i, spots)
            for g in range(KV_HEADS):
                pair = key_pair(kv, g, spots)
                both = qd[g]
                sd = dot_tr(both, pair)
                p = jnp.exp2(masked(sd[:STACK], bias) - stats[g, :, 0:1])
                ds = (p * (sd[STACK:] - stats[g, :, HEAD : HEAD + 1])).astype(BF16)
                p = p.astype(BF16)
                dq[g] += dot(ds, pair)
                moved = dot_cc(jnp.concatenate([ds, p], axis=0), both)
                for n, (first, _) in enumerate(spots):
                    dkv[g, pl.ds(first, BK), :] += moved[n * BK : (n + 1) * BK]
            return 0

        lax.fori_loop(0, (meta_ref[1 + i] + 1) // 2, k_loop, 0)
        cos = cos_ref[at, :]
        sin = sin_ref[at, :]
        low = (lane % HEAD) < HEAD // 2
        for g in range(KV_HEADS):
            for pair in range(GROUP // 2):
                first = dq[g, 2 * pair * BQ : (2 * pair + 1) * BQ]
                second = dq[g, (2 * pair + 1) * BQ : (2 * pair + 2) * BQ]
                z = jnp.where(left, first, pltpu.roll(second, HEAD, 1)) * SCALE
                z = z * cos - half_turn(z, low) * sin
                column = (g * GROUP // 2 + pair) * LANES
                dq_ref[at, column : column + LANES] = z.astype(BF16)
        return 0

    lax.fori_loop(0, rows // BQ, q_loop, 0)
    factor = jnp.where(lane < HEAD, SCALE, 1.0)
    for e in range(span):
        target = near_ref if e % 2 == 0 else far_ref
        first = (block ^ e) * rows

        def leave(n, _):
            at = pl.ds(pl.multiple_of(n * BQ, BQ), BQ)
            source = pl.ds(pl.multiple_of(first + n * BQ, BQ), BQ)
            for g in range(KV_HEADS):
                target[e // 2, g, at, :] = (dkv[g, source, :] * factor).astype(BF16)
            return 0

        lax.fori_loop(0, rows // BQ, leave, 0)


def attention_backward(meta, q, da, att, lse, cos, sin, kvs, info, seg):
    rows = q.shape[1]
    span = len(kvs)
    keys = span * rows
    tiles = keys // BK
    return pl.pallas_call(
        functools.partial(backward_kernel, tiles=tiles, span=span),
        out_shape=[
            jax.ShapeDtypeStruct((rows, D), BF16),
            jax.ShapeDtypeStruct((span // 2, KV_HEADS, rows, LANES), BF16),
            jax.ShapeDtypeStruct((span // 2, KV_HEADS, rows, LANES), BF16),
        ],
        in_specs=[SMEM_SPACE] + [VMEM_SPACE] * 6 + [ANY_SPACE] * span + [VMEM_SPACE] * 2,
        out_specs=[VMEM_SPACE] * 3,
        scratch_shapes=[
            pltpu.VMEM((KV_HEADS, keys, LANES), BF16),
            pltpu.VMEM((KV_HEADS, keys, LANES), F32),
            pltpu.VMEM((KV_HEADS, STACK, LANES), F32),
            pltpu.VMEM((KV_HEADS, 2 * STACK, LANES), BF16),
            pltpu.VMEM((KV_HEADS, STACK, LANES), F32),
            pltpu.SemaphoreType.DMA((span,)),
        ],
        compiler_params=params(60),
        cost_estimate=pl.CostEstimate(
            flops=60 * 10**9, bytes_accessed=30 * 10**6, transcendentals=3 * 10**7
        ),
        name="attention_backward",
    )(meta, q, da, att, lse, cos, sin, *kvs, info, seg)


def middle_kernel(x_ref, att_ref, w_ref, gain_ref, mid_ref, n_ref):
    mid_ref[...] = dot_tr(att_ref[...], w_ref[...])
    gain2 = gain_ref[1:2, :]

    def norm(i, _):
        at = pl.ds(pl.multiple_of(i * BQ, BQ), BQ)
        mid = x_ref[at, :].astype(F32) + mid_ref[at, :]
        scale = lax.rsqrt(jnp.mean(mid * mid, axis=1, keepdims=True) + EPSILON)
        mid_ref[at, :] = mid
        n_ref[at, :] = (mid * scale * gain2).astype(BF16)
        return 0

    lax.fori_loop(0, mid_ref.shape[0] // BQ, norm, 0)


def middle(x, att, w, gains):
    rows = x.shape[0]
    return pl.pallas_call(
        middle_kernel,
        out_shape=[
            jax.ShapeDtypeStruct((rows, D), F32),
            jax.ShapeDtypeStruct((rows, D), BF16),
        ],
        compiler_params=params(32),
        name="middle",
    )(x, att, w, gains)


def feed_forward_kernel(
    n1_ref, n2_ref, og1_ref, og2_ref, wg_ref, wu_ref, wd_ref,
    own_ref, far_ref, dw_ref,
    n, og, nt, ogt, oacc, nacc, hid, dgate, dup,
):
    f = pl.program_id(0)
    part = pl.program_id(1)
    rows = n1_ref.shape[0]

    @pl.when((f == 0) & (part == 0))
    def _():
        n[:rows] = n1_ref[...]
        n[rows:] = n2_ref[...]
        og[:rows] = og1_ref[...]
        og[rows:] = og2_ref[...]
        nt[...] = n[...].T
        ogt[...] = og[...].T
        oacc[...] = jnp.zeros_like(oacc)
        nacc[...] = jnp.zeros_like(nacc)

    @pl.when(part == 0)
    def _():
        for k in range(2):
            at = slice(k * rows, (k + 1) * rows)
            gate = dot(n[at], wg_ref[...])
            up = dot(n[at], wu_ref[...])
            grad = dot(og[at], wd_ref[...])
            sig = jax.nn.sigmoid(gate)
            silu = gate * sig
            hid[at] = (silu * up).astype(BF16)
            dgate[at] = (grad * up * sig * (1.0 + gate * (1.0 - sig))).astype(BF16)
            dup[at] = (grad * silu).astype(BF16)
        dw_ref[...] = dot(nt[...], dgate[...]).astype(BF16)

    @pl.when(part == 1)
    def _():
        nacc[...] += dot_tr(dgate[...], wg_ref[...]) + dot_tr(dup[...], wu_ref[...])
        dw_ref[...] = dot(nt[...], dup[...]).astype(BF16)

    @pl.when(part == 2)
    def _():
        oacc[...] += dot_tr(hid[...], wd_ref[...])
        dw_ref[...] = dot(ogt[...], hid[...]).astype(BF16)

    @pl.when((f == pl.num_programs(0) - 1) & (part == 2))
    def _():
        own_ref[0] = oacc[:rows].astype(BF16)
        own_ref[1] = nacc[:rows].astype(BF16)
        far_ref[0] = oacc[rows:].astype(BF16)
        far_ref[1] = nacc[rows:].astype(BF16)


def feed_forward(n_own, n_far, og_own, og_far, w):
    rows = n_own.shape[0]
    block = 256
    steps = HALF // block
    whole = pl.BlockSpec((rows, D), lambda f, k: (0, 0), pipeline_mode=pl.Buffered(1))
    sides = pl.BlockSpec((2, rows, D), lambda f, k: (0, 0, 0))
    slab = [pl.BlockSpec((D, block), lambda f, k, m=m: (0, m * steps + f)) for m in range(3)]
    return pl.pallas_call(
        feed_forward_kernel,
        grid=(steps, 3),
        in_specs=[whole] * 4 + slab,
        out_specs=[sides, sides, pl.BlockSpec((D, block), lambda f, k: (0, k * steps + f))],
        out_shape=[
            jax.ShapeDtypeStruct((2, rows, D), BF16),
            jax.ShapeDtypeStruct((2, rows, D), BF16),
            jax.ShapeDtypeStruct((D, 3 * HALF), BF16),
        ],
        scratch_shapes=[
            pltpu.VMEM((2 * rows, D), BF16),
            pltpu.VMEM((2 * rows, D), BF16),
            pltpu.VMEM((D, 2 * rows), BF16),
            pltpu.VMEM((D, 2 * rows), BF16),
            pltpu.VMEM((2 * rows, D), F32),
            pltpu.VMEM((2 * rows, D), F32),
            pltpu.VMEM((2 * rows, block), BF16),
            pltpu.VMEM((2 * rows, block), BF16),
            pltpu.VMEM((2 * rows, block), BF16),
        ],
        compiler_params=params(62),
        cost_estimate=pl.CostEstimate(
            flops=52 * 10**9, bytes_accessed=40 * 10**6, transcendentals=3 * 10**6
        ),
        name="feed_forward",
    )(n_own, n_far, og_own, og_far, w, w, w)


def turn_kernel(
    mid_ref, own_ref, got_ref, og_ref, gain_ref, w_ref, att_ref,
    out_ref, gm_ref, da_ref, dw_ref, dgain_ref, gmb,
):
    gain2 = gain_ref[1:2, :]

    def step(i, dgain):
        at = pl.ds(pl.multiple_of(i * BQ, BQ), BQ)
        mid = mid_ref[at, :]
        out = mid + (own_ref[0, at, :].astype(F32) + got_ref[0, at, :].astype(F32))
        out_ref[at, :] = out.astype(BF16)
        dn = own_ref[1, at, :].astype(F32) + got_ref[1, at, :].astype(F32)
        scale = lax.rsqrt(jnp.mean(mid * mid, axis=1, keepdims=True) + EPSILON)
        dgain = dgain + jnp.sum((dn * mid * scale).reshape(BQ // 8, 8, D), axis=0)
        q2 = dn * gain2
        mean = jnp.mean(q2 * mid, axis=1, keepdims=True)
        gm = og_ref[at, :].astype(F32) + scale * q2 - mid * (scale * scale * scale * mean)
        gm_ref[at, :] = gm
        gmb[at, :] = gm.astype(BF16)
        return dgain

    dgain = lax.fori_loop(0, mid_ref.shape[0] // BQ, step, jnp.zeros((8, D), F32))
    dgain_ref[...] = dgain
    da_ref[...] = dot(gmb[...], w_ref[...]).astype(BF16)
    dw_ref[...] = dot_cc(gmb[...], att_ref[...]).astype(BF16)


def turn(mid, own, got, og, gains, w, att):
    rows = mid.shape[0]
    return pl.pallas_call(
        turn_kernel,
        out_shape=[
            jax.ShapeDtypeStruct((rows, D), BF16),
            jax.ShapeDtypeStruct((rows, D), F32),
            jax.ShapeDtypeStruct((rows, D), BF16),
            jax.ShapeDtypeStruct((D, D), BF16),
            jax.ShapeDtypeStruct((8, D), F32),
        ],
        scratch_shapes=[pltpu.VMEM((rows, D), BF16)],
        compiler_params=params(56),
        name="turn",
    )(mid, own, got, og, gains, w, att)


def finish_kernel(
    x_ref, n_ref, gm_ref, dq_ref, k0_ref, k1_ref, k2_ref, k3_ref, k4_ref, w_ref, gain_ref,
    dgain_ref, cos_ref, sin_ref, in_ref, dw_ref, dz, dn,
):
    rows = x_ref.shape[0]
    lane = lane_iota((BQ, LANES))
    low = (lane % HEAD) < HEAD // 2
    left = lane < HEAD

    def turn_back(i, _):
        at = pl.ds(pl.multiple_of(i * BQ, BQ), BQ)
        cos = cos_ref[at, :]
        sin = sin_ref[at, :]
        for g in range(KV_HEADS):
            z = sum(
                ref[g, at, :].astype(F32) for ref in (k0_ref, k1_ref, k2_ref, k3_ref, k4_ref)
            )
            rot = z * cos - half_turn(z, low) * sin
            base = g * GROUP_COLS
            span = GROUP * HEAD
            dz[at, base : base + span] = dq_ref[at, g * span : (g + 1) * span]
            dz[at, base + span : base + span + LANES] = jnp.where(left, rot, z).astype(BF16)
        return 0

    lax.fori_loop(0, rows // BQ, turn_back, 0)
    dw_ref[:, :QKV] = dot_cc(n_ref[...], dz[...]).astype(BF16)
    dn[...] = dot_tr(dz[...], w_ref[:, :QKV])
    gain1 = gain_ref[0:1, :]

    def step(i, dgain):
        at = pl.ds(pl.multiple_of(i * BQ, BQ), BQ)
        x = x_ref[at, :].astype(F32)
        grad = dn[at, :]
        scale = lax.rsqrt(jnp.mean(x * x, axis=1, keepdims=True) + EPSILON)
        dgain = dgain + jnp.sum((grad * x * scale).reshape(BQ // 8, 8, D), axis=0)
        q1 = grad * gain1
        mean = jnp.mean(q1 * x, axis=1, keepdims=True)
        in_ref[at, :] = gm_ref[at, :] + scale * q1 - x * (scale * scale * scale * mean)
        return dgain

    dgain1 = lax.fori_loop(0, rows // BQ, step, jnp.zeros((8, D), F32))
    dgain1 = jnp.sum(dgain1, axis=0, keepdims=True)
    dgain2 = jnp.sum(dgain_ref[...], axis=0, keepdims=True)
    row = lax.broadcasted_iota(jnp.int32, (LANES, D), 0)
    both = jnp.where(row == 0, dgain1, jnp.where(row == 1, dgain2, 0.0))
    dw_ref[:, QKV:] = both.T.astype(BF16)


def finish(x, n, gm, dq, pieces, w, gains, dgain, cos, sin):
    rows = x.shape[0]
    return pl.pallas_call(
        finish_kernel,
        out_shape=[
            jax.ShapeDtypeStruct((rows, D), F32),
            jax.ShapeDtypeStruct((D, QKV_PAD), BF16),
        ],
        scratch_shapes=[pltpu.VMEM((rows, QKV), BF16), pltpu.VMEM((rows, D), F32)],
        compiler_params=params(60),
        name="finish",
    )(x, n, gm, dq, *pieces, w, gains, dgain, cos, sin)


def body(
    layer_in, out_grad, segment_ids, segment_parents, norm_gain1, w_query, w_key, w_value, w_output,
    norm_gain2, w_gate, w_up, w_down,
):
    size = lax.axis_size("fsdp")
    rows = layer_in.shape[0]
    span = TREE // rows
    shard = D // size
    me = lax.axis_index("fsdp")
    block = me % span
    tree = me // span
    core = me % 2

    def swap(v, bit):
        return lax.ppermute(v, "fsdp", [(i, i ^ bit) for i in range(size)])

    same_core = [list(range(c, size, 2)) for c in range(2)]

    grouped = [w_query.reshape(shard, KV_HEADS, GROUP * HEAD)]
    grouped += [w.reshape(shard, KV_HEADS, HEAD) for w in (w_key, w_value)]
    grouped = jnp.concatenate(grouped, axis=2).reshape(shard, QKV)
    gain_pair = jnp.stack([norm_gain1, norm_gain2], axis=1)
    gain_pair = jnp.pad(gain_pair, ((0, 0), (0, LANES - 2)))
    qkv_w = lax.all_gather(
        jnp.concatenate([grouped, gain_pair], axis=1), "fsdp", axis=0, tiled=True
    )
    out_w = lax.all_gather(w_output.T, "fsdp", axis=0, tiled=True)
    sides = [
        jnp.concatenate([w[:, c * HALF : (c + 1) * HALF] for w in (w_gate, w_up, w_down.T)], axis=1)
        for c in range(2)
    ]
    keep = jnp.where(core == 0, sides[0], sides[1])
    got = swap(jnp.where(core == 0, sides[1], sides[0]), 1)
    ordered = jnp.where(
        core == 0, jnp.concatenate([keep, got], axis=0), jnp.concatenate([got, keep], axis=0)
    )
    ff_w = lax.all_gather(ordered, "fsdp", axis=0, tiled=True, axis_index_groups=same_core)

    tree_seg = segment_ids
    bit = 1
    while bit < span:
        other = swap(tree_seg, bit)
        first = (me & bit) == 0
        tree_seg = jnp.concatenate(
            [jnp.where(first, tree_seg, other), jnp.where(first, other, tree_seg)], axis=0
        )
        bit *= 2
    seg_count = segment_parents.shape[0] * span // size
    seg_base = tree * seg_count
    tree_seg = tree_seg - seg_base
    own_seg = segment_ids - seg_base
    ids = jnp.arange(seg_count, dtype=jnp.int32)
    parent = lax.dynamic_slice_in_dim(segment_parents, seg_base, seg_count) - seg_base

    def look(index, table):
        return jnp.sum(jnp.where(index[:, None] == ids[None, :], table[None, :], 0), axis=1)

    grand = look(parent, parent)
    lengths = jnp.sum((tree_seg[None, :] == ids[:, None]).astype(jnp.int32), axis=1)
    starts = jnp.sum(jnp.where(ids[None, :] < ids[:, None], lengths[None, :], 0), axis=1)
    depth = jnp.where(parent != ids, look(parent, lengths), 0)
    depth = depth + jnp.where(grand != parent, look(grand, lengths), 0)
    own_row = block * rows + jnp.arange(rows, dtype=jnp.int32)
    positions = (look(own_seg, depth - starts) + own_row).astype(F32)
    lane = jnp.arange(LANES, dtype=jnp.int32)
    inverse = jnp.exp((lane % 32).astype(F32) * (-2.0 * math.log(ROPE_BASE) / HEAD))
    angles = positions[:, None] * inverse[None, :]
    cos = jnp.cos(angles)
    sin = jnp.sin(angles) * jnp.where(lane % HEAD < HEAD // 2, -1.0, 1.0)[None, :]
    info = [own_seg, look(own_seg, parent), look(own_seg, grand), own_row]
    info = sum(jnp.where(lane[None, :] == c, v[:, None], 0) for c, v in enumerate(info))
    tiles = TREE // BK
    steps = rows // BQ
    tile_seg = tree_seg.reshape(tiles, BK)
    tile_first, tile_last = tile_seg[:, 0], tile_seg[:, -1]
    step_seg = own_seg.reshape(steps, BQ)

    def inside(s):
        return (tile_first[None, :] <= s[:, None]) & (s[:, None] <= tile_last[None, :])

    hit = inside(ids) | inside(parent) | inside(grand)
    here = (step_seg[:, :1] <= ids[None, :]) & (ids[None, :] <= step_seg[:, -1:])
    active = jnp.any(here[:, :, None] & hit[None, :, :], axis=1)
    tile_range = jnp.arange(tiles, dtype=jnp.int32)
    last_row = block * rows + (jnp.arange(steps, dtype=jnp.int32) + 1) * BQ - 1
    active = active & (tile_range[None, :] * BK <= last_row[:, None])
    before = tile_range[:, None] < tile_range[None, :]
    place = jnp.sum((active[:, :, None] & before[None]).astype(jnp.int32), axis=1)
    chosen = active[:, :, None] & (place[:, :, None] == tile_range[None, None, :])
    listed = jnp.sum(jnp.where(chosen, tile_range[None, :, None], 0), axis=1)
    counts = jnp.sum(active.astype(jnp.int32), axis=1)
    meta = jnp.concatenate(
        [block[None], jnp.pad(counts, (0, BQ - steps)), listed.reshape(steps * tiles)]
    )
    seg_row = tree_seg[None, :]

    og_far = swap(out_grad, 1)
    normed1, q, kv, gains = project(layer_in, qkv_w, cos, sin)
    kvs = [kv, swap(kv, 1)]
    for chip in range(1, span // 2):
        piece = swap(kv, 2 * chip)
        kvs += [piece, swap(piece, 1)]
    att, lse = attention_forward(meta, q, kvs, info, seg_row)
    mid, normed2 = middle(layer_in, att, out_w, gains)
    own, far, ff_dw = feed_forward(normed2, swap(normed2, 1), out_grad, og_far, ff_w)
    layer_out, grad_mid, da, out_dw, dgain2 = turn(
        mid, own, swap(far, 1), out_grad, gains, out_w, att
    )
    ff_dw = lax.psum_scatter(
        ff_dw, "fsdp", scatter_dimension=0, tiled=True, axis_index_groups=same_core
    )
    out_dw = lax.psum_scatter(out_dw, "fsdp", scatter_dimension=0, tiled=True)
    dq, near, far = attention_backward(meta, q, da, att, lse, cos, sin, kvs, info, seg_row)
    got = swap(far, 1)
    pieces = [near[0], got[0]]
    for chip in range(1, span // 2):
        both = (near[chip].astype(F32) + got[chip].astype(F32)).astype(BF16)
        pieces.append(swap(both, 2 * chip))
    input_grad, qkv_dw = finish(
        layer_in, normed1, grad_mid, dq, pieces, qkv_w, gains, dgain2, cos, sin
    )
    qkv_dw = lax.psum_scatter(qkv_dw, "fsdp", scatter_dimension=0, tiled=True).astype(F32)

    groups = qkv_dw[:, :QKV].reshape(shard, KV_HEADS, GROUP_COLS)
    grad_query = groups[:, :, : GROUP * HEAD].reshape(shard, HEADS * HEAD)
    grad_key = groups[:, :, GROUP * HEAD : GROUP * HEAD + HEAD].reshape(shard, KV_HEADS * HEAD)
    grad_value = groups[:, :, GROUP * HEAD + HEAD :].reshape(shard, KV_HEADS * HEAD)
    mine = jnp.where(core == 0, ff_dw[:shard], ff_dw[shard:])
    got = swap(jnp.where(core == 0, ff_dw[shard:], ff_dw[:shard]), 1)
    low = jnp.where(core == 0, mine, got).astype(F32).reshape(shard, 3, HALF)
    high = jnp.where(core == 0, got, mine).astype(F32).reshape(shard, 3, HALF)
    ff_grads = jnp.concatenate([low, high], axis=2)
    return (
        layer_out,
        input_grad,
        qkv_dw[:, QKV],
        grad_query,
        grad_key,
        grad_value,
        out_dw.astype(F32).T,
        qkv_dw[:, QKV + 1],
        ff_grads[:, 0],
        ff_grads[:, 1],
        ff_grads[:, 2].T,
    )


def solution(mesh):
    rows, cols, flat = P("fsdp", None), P(None, "fsdp"), P("fsdp")
    return jax.shard_map(
        body,
        mesh=mesh,
        in_specs=(rows, rows, flat, P(), flat, rows, rows, rows, cols, flat, rows, rows, cols),
        out_specs=(rows, rows, flat, rows, rows, rows, cols, flat, rows, rows, cols),
        check_vma=False,
    )
```

```python
import functools
import math

import jax
import jax.numpy as jnp
from jax import lax
from jax.experimental import pallas as pl
from jax.experimental.pallas import tpu as pltpu
from jax.sharding import PartitionSpec as P

HEADS = 20
KV_HEADS = 5
GROUP = HEADS // KV_HEADS
HEAD = 64
TREE = 5120
D = 1280
FF = 3584
HALF = FF // 2
LANES = 128
GROUP_COLS = GROUP * HEAD + 2 * HEAD
QKV = KV_HEADS * GROUP_COLS
QKV_PAD = QKV + LANES
BQ = 128
BK = 256
STACK = GROUP * BQ
HEAD_PARTS = ((0, 3), (3, 2))

EPSILON = 1e-05
ROPE_BASE = 10000.0
MASKED = -1e30
SCALE = HEAD**-0.5
SCALE2 = SCALE * math.log2(math.e)
SAFE_EXPONENT = 60.0
FAR = 1 << 20

F32 = jnp.float32
BF16 = jnp.bfloat16
ROWS_BY_ROWS = (((1,), (1,)), ((), ()))
COLS_BY_COLS = (((0,), (0,)), ((), ()))
VMEM_SPACE = pl.BlockSpec(memory_space=pltpu.VMEM)
SMEM_SPACE = pl.BlockSpec(memory_space=pltpu.SMEM)
ANY_SPACE = pl.BlockSpec(memory_space=pl.ANY)


def params(mib):
    return pltpu.CompilerParams(vmem_limit_bytes=mib * 2**20)


def lane_iota(shape):
    return lax.broadcasted_iota(jnp.int32, shape, len(shape) - 1)


def dot(a, b):
    return jnp.dot(a, b, preferred_element_type=F32)


def dot_tr(a, b):
    return lax.dot_general(a, b, ROWS_BY_ROWS, preferred_element_type=F32)


def dot_cc(a, b):
    return lax.dot_general(a, b, COLS_BY_COLS, preferred_element_type=F32)


def half_turn(z, low):
    return jnp.where(low, pltpu.roll(z, LANES - 32, 1), pltpu.roll(z, 32, 1))


def assembly(place_ref, piece_refs, w, sems):
    copies = []
    for e, ref in enumerate(piece_refs):
        parts, rows, cols = ref.shape
        col = pl.multiple_of(place_ref[e] * cols, LANES)
        for part in range(parts):
            k = len(copies)
            row = pl.multiple_of(place_ref[len(piece_refs) + k] * rows, 16)
            to = w.at[pl.ds(row, rows), pl.ds(col, cols)]
            copies.append(pltpu.make_async_copy(ref.at[part], to, sems.at[k]))
    for copy in copies:
        copy.start()
    return copies


def project_kernel(place_ref, x_ref, cos_ref, sin_ref, *refs):
    piece_refs, (n_ref, q_ref, kv_ref, gain_ref, w_ref, top_ref, sems) = refs[:-7], refs[-7:]
    for copy in assembly(place_ref, piece_refs, w_ref, sems):
        copy.wait()
    gains = w_ref[:, QKV:].astype(F32).T
    gain_ref[...] = gains[:8, :]
    gain1 = gains[0:1, :]
    rows = x_ref.shape[0]

    def norm(i, _):
        at = pl.ds(i * BQ, BQ)
        x = x_ref[at, :].astype(F32)
        scale = lax.rsqrt(jnp.mean(x * x, axis=1, keepdims=True) + EPSILON)
        n_ref[at, :] = (x * scale * gain1).astype(BF16)
        return 0

    lax.fori_loop(0, rows // BQ, norm, 0)
    lane = lane_iota((rows, LANES))
    low = (lane % HEAD) < HEAD // 2
    left = lane < HEAD
    cos = cos_ref[...]
    sin = sin_ref[...]
    same = (lax.broadcasted_iota(jnp.int32, (LANES, LANES), 0) < HEAD) == left[:LANES]
    same = jnp.where(same, 1.0, 0.0).astype(BF16)

    def squares(z):
        sums = dot((z * z).astype(BF16), same)
        return jnp.max(sums.reshape(rows // 8, 8, LANES), axis=0)

    q_top = jnp.zeros((8, LANES), F32)
    k_top = jnp.zeros((8, LANES), F32)
    for g in range(KV_HEADS):
        z = dot(n_ref[...], w_ref[:, g * GROUP_COLS : (g + 1) * GROUP_COLS])
        for pair in range(GROUP // 2):
            zp = z[:, pair * LANES : (pair + 1) * LANES]
            rot = (zp * cos + half_turn(zp, low) * sin).astype(BF16).astype(F32)
            q_top = jnp.maximum(q_top, squares(rot))
            head = g * GROUP + 2 * pair
            q_ref[head] = jnp.where(left, rot, 0.0).astype(BF16)
            q_ref[head + 1] = jnp.where(left, pltpu.roll(rot, HEAD, 1), 0.0).astype(BF16)
        zk = z[:, GROUP * HEAD :]
        rot = zk * cos + half_turn(zk, low) * sin
        k_top = jnp.maximum(k_top, squares(rot))
        kv_ref[g, :rows] = jnp.where(left, rot, zk).astype(BF16)
    top_ref[...] = q_top
    k_top = jnp.max(jnp.where(left[:8], k_top, 0.0)) * 1.02
    kv_ref[:, rows:] = jnp.full((KV_HEADS, 16, LANES), k_top, F32).astype(BF16)


def project(place, x, cos, sin, pieces):
    rows = x.shape[0]
    count = sum(p.shape[0] for p in pieces)
    return pl.pallas_call(
        project_kernel,
        out_shape=[
            jax.ShapeDtypeStruct((rows, D), BF16),
            jax.ShapeDtypeStruct((HEADS, rows, LANES), BF16),
            jax.ShapeDtypeStruct((KV_HEADS, rows + 16, LANES), BF16),
            jax.ShapeDtypeStruct((8, D), F32),
            jax.ShapeDtypeStruct((D, QKV_PAD), BF16),
            jax.ShapeDtypeStruct((8, LANES), F32),
        ],
        in_specs=[SMEM_SPACE] + [VMEM_SPACE] * 3 + [ANY_SPACE] * len(pieces),
        out_specs=[VMEM_SPACE] * 6,
        scratch_shapes=[pltpu.SemaphoreType.DMA((count,))],
        compiler_params=params(48),
        name="project",
    )(place, x, cos, sin, *pieces)


def gather_keys(block, kv_refs, kv, sems, heads):
    rows = kv_refs[0].shape[1] - 16
    copies = []
    for e, ref in enumerate(kv_refs):
        at = pl.multiple_of((block ^ e) * rows, LANES)
        to = kv.at[:, pl.ds(at, rows), :]
        copies.append(pltpu.make_async_copy(ref.at[heads, pl.ds(0, rows), :], to, sems.at[e]))
    return copies


def tile_pair(meta_ref, tiles, i, k):
    spots = []
    count = meta_ref[1 + i]
    for k in (k, k + 1):
        first = pl.multiple_of(meta_ref[1 + BQ + i * tiles + jnp.minimum(k, count - 1)] * BK, BK)
        spots.append((first, jnp.where(k < count, first, FAR)))
    return spots


def open_tiles(meta_ref, i):
    return meta_ref[1 + BQ // 2 + i] // 2 * 2


def mask_bias(info_ref, seg_ref, i, spots):
    info = info_ref[pl.ds(i * BQ, BQ), :]
    own, parent, grand, row = (info[:, c : c + 1] for c in range(4))
    parts = []
    for first, name in spots:
        seg = seg_ref[:, pl.ds(first, BK)]
        key_row = lane_iota((1, BK)) + name
        ok = ((seg == own) | (seg == parent) | (seg == grand)) & (key_row <= row)
        parts.append(jnp.where(ok, 0.0, MASKED))
    return jnp.concatenate(parts, axis=1)


def key_pair(kv, g, spots):
    return jnp.concatenate([kv[g, pl.ds(first, BK), :] for first, _ in spots], axis=0)


def masked(s, bias):
    return (s.reshape(GROUP, BQ, 2 * BK) * SCALE2 + bias[None]).reshape(STACK, 2 * BK)


def split_keys(kv, first, second):
    left = lane_iota((BK, LANES)) < HEAD
    one = jnp.ones((BK, LANES), BF16)

    def step(n, _):
        at = pl.ds(pl.multiple_of(n * BK, BK), BK)
        for g in range(kv.shape[0]):
            v = kv[g, at, :]
            second[g, at, :] = jnp.where(left, one, v)
            if first is not None:
                first[g, at, :] = jnp.where(left, v, one)
        return 0

    lax.fori_loop(0, kv.shape[1] // BK, step, 0)


def forward_kernel(meta_ref, q_ref, top_ref, *refs, tiles, span):
    kv_refs = refs[:span]
    info_ref, seg_ref, att_ref, lse_ref, kv, val, acc, top, k_tops, sems = refs[span:]
    rows = q_ref.shape[1]
    copies = gather_keys(meta_ref[0], kv_refs, kv, sems, pl.ds(0, KV_HEADS))
    for e, ref in enumerate(kv_refs):
        source = ref.at[0, pl.ds(rows, 16), :]
        copies.append(pltpu.make_async_copy(source, k_tops.at[e], sems.at[span + e]))
    for copy in copies:
        copy.start()
    for copy in copies:
        copy.wait()
    split_keys(kv, None, val)

    def q_rows(i, g):
        at = pl.ds(pl.multiple_of(i * BQ, BQ), BQ)
        return q_ref[pl.ds(g * GROUP, GROUP), at, :].reshape(STACK, LANES)

    def fold(i, g, spots, bias, ceiling):
        s = dot_tr(q_rows(i, g), key_pair(kv, g, spots))
        s = s * SCALE2 if bias is None else masked(s, bias)
        if ceiling:
            s = s - top[g, :, 0:1]
        acc[g] += dot(jnp.exp2(s).astype(BF16), key_pair(val, g, spots))

    def finish(i, ceiling):
        at = pl.ds(pl.multiple_of(i * BQ, BQ), BQ)
        lane = lane_iota((BQ, LANES))
        logs = jnp.zeros((BQ, LANES), F32)
        for g in range(KV_HEADS):
            sums = acc[g]
            lse = jnp.log2(sums)
            if ceiling:
                lse = lse + top[g, :, 0:1]
            out = sums * pltpu.roll(1.0 / sums, HEAD, 1)
            for h in range(GROUP):
                logs = jnp.where(lane == g * GROUP + h, lse[h * BQ : (h + 1) * BQ, 0:1], logs)
            for pair in range(GROUP // 2):
                first = out[2 * pair * BQ : (2 * pair + 1) * BQ]
                second = out[(2 * pair + 1) * BQ : (2 * pair + 2) * BQ]
                both = jnp.where(lane < HEAD, pltpu.roll(first, HEAD, 1), second)
                column = (g * GROUP // 2 + pair) * LANES
                att_ref[at, column : column + LANES] = both.astype(BF16)
        lse_ref[at, :] = logs

    def run(ceiling):
        def q_loop(i, _):
            acc[...] = jnp.zeros_like(acc)
            count = meta_ref[1 + i]
            free = open_tiles(meta_ref, i)
            if ceiling:
                free = free * 0
                top[...] = jnp.full_like(top, 2 * MASKED)

                def top_loop(t, _):
                    spots = tile_pair(meta_ref, tiles, i, 2 * t)
                    bias = mask_bias(info_ref, seg_ref, i, spots)

                    def top_group(g, _):
                        s = masked(dot_tr(q_rows(i, g), key_pair(kv, g, spots)), bias)
                        top[g] = jnp.maximum(top[g], jnp.max(s, axis=1, keepdims=True))
                        return 0

                    lax.fori_loop(0, KV_HEADS, top_group, 0)
                    return 0

                lax.fori_loop(0, (count + 1) // 2, top_loop, 0)
            else:

                def open_loop(t, _):
                    spots = tile_pair(meta_ref, tiles, i, 2 * t)
                    for g in range(KV_HEADS):
                        fold(i, g, spots, None, False)
                    return 0

                lax.fori_loop(0, free // 2, open_loop, 0)

            def k_loop(t, _):
                spots = tile_pair(meta_ref, tiles, i, free + 2 * t)
                bias = mask_bias(info_ref, seg_ref, i, spots)
                if ceiling:

                    def group(g, _):
                        fold(i, g, spots, bias, True)
                        return 0

                    lax.fori_loop(0, KV_HEADS, group, 0)
                else:
                    for g in range(KV_HEADS):
                        fold(i, g, spots, bias, False)
                return 0

            lax.fori_loop(0, (count - free + 1) // 2, k_loop, 0)
            finish(i, ceiling)
            return 0

        lax.fori_loop(0, rows // BQ, q_loop, 0)

    bound = jnp.max(top_ref[...]) * jnp.max(k_tops[...].astype(F32))
    safe = bound < (SAFE_EXPONENT / SCALE2) ** 2

    @pl.when(safe)
    def _():
        run(False)

    @pl.when(jnp.logical_not(safe))
    def _():
        run(True)


def attention_forward(meta, q, top, kvs, info, seg):
    rows = q.shape[1]
    span = len(kvs)
    keys = span * rows
    tiles = keys // BK
    return pl.pallas_call(
        functools.partial(forward_kernel, tiles=tiles, span=span),
        out_shape=[
            jax.ShapeDtypeStruct((rows, D), BF16),
            jax.ShapeDtypeStruct((rows, LANES), F32),
        ],
        in_specs=[SMEM_SPACE] + [VMEM_SPACE] * 2 + [ANY_SPACE] * span + [VMEM_SPACE] * 2,
        out_specs=[VMEM_SPACE] * 2,
        scratch_shapes=[
            pltpu.VMEM((KV_HEADS, keys, LANES), BF16),
            pltpu.VMEM((KV_HEADS, keys, LANES), BF16),
            pltpu.VMEM((KV_HEADS, STACK, LANES), F32),
            pltpu.VMEM((KV_HEADS, STACK, LANES), F32),
            pltpu.VMEM((span, 16, LANES), BF16),
            pltpu.SemaphoreType.DMA((2 * span,)),
        ],
        compiler_params=params(52),
        cost_estimate=pl.CostEstimate(
            flops=80 * 10**9, bytes_accessed=15 * 10**6, transcendentals=3 * 10**7
        ),
        name="attention_forward",
    )(meta, q, top, *kvs, info, seg)


def backward_kernel(
    meta_ref, q_ref, da_ref, att_ref, lse_ref, cos_ref, sin_ref, *refs, tiles, span, heads
):
    first_head, groups = heads
    kv_refs = refs[:span]
    info_ref, seg_ref, dq_ref, near_ref, far_ref, key, val, dkv, dq, qd, lifted, sems = refs[span:]
    rows = q_ref.shape[1]
    block = meta_ref[0]
    copies = gather_keys(block, kv_refs, key, sems, pl.ds(first_head, groups))
    for copy in copies:
        copy.start()

    def clear(n, _):
        dkv[:, pl.ds(n * BK, BK), :] = jnp.zeros((groups, BK, LANES), F32)
        return 0

    lax.fori_loop(0, key.shape[1] // BK, clear, 0)
    for copy in copies:
        copy.wait()
    split_keys(key, key, val)
    lane = lane_iota((BQ, LANES))
    left = lane < HEAD

    def lanes_of(column, first):
        out = jnp.zeros((BQ, LANES), F32)
        for k in range(3):
            top = column.astype(BF16).astype(F32)
            out = jnp.where(lane == first + k, top, out)
            column = column - top
        return out

    def q_loop(i, _):
        at = pl.ds(pl.multiple_of(i * BQ, BQ), BQ)
        dq[...] = jnp.zeros_like(dq)
        logs = lse_ref[at, :] * (-1.0 / SCALE2)
        for h in range(first_head * GROUP, (first_head + groups) * GROUP):
            g, r = h // GROUP - first_head, h % GROUP
            column = h // 2 * LANES
            da = da_ref[at, column : column + LANES].astype(F32)
            delta = da * att_ref[at, column : column + LANES].astype(F32)
            mine = left if h % 2 == 0 else jnp.logical_not(left)
            delta = jnp.sum(jnp.where(mine, delta, 0.0), axis=1, keepdims=True)
            if h % 2 == 0:
                da = pltpu.roll(da, HEAD, 1)
            q = q_ref[h, at, :]
            own = slice(r * BQ, (r + 1) * BQ)
            other = slice(STACK + r * BQ, STACK + (r + 1) * BQ)
            qd[g, own, :] = q
            qd[g, other, :] = jnp.where(left, 0.0, da).astype(BF16)
            lse = lanes_of(logs[:, h : h + 1], HEAD)
            lifted[g, own, :] = jnp.where(left, q.astype(F32), lse).astype(BF16)
            lifted[g, other, :] = jnp.where(left, lanes_of(-delta, 0), da).astype(BF16)

        def fold(g, spots, bias):
            keys = key_pair(key, g, spots)
            s = dot_tr(lifted[g, :STACK, :], keys)
            p = jnp.exp2(s * SCALE2 if bias is None else masked(s, bias))
            ds = (p * dot_tr(lifted[g, STACK:, :], key_pair(val, g, spots))).astype(BF16)
            p = p.astype(BF16)
            dq[g] += dot(ds, keys)
            moved = dot_cc(jnp.concatenate([ds, p], axis=0), qd[g])
            for n, (first, _) in enumerate(spots):
                dkv[g, pl.ds(first, BK), :] += moved[n * BK : (n + 1) * BK]

        count = meta_ref[1 + i]
        free = open_tiles(meta_ref, i)

        def open_loop(t, _):
            spots = tile_pair(meta_ref, tiles, i, 2 * t)
            for g in range(groups):
                fold(g, spots, None)
            return 0

        lax.fori_loop(0, free // 2, open_loop, 0)

        def k_loop(t, _):
            spots = tile_pair(meta_ref, tiles, i, free + 2 * t)
            bias = mask_bias(info_ref, seg_ref, i, spots)
            for g in range(groups):
                fold(g, spots, bias)
            return 0

        lax.fori_loop(0, (count - free + 1) // 2, k_loop, 0)
        cos = cos_ref[at, :]
        sin = sin_ref[at, :]
        low = (lane % HEAD) < HEAD // 2
        for g in range(groups):
            for pair in range(GROUP // 2):
                first = dq[g, 2 * pair * BQ : (2 * pair + 1) * BQ]
                second = dq[g, (2 * pair + 1) * BQ : (2 * pair + 2) * BQ]
                z = jnp.where(left, first, pltpu.roll(second, HEAD, 1)) * SCALE
                z = z * cos - half_turn(z, low) * sin
                column = (g * GROUP // 2 + pair) * LANES
                dq_ref[at, column : column + LANES] = z.astype(BF16)
        return 0

    lax.fori_loop(0, rows // BQ, q_loop, 0)
    factor = jnp.where(lane < HEAD, SCALE, 1.0)
    for e in range(span):
        target = near_ref if e % 2 == 0 else far_ref
        first = (block ^ e) * rows

        def leave(n, _):
            at = pl.ds(pl.multiple_of(n * BQ, BQ), BQ)
            source = pl.ds(pl.multiple_of(first + n * BQ, BQ), BQ)
            for g in range(groups):
                target[e // 2, g, at, :] = (dkv[g, source, :] * factor).astype(BF16)
            return 0

        lax.fori_loop(0, rows // BQ, leave, 0)


def attention_backward(heads, meta, q, da, att, lse, cos, sin, kvs, info, seg):
    rows = q.shape[1]
    span = len(kvs)
    keys = span * rows
    tiles = keys // BK
    groups = heads[1]
    work = 36 * 10**9 * groups
    return pl.pallas_call(
        functools.partial(backward_kernel, tiles=tiles, span=span, heads=heads),
        out_shape=[
            jax.ShapeDtypeStruct((rows, groups * GROUP * HEAD), BF16),
            jax.ShapeDtypeStruct((span // 2, groups, rows, LANES), BF16),
            jax.ShapeDtypeStruct((span // 2, groups, rows, LANES), BF16),
        ],
        in_specs=[SMEM_SPACE] + [VMEM_SPACE] * 6 + [ANY_SPACE] * span + [VMEM_SPACE] * 2,
        out_specs=[VMEM_SPACE] * 3,
        scratch_shapes=[
            pltpu.VMEM((groups, keys, LANES), BF16),
            pltpu.VMEM((groups, keys, LANES), BF16),
            pltpu.VMEM((groups, keys, LANES), F32),
            pltpu.VMEM((groups, STACK, LANES), F32),
            pltpu.VMEM((groups, 2 * STACK, LANES), BF16),
            pltpu.VMEM((groups, 2 * STACK, LANES), BF16),
            pltpu.SemaphoreType.DMA((span,)),
        ],
        compiler_params=params(56),
        cost_estimate=pl.CostEstimate(
            flops=work, bytes_accessed=30 * 10**6, transcendentals=3 * 10**7
        ),
        name="attention_backward",
    )(meta, q, da, att, lse, cos, sin, *kvs, info, seg)


def middle_kernel(place_ref, x_ref, att_ref, gain_ref, *refs):
    piece_refs, (mid_ref, n_ref, w_ref, sems) = refs[:-4], refs[-4:]
    for copy in assembly(place_ref, piece_refs, w_ref, sems):
        copy.wait()
    mid_ref[...] = dot_tr(att_ref[...], w_ref[...])
    gain2 = gain_ref[1:2, :]

    def norm(i, _):
        at = pl.ds(pl.multiple_of(i * BQ, BQ), BQ)
        mid = x_ref[at, :].astype(F32) + mid_ref[at, :]
        scale = lax.rsqrt(jnp.mean(mid * mid, axis=1, keepdims=True) + EPSILON)
        mid_ref[at, :] = mid
        n_ref[at, :] = (mid * scale * gain2).astype(BF16)
        return 0

    lax.fori_loop(0, mid_ref.shape[0] // BQ, norm, 0)


def middle(x, att, gains, pieces, place):
    rows = x.shape[0]
    count = sum(p.shape[0] for p in pieces)
    return pl.pallas_call(
        middle_kernel,
        out_shape=[
            jax.ShapeDtypeStruct((rows, D), F32),
            jax.ShapeDtypeStruct((rows, D), BF16),
            jax.ShapeDtypeStruct((D, D), BF16),
        ],
        in_specs=[SMEM_SPACE] + [VMEM_SPACE] * 3 + [ANY_SPACE] * len(pieces),
        out_specs=[VMEM_SPACE] * 3,
        scratch_shapes=[pltpu.SemaphoreType.DMA((count,))],
        compiler_params=params(32),
        name="middle",
    )(place, x, att, gains, *pieces)


def feed_forward_kernel(
    n1_ref, n2_ref, og1_ref, og2_ref, wg_ref, wu_ref, wd_ref,
    own_ref, far_ref, dw_ref,
    n, og, nt, ogt, oacc, nacc, hid, dgate, dup,
):
    f = pl.program_id(0)
    part = pl.program_id(1)
    rows = n1_ref.shape[0]

    @pl.when((f == 0) & (part == 0))
    def _():
        n[:rows] = n1_ref[...]
        n[rows:] = n2_ref[...]
        og[:rows] = og1_ref[...]
        og[rows:] = og2_ref[...]
        nt[...] = n[...].T
        ogt[...] = og[...].T
        oacc[...] = jnp.zeros_like(oacc)
        nacc[...] = jnp.zeros_like(nacc)

    @pl.when(part == 0)
    def _():
        for k in range(2):
            at = slice(k * rows, (k + 1) * rows)
            gate = dot(n[at], wg_ref[...])
            up = dot(n[at], wu_ref[...])
            grad = dot(og[at], wd_ref[...])
            sig = jax.nn.sigmoid(gate)
            silu = gate * sig
            hid[at] = (silu * up).astype(BF16)
            dgate[at] = (grad * up * sig * (1.0 + gate * (1.0 - sig))).astype(BF16)
            dup[at] = (grad * silu).astype(BF16)
        dw_ref[...] = dot(nt[...], dgate[...]).astype(BF16)

    @pl.when(part == 1)
    def _():
        nacc[...] += dot_tr(dgate[...], wg_ref[...]) + dot_tr(dup[...], wu_ref[...])
        dw_ref[...] = dot(nt[...], dup[...]).astype(BF16)

    @pl.when(part == 2)
    def _():
        oacc[...] += dot_tr(hid[...], wd_ref[...])
        dw_ref[...] = dot(ogt[...], hid[...]).astype(BF16)

    @pl.when((f == pl.num_programs(0) - 1) & (part == 2))
    def _():
        own_ref[0] = oacc[:rows].astype(BF16)
        own_ref[1] = nacc[:rows].astype(BF16)
        far_ref[0] = oacc[rows:].astype(BF16)
        far_ref[1] = nacc[rows:].astype(BF16)


def feed_forward(n_own, n_far, og_own, og_far, w):
    rows = n_own.shape[0]
    block = 256
    steps = HALF // block
    whole = pl.BlockSpec((rows, D), lambda f, k: (0, 0), pipeline_mode=pl.Buffered(1))
    sides = pl.BlockSpec((2, rows, D), lambda f, k: (0, 0, 0))
    slab = [pl.BlockSpec((D, block), lambda f, k, m=m: (0, m * steps + f)) for m in range(3)]
    return pl.pallas_call(
        feed_forward_kernel,
        grid=(steps, 3),
        in_specs=[whole] * 4 + slab,
        out_specs=[sides, sides, pl.BlockSpec((D, block), lambda f, k: (0, k * steps + f))],
        out_shape=[
            jax.ShapeDtypeStruct((2, rows, D), BF16),
            jax.ShapeDtypeStruct((2, rows, D), BF16),
            jax.ShapeDtypeStruct((D, 3 * HALF), BF16),
        ],
        scratch_shapes=[
            pltpu.VMEM((2 * rows, D), BF16),
            pltpu.VMEM((2 * rows, D), BF16),
            pltpu.VMEM((D, 2 * rows), BF16),
            pltpu.VMEM((D, 2 * rows), BF16),
            pltpu.VMEM((2 * rows, D), F32),
            pltpu.VMEM((2 * rows, D), F32),
            pltpu.VMEM((2 * rows, block), BF16),
            pltpu.VMEM((2 * rows, block), BF16),
            pltpu.VMEM((2 * rows, block), BF16),
        ],
        compiler_params=params(62),
        cost_estimate=pl.CostEstimate(
            flops=52 * 10**9, bytes_accessed=40 * 10**6, transcendentals=3 * 10**6
        ),
        name="feed_forward",
    )(n_own, n_far, og_own, og_far, w, w, w)


def turn_kernel(
    mid_ref, own_ref, got_ref, og_ref, gain_ref, w_ref, att_ref,
    out_ref, gm_ref, da_ref, dw_ref, dgain_ref, gmb,
):
    gain2 = gain_ref[1:2, :]

    def step(i, dgain):
        at = pl.ds(pl.multiple_of(i * BQ, BQ), BQ)
        mid = mid_ref[at, :]
        out = mid + (own_ref[0, at, :].astype(F32) + got_ref[0, at, :].astype(F32))
        out_ref[at, :] = out.astype(BF16)
        dn = own_ref[1, at, :].astype(F32) + got_ref[1, at, :].astype(F32)
        scale = lax.rsqrt(jnp.mean(mid * mid, axis=1, keepdims=True) + EPSILON)
        dgain = dgain + jnp.sum((dn * mid * scale).reshape(BQ // 8, 8, D), axis=0)
        q2 = dn * gain2
        mean = jnp.mean(q2 * mid, axis=1, keepdims=True)
        gm = og_ref[at, :].astype(F32) + scale * q2 - mid * (scale * scale * scale * mean)
        gm_ref[at, :] = gm
        gmb[at, :] = gm.astype(BF16)
        return dgain

    dgain = lax.fori_loop(0, mid_ref.shape[0] // BQ, step, jnp.zeros((8, D), F32))
    dgain_ref[...] = dgain
    da_ref[...] = dot(gmb[...], w_ref[...]).astype(BF16)
    dw_ref[...] = dot_cc(gmb[...], att_ref[...]).astype(BF16)


def turn(mid, own, got, og, gains, w, att):
    rows = mid.shape[0]
    return pl.pallas_call(
        turn_kernel,
        out_shape=[
            jax.ShapeDtypeStruct((rows, D), BF16),
            jax.ShapeDtypeStruct((rows, D), F32),
            jax.ShapeDtypeStruct((rows, D), BF16),
            jax.ShapeDtypeStruct((D, D), BF16),
            jax.ShapeDtypeStruct((8, D), F32),
        ],
        scratch_shapes=[pltpu.VMEM((rows, D), BF16)],
        compiler_params=params(56),
        name="turn",
    )(mid, own, got, og, gains, w, att)


def query_grad_kernel(n_ref, dq_ref, dw_ref):
    dw_ref[...] = dot_cc(n_ref[...], dq_ref[...]).astype(BF16)


def query_grad(n, dq):
    return pl.pallas_call(
        query_grad_kernel,
        out_shape=jax.ShapeDtypeStruct((D, dq.shape[1]), BF16),
        compiler_params=params(32),
        cost_estimate=pl.CostEstimate(
            flops=4 * 10**9, bytes_accessed=10**7, transcendentals=0
        ),
        name="query_grad",
    )(n, dq)


def project_back_kernel(
    x_ref, n_ref, dqa_ref, dqb_ref, ka_refs, kb_refs, w_ref, dgain_ref,
    cos_ref, sin_ref, dn_ref, dw_ref, dz,
):
    rows = x_ref.shape[0]
    lane = lane_iota((BQ, LANES))
    low = (lane % HEAD) < HEAD // 2
    left = lane < HEAD
    first = dqa_ref.shape[1] // (GROUP * HEAD)

    def turn_back(i, _):
        at = pl.ds(pl.multiple_of(i * BQ, BQ), BQ)
        cos = cos_ref[at, :]
        sin = sin_ref[at, :]
        for g in range(KV_HEADS):
            refs, k, dq_ref = (ka_refs, g, dqa_ref) if g < first else (kb_refs, g - first, dqb_ref)
            z = sum(ref[k, at, :].astype(F32) for ref in refs)
            rot = z * cos - half_turn(z, low) * sin
            base = g * GROUP_COLS
            span = GROUP * HEAD
            dz[at, base : base + span] = dq_ref[at, k * span : (k + 1) * span]
            dz[at, base + span : base + span + LANES] = jnp.where(left, rot, z).astype(BF16)
        return 0

    lax.fori_loop(0, rows // BQ, turn_back, 0)
    kv_cols = [dz[:, g * GROUP_COLS + GROUP * HEAD : (g + 1) * GROUP_COLS] for g in range(KV_HEADS)]
    dw_ref[:, : KV_HEADS * LANES] = dot_cc(
        n_ref[...], jnp.concatenate(kv_cols, axis=1)
    ).astype(BF16)
    dn_ref[...] = dot_tr(dz[...], w_ref[:, :QKV])

    def step(i, dgain):
        at = pl.ds(pl.multiple_of(i * BQ, BQ), BQ)
        x = x_ref[at, :].astype(F32)
        scale = lax.rsqrt(jnp.mean(x * x, axis=1, keepdims=True) + EPSILON)
        return dgain + jnp.sum((dn_ref[at, :] * x * scale).reshape(BQ // 8, 8, D), axis=0)

    dgain1 = lax.fori_loop(0, rows // BQ, step, jnp.zeros((8, D), F32))
    dgain1 = jnp.sum(dgain1, axis=0, keepdims=True)
    dgain2 = jnp.sum(dgain_ref[...], axis=0, keepdims=True)
    row = lax.broadcasted_iota(jnp.int32, (LANES, D), 0)
    both = jnp.where(row == 0, dgain1, jnp.where(row == 1, dgain2, 0.0))
    dw_ref[:, KV_HEADS * LANES :] = both.T.astype(BF16)


def project_back(x, n, dqs, pieces, w, dgain, cos, sin):
    rows = x.shape[0]

    def kernel(x_ref, n_ref, dqa_ref, dqb_ref, *refs):
        count = len(pieces[0])
        return project_back_kernel(
            x_ref, n_ref, dqa_ref, dqb_ref, refs[:count], refs[count : 2 * count],
            *refs[2 * count :],
        )

    return pl.pallas_call(
        kernel,
        out_shape=[
            jax.ShapeDtypeStruct((rows, D), F32),
            jax.ShapeDtypeStruct((D, (KV_HEADS + 1) * LANES), BF16),
        ],
        scratch_shapes=[pltpu.VMEM((rows, QKV), BF16)],
        compiler_params=params(48),
        name="project_back",
    )(x, n, *dqs, *pieces[0], *pieces[1], w, dgain, cos, sin)


def input_grad_kernel(x_ref, gm_ref, dn_ref, gain_ref, in_ref):
    x = x_ref[...].astype(F32)
    scale = lax.rsqrt(jnp.mean(x * x, axis=1, keepdims=True) + EPSILON)
    q1 = dn_ref[...] * gain_ref[0:1, :]
    mean = jnp.mean(q1 * x, axis=1, keepdims=True)
    in_ref[...] = gm_ref[...] + scale * q1 - x * (scale * scale * scale * mean)


def input_gradient(x, gm, dn, gains):
    rows = x.shape[0]
    block = pl.BlockSpec((BQ, D), lambda i: (i, 0))
    return pl.pallas_call(
        input_grad_kernel,
        grid=(rows // BQ,),
        in_specs=[block] * 3 + [pl.BlockSpec((8, D), lambda i: (0, 0))],
        out_specs=block,
        out_shape=jax.ShapeDtypeStruct((rows, D), F32),
        compiler_params=params(32),
        cost_estimate=pl.CostEstimate(flops=10**7, bytes_accessed=10**7, transcendentals=0),
        name="input_gradient",
    )(x, gm, dn, gains)


def body(
    layer_in, out_grad, segment_ids, segment_parents, norm_gain1, w_query, w_key, w_value, w_output,
    norm_gain2, w_gate, w_up, w_down,
):
    size = lax.axis_size("fsdp")
    rows = layer_in.shape[0]
    span = TREE // rows
    shard = D // size
    me = lax.axis_index("fsdp")
    block = me % span
    tree = me // span
    core = me % 2

    def swap(v, bit):
        return lax.ppermute(v, "fsdp", [(i, i ^ bit) for i in range(size)])

    same_core = [list(range(c, size, 2)) for c in range(2)]

    trees = size // span
    chips = span // 2
    chip = block // 2

    def stage(*values):
        return lax.optimization_barrier(values)

    def half_columns(*weights):
        halves = [
            jnp.concatenate([w[:, c * w.shape[1] // 2 :][:, : w.shape[1] // 2] for w in weights], axis=1)
            for c in range(2)
        ]
        keep = jnp.where(core == 0, halves[0], halves[1])
        got = swap(jnp.where(core == 0, halves[1], halves[0]), 1)
        return jnp.where(
            core == 0, jnp.concatenate([keep, got], axis=0), jnp.concatenate([got, keep], axis=0)
        )

    def part(v, index, axis):
        return lax.dynamic_index_in_dim(v, index, axis, keepdims=False)

    def send_cores(grad):
        grad = grad.reshape(trees, chips, 2, shard, grad.shape[1])
        return part(grad, core, 2), swap(part(grad, 1 - core, 2), 1)

    def send_chips(total):
        return part(total, chip, 1), *(swap(part(total, chip ^ c, 1), 2 * c) for c in range(1, chips))

    def send_trees(total):
        if trees > 4:
            across = [list(range(k, size, span)) for k in range(span)]
            total = lax.psum_scatter(total, "fsdp", axis_index_groups=across)
            return (total.reshape(total.shape[-2:]),)
        return part(total, tree, 0), *(
            swap(part(total, tree ^ t, 0), span * t) for t in range(1, trees)
        )

    def add(terms):
        return sum((t.astype(F32) for t in terms[1:]), terms[0].astype(F32))

    def add16(terms):
        return add(terms).astype(BF16)

    turned = w_output.T
    grouped = [w_query.reshape(shard, KV_HEADS, GROUP * HEAD)]
    grouped += [w.reshape(shard, KV_HEADS, HEAD) for w in (w_key, w_value)]
    grouped = jnp.concatenate(grouped, axis=2).reshape(shard, QKV)
    gain_pair = jnp.stack([norm_gain1, norm_gain2], axis=1)
    gain_pair = jnp.pad(gain_pair, ((0, 0), (0, LANES - 2)))
    grouped = jnp.concatenate([grouped, gain_pair], axis=1)
    chip_rows = half_columns(grouped, w_gate, w_up, w_down.T, turned)
    ff_w = lax.all_gather(
        chip_rows[:, QKV_PAD // 2 :], "fsdp", tiled=True, axis_index_groups=same_core
    )
    qkv_rows = chip_rows[:, : QKV_PAD // 2]
    if trees > 4:
        qkv_rows = lax.all_gather(qkv_rows, "fsdp", tiled=True, axis_index_groups=same_core)[None]
        qkv_pieces, order = [qkv_rows], jnp.zeros((1,), jnp.int32)
    else:
        qkv_rows = jnp.stack([qkv_rows] + [swap(qkv_rows, span * t) for t in range(1, trees)])
        qkv_pieces = [qkv_rows] + [swap(qkv_rows, 2 * c) for c in range(1, chips)]
        order = [(tree ^ t) * chips + (chip ^ c) for c in range(chips) for t in range(trees)]
        order = jnp.stack(order)
    qkv_place = jnp.stack([core] * len(qkv_pieces) + [1 - core] * len(qkv_pieces))
    qkv_place = jnp.concatenate([qkv_place, order, order])
    qkv_pieces = qkv_pieces + [swap(p, 1) for p in qkv_pieces]

    tree_seg = segment_ids
    bit = 1
    while bit < span:
        other = swap(tree_seg, bit)
        first = (me & bit) == 0
        tree_seg = jnp.concatenate(
            [jnp.where(first, tree_seg, other), jnp.where(first, other, tree_seg)], axis=0
        )
        bit *= 2
    seg_count = segment_parents.shape[0] * span // size
    seg_base = tree * seg_count
    tree_seg = tree_seg - seg_base
    own_seg = segment_ids - seg_base
    ids = jnp.arange(seg_count, dtype=jnp.int32)
    parent = lax.dynamic_slice_in_dim(segment_parents, seg_base, seg_count) - seg_base

    def look(index, table):
        return jnp.sum(jnp.where(index[:, None] == ids[None, :], table[None, :], 0), axis=1)

    grand = look(parent, parent)
    lengths = jnp.sum((tree_seg[None, :] == ids[:, None]).astype(jnp.int32), axis=1)
    starts = jnp.sum(jnp.where(ids[None, :] < ids[:, None], lengths[None, :], 0), axis=1)
    depth = jnp.where(parent != ids, look(parent, lengths), 0)
    depth = depth + jnp.where(grand != parent, look(grand, lengths), 0)
    own_row = block * rows + jnp.arange(rows, dtype=jnp.int32)
    positions = (look(own_seg, depth - starts) + own_row).astype(F32)
    lane = jnp.arange(LANES, dtype=jnp.int32)
    inverse = jnp.exp((lane % 32).astype(F32) * (-2.0 * math.log(ROPE_BASE) / HEAD))
    angles = positions[:, None] * inverse[None, :]
    cos = jnp.cos(angles)
    sin = jnp.sin(angles) * jnp.where(lane % HEAD < HEAD // 2, -1.0, 1.0)[None, :]
    info = [own_seg, look(own_seg, parent), look(own_seg, grand), own_row]
    info = sum(jnp.where(lane[None, :] == c, v[:, None], 0) for c, v in enumerate(info))
    tiles = TREE // BK
    steps = rows // BQ
    tile_seg = tree_seg.reshape(tiles, BK)
    tile_first, tile_last = tile_seg[:, 0], tile_seg[:, -1]
    step_seg = own_seg.reshape(steps, BQ)

    def inside(s):
        return (tile_first[None, :] <= s[:, None]) & (s[:, None] <= tile_last[None, :])

    hit = inside(ids) | inside(parent) | inside(grand)
    here = (step_seg[:, :1] <= ids[None, :]) & (ids[None, :] <= step_seg[:, -1:])
    active = jnp.any(here[:, :, None] & hit[None, :, :], axis=1)
    tile_range = jnp.arange(tiles, dtype=jnp.int32)
    last_row = block * rows + (jnp.arange(steps, dtype=jnp.int32) + 1) * BQ - 1
    active = active & (tile_range[None, :] * BK <= last_row[:, None])
    before = tile_range[:, None] < tile_range[None, :]
    place = jnp.sum((active[:, :, None] & before[None]).astype(jnp.int32), axis=1)
    barred = (ids[None, :] != ids[:, None]) & (ids[None, :] != parent[:, None])
    barred = barred & (ids[None, :] != grand[:, None])
    tile_has = (tile_first[:, None] <= ids[None, :]) & (ids[None, :] <= tile_last[:, None])
    barred = jnp.any(barred[:, None, :] & tile_has[None, :, :], axis=2)
    barred = jnp.any(here[:, :, None] & barred[None, :, :], axis=1)
    whole = active & ~barred & ((tile_range[None, :] + 1) * BK <= last_row[:, None] - BQ + 1)
    whole_count = jnp.sum(whole.astype(jnp.int32), axis=1)
    rank = jnp.sum((whole[:, :, None] & before[None]).astype(jnp.int32), axis=1)
    place = jnp.where(whole, rank, whole_count[:, None] + place - rank)
    chosen = active[:, :, None] & (place[:, :, None] == tile_range[None, None, :])
    listed = jnp.sum(jnp.where(chosen, tile_range[None, :, None], 0), axis=1)
    counts = jnp.sum(active.astype(jnp.int32), axis=1)
    counts = [jnp.pad(v, (0, BQ // 2 - steps)) for v in (counts, whole_count)]
    meta = jnp.concatenate([block[None], *counts, listed.reshape(steps * tiles)])
    seg_row = tree_seg[None, :]

    og_far = swap(out_grad, 1)
    normed1, q, kv, gains, qkv_w, q_top = project(qkv_place, layer_in, cos, sin, qkv_pieces)
    kvs = [kv, swap(kv, 1)]
    for c in range(1, chips):
        piece = swap(kv, 2 * c)
        kvs += [piece, swap(piece, 1)]
    att, lse = attention_forward(meta, q, q_top, kvs, info, seg_row)
    att, ff_w = stage(att, ff_w)
    out_w = ff_w[None, :, 3 * HALF :]
    out_place = jnp.stack([core, 1 - core, 0, 0])
    mid, normed2, out_w = middle(layer_in, att, gains, [out_w, swap(out_w, 1)], out_place)
    own, far, ff_dw = feed_forward(normed2, swap(normed2, 1), out_grad, og_far, ff_w)
    layer_out, grad_mid, da, out_dw, dgain2 = turn(
        mid, own, swap(far, 1), out_grad, gains, out_w, att
    )
    ff_dw = lax.psum_scatter(
        ff_dw, "fsdp", scatter_dimension=0, tiled=True, axis_index_groups=same_core
    )

    def backward(n, meta):
        return attention_backward(
            HEAD_PARTS[n], meta, q, da, att, lse, cos, sin, kvs, info, seg_row
        )

    def meet(near, far):
        got = swap(far, 1)
        return [near[0], got[0]], [add16((near[c], got[c])) for c in range(1, chips)]

    dq_a, near, far = backward(0, meta)
    pieces_a, both = meet(near, far)
    query_a = query_grad(normed1, dq_a)
    meta_b, early, *both = stage(meta, jnp.concatenate([out_dw, query_a], axis=1), *both)
    both = [swap(v, 2 * c + 2) for c, v in enumerate(both)]
    early = send_cores(early)
    dq_b, near, far = backward(1, meta_b)
    near, far, dq_b, *values = stage(near, far, dq_b, *both, *early)
    pieces_a += values[: len(both)]
    early = add16(values[len(both) :])
    pieces_b, both = meet(near, far)
    query_b = query_grad(normed1, dq_b)
    early, query_b, *both = stage(early, query_b, *both)
    pieces_b += [swap(v, 2 * c + 2) for c, v in enumerate(both)]
    early = send_chips(early)
    dn, kv_dw = project_back(
        layer_in, normed1, (dq_a, dq_b), (pieces_a, pieces_b), qkv_w, dgain2, cos, sin
    )
    late = jnp.concatenate([kv_dw, query_b], axis=1)
    late, dn, *early = stage(late, dn, *early)
    early, late = send_trees(add16(early)), send_cores(late)
    input_grad = input_gradient(layer_in, grad_mid, dn, gains)
    early, late = add(early), add16(late)
    late = add(send_trees(add16(send_chips(late))))
    out_dw, kv_dw = early[:, :D], late[:, : (KV_HEADS + 1) * LANES]
    query_dw = jnp.concatenate([early[:, D:], late[:, (KV_HEADS + 1) * LANES :]], axis=1)

    groups = kv_dw[:, : KV_HEADS * LANES].reshape(shard, KV_HEADS, LANES)
    grad_key = groups[:, :, :HEAD].reshape(shard, KV_HEADS * HEAD)
    grad_value = groups[:, :, HEAD:].reshape(shard, KV_HEADS * HEAD)

    def join(grad):
        mine, other = grad[:shard], grad[shard:]
        keep = jnp.where(core == 0, mine, other)
        got = swap(jnp.where(core == 0, other, mine), 1)
        low = jnp.where(core == 0, keep, got).astype(F32).reshape(shard, -1, HALF)
        high = jnp.where(core == 0, got, keep).astype(F32).reshape(shard, -1, HALF)
        return jnp.concatenate([low, high], axis=2)

    ff_grads = join(ff_dw)
    return (
        layer_out,
        input_grad,
        kv_dw[:, KV_HEADS * LANES],
        query_dw,
        grad_key,
        grad_value,
        out_dw.T,
        kv_dw[:, KV_HEADS * LANES + 1],
        ff_grads[:, 0],
        ff_grads[:, 1],
        ff_grads[:, 2].T,
    )


def solution(mesh):
    rows, cols, flat = P("fsdp", None), P(None, "fsdp"), P("fsdp")
    return jax.shard_map(
        body,
        mesh=mesh,
        in_specs=(rows, rows, flat, P(), flat, rows, rows, rows, cols, flat, rows, rows, cols),
        out_specs=(rows, rows, flat, rows, rows, rows, cols, flat, rows, rows, cols),
        check_vma=False,
    )
```

```python
import functools
import math

import jax
import jax.numpy as jnp
from jax import lax
from jax.experimental import pallas as pl
from jax.experimental.pallas import tpu as pltpu
from jax.sharding import PartitionSpec as P

HEADS = 20
KV_HEADS = 5
GROUP = HEADS // KV_HEADS
HEAD = 64
TREE = 5120
D = 1280
FF = 3584
HALF = FF // 2
LANES = 128
GROUP_COLS = GROUP * HEAD + 2 * HEAD
QKV = KV_HEADS * GROUP_COLS
QKV_PAD = QKV + LANES
BQ = 160
BK = 256
STACK = GROUP * BQ
FF_BLOCK = 256
FF_STEPS = (4, 3)
HEAD_PARTS = ((0, 3), (3, 2))

EPSILON = 1e-05
ROPE_BASE = 10000.0
MASKED = -1e30
SCALE = HEAD**-0.5
SCALE2 = SCALE * math.log2(math.e)
SAFE_EXPONENT = 60.0
FAR = 1 << 20

F32 = jnp.float32
BF16 = jnp.bfloat16
ROWS_BY_ROWS = (((1,), (1,)), ((), ()))
COLS_BY_COLS = (((0,), (0,)), ((), ()))
SMALL = pl.CostEstimate(flops=10**6, bytes_accessed=10**4, transcendentals=0)
VMEM_SPACE = pl.BlockSpec(memory_space=pltpu.VMEM)
SMEM_SPACE = pl.BlockSpec(memory_space=pltpu.SMEM)
ANY_SPACE = pl.BlockSpec(memory_space=pl.ANY)


def params(mib):
    return pltpu.CompilerParams(vmem_limit_bytes=mib * 2**20)


def lane_iota(shape):
    return lax.broadcasted_iota(jnp.int32, shape, len(shape) - 1)


def dot(a, b):
    return jnp.dot(a, b, preferred_element_type=F32)


def dot_tr(a, b):
    return lax.dot_general(a, b, ROWS_BY_ROWS, preferred_element_type=F32)


def dot_cc(a, b):
    return lax.dot_general(a, b, COLS_BY_COLS, preferred_element_type=F32)


def half_turn(z, low):
    return jnp.where(low, pltpu.roll(z, LANES - 32, 1), pltpu.roll(z, 32, 1))


def assembly(place_ref, piece_refs, w, sems):
    copies = []
    for e, ref in enumerate(piece_refs):
        parts, rows, cols = ref.shape
        col = pl.multiple_of(place_ref[e] * cols, LANES)
        for part in range(parts):
            k = len(copies)
            row = pl.multiple_of(place_ref[len(piece_refs) + k] * rows, 16)
            to = w.at[pl.ds(row, rows), pl.ds(col, cols)]
            copies.append(pltpu.make_async_copy(ref.at[part], to, sems.at[k]))
    for copy in copies:
        copy.start()
    return copies


def project_kernel(place_ref, x_ref, cos_ref, sin_ref, *refs):
    piece_refs, (n_ref, q_ref, kv_ref, gain_ref, w_ref, top_ref, sems) = refs[:-7], refs[-7:]
    for copy in assembly(place_ref, piece_refs, w_ref, sems):
        copy.wait()
    gains = w_ref[:, QKV:].astype(F32).T
    gain_ref[...] = gains[:8, :]
    gain1 = gains[0:1, :]
    rows = x_ref.shape[0]

    def norm(i, _):
        at = pl.ds(i * BQ, BQ)
        x = x_ref[at, :].astype(F32)
        scale = lax.rsqrt(jnp.mean(x * x, axis=1, keepdims=True) + EPSILON)
        n_ref[at, :] = (x * scale * gain1).astype(BF16)
        return 0

    lax.fori_loop(0, rows // BQ, norm, 0)
    lane = lane_iota((rows, LANES))
    low = (lane % HEAD) < HEAD // 2
    left = lane < HEAD
    cos = cos_ref[...]
    sin = sin_ref[...]
    same = (lax.broadcasted_iota(jnp.int32, (LANES, LANES), 0) < HEAD) == left[:LANES]
    same = jnp.where(same, 1.0, 0.0).astype(BF16)

    def squares(z):
        sums = dot((z * z).astype(BF16), same)
        return jnp.max(sums.reshape(rows // 8, 8, LANES), axis=0)

    q_top = jnp.zeros((8, LANES), F32)
    k_top = jnp.zeros((8, LANES), F32)
    for g in range(KV_HEADS):
        z = dot(n_ref[...], w_ref[:, g * GROUP_COLS : (g + 1) * GROUP_COLS])
        for pair in range(GROUP // 2):
            zp = z[:, pair * LANES : (pair + 1) * LANES]
            rot = (zp * cos + half_turn(zp, low) * sin).astype(BF16).astype(F32)
            q_top = jnp.maximum(q_top, squares(rot))
            head = g * GROUP + 2 * pair
            q_ref[head] = jnp.where(left, rot, 0.0).astype(BF16)
            q_ref[head + 1] = jnp.where(left, pltpu.roll(rot, HEAD, 1), 0.0).astype(BF16)
        zk = z[:, GROUP * HEAD :]
        rot = zk * cos + half_turn(zk, low) * sin
        k_top = jnp.maximum(k_top, squares(rot))
        kv_ref[g, :rows] = jnp.where(left, rot, zk).astype(BF16)
    top_ref[...] = q_top
    k_top = jnp.max(jnp.where(left[:8], k_top, 0.0)) * 1.02
    kv_ref[:, rows:] = jnp.full((KV_HEADS, 16, LANES), k_top, F32).astype(BF16)


def project(place, x, cos, sin, pieces):
    rows = x.shape[0]
    count = sum(p.shape[0] for p in pieces)
    return pl.pallas_call(
        project_kernel,
        out_shape=[
            jax.ShapeDtypeStruct((rows, D), BF16),
            jax.ShapeDtypeStruct((HEADS, rows, LANES), BF16),
            jax.ShapeDtypeStruct((KV_HEADS, rows + 16, LANES), BF16),
            jax.ShapeDtypeStruct((8, D), F32),
            jax.ShapeDtypeStruct((D, QKV_PAD), BF16),
            jax.ShapeDtypeStruct((8, LANES), F32),
        ],
        in_specs=[SMEM_SPACE] + [VMEM_SPACE] * 3 + [ANY_SPACE] * len(pieces),
        out_specs=[VMEM_SPACE] * 6,
        scratch_shapes=[pltpu.SemaphoreType.DMA((count,))],
        compiler_params=params(48),
        name="project",
    )(place, x, cos, sin, *pieces)


def first_row(device, half, rows, span):
    device = device ^ (span - 1) if half else device
    return pl.multiple_of(device * rows + half * (rows // 2), BQ)


def gather_keys(block, kv_refs, kv, sems, heads):
    rows, span = kv_refs[0].shape[1] - 16, len(kv_refs)
    copies = []
    for e, ref in enumerate(kv_refs):
        for half in range(2):
            source = ref.at[heads, pl.ds(half * (rows // 2), rows // 2), :]
            to = kv.at[:, pl.ds(first_row(block ^ e, half, rows, span), rows // 2), :]
            copies.append(pltpu.make_async_copy(source, to, sems.at[2 * e + half]))
    return copies


def tile_pair(meta_ref, tiles, i, k):
    spots = []
    count = meta_ref[1 + i]
    for k in (k, k + 1):
        first = pl.multiple_of(meta_ref[1 + BQ + i * tiles + jnp.minimum(k, count - 1)] * BK, BK)
        spots.append((first, jnp.where(k < count, first, FAR)))
    return spots


def open_tiles(meta_ref, i):
    return meta_ref[1 + BQ // 2 + i] // 2 * 2


def mask_bias(info_ref, seg_ref, i, spots):
    info = info_ref[pl.ds(i * BQ, BQ), :]
    own, parent, grand, row = (info[:, c : c + 1] for c in range(4))
    parts = []
    for first, name in spots:
        seg = seg_ref[:, pl.ds(first, BK)]
        key_row = lane_iota((1, BK)) + name
        ok = ((seg == own) | (seg == parent) | (seg == grand)) & (key_row <= row)
        parts.append(jnp.where(ok, 0.0, MASKED))
    return jnp.concatenate(parts, axis=1)


def key_pair(kv, g, spots):
    return jnp.concatenate([kv[g, pl.ds(first, BK), :] for first, _ in spots], axis=0)


def masked(s, bias):
    return (s.reshape(GROUP, BQ, 2 * BK) * SCALE2 + bias[None]).reshape(STACK, 2 * BK)


def split_keys(kv, first, second):
    left = lane_iota((BK, LANES)) < HEAD
    one = jnp.ones((BK, LANES), BF16)

    def step(n, _):
        at = pl.ds(pl.multiple_of(n * BK, BK), BK)
        for g in range(kv.shape[0]):
            v = kv[g, at, :]
            second[g, at, :] = jnp.where(left, one, v)
            if first is not None:
                first[g, at, :] = jnp.where(left, v, one)
        return 0

    lax.fori_loop(0, kv.shape[1] // BK, step, 0)


def forward_kernel(meta_ref, q_ref, top_ref, *refs, tiles, span):
    kv_refs = refs[:span]
    info_ref, seg_ref, att_ref, lse_ref, kv, val, acc, top, k_tops, sems = refs[span:]
    rows = q_ref.shape[1]
    copies = gather_keys(meta_ref[0], kv_refs, kv, sems, pl.ds(0, KV_HEADS))
    for e, ref in enumerate(kv_refs):
        source = ref.at[0, pl.ds(rows, 16), :]
        copies.append(pltpu.make_async_copy(source, k_tops.at[e], sems.at[2 * span + e]))
    for copy in copies:
        copy.start()
    for copy in copies:
        copy.wait()
    split_keys(kv, None, val)

    def q_rows(i, g):
        at = pl.ds(pl.multiple_of(i * BQ, BQ), BQ)
        return q_ref[pl.ds(g * GROUP, GROUP), at, :].reshape(STACK, LANES)

    def fold(i, g, spots, bias, ceiling):
        s = dot_tr(q_rows(i, g), key_pair(kv, g, spots))
        s = s * SCALE2 if bias is None else masked(s, bias)
        if ceiling:
            s = s - top[g, :, 0:1]
        acc[g] += dot(jnp.exp2(s).astype(BF16), key_pair(val, g, spots))

    def finish(i, ceiling):
        at = pl.ds(pl.multiple_of(i * BQ, BQ), BQ)
        lane = lane_iota((BQ, LANES))
        logs = jnp.zeros((BQ, LANES), F32)
        for g in range(KV_HEADS):
            sums = acc[g]
            lse = jnp.log2(sums)
            if ceiling:
                lse = lse + top[g, :, 0:1]
            out = sums * pltpu.roll(1.0 / sums, HEAD, 1)
            for h in range(GROUP):
                logs = jnp.where(lane == g * GROUP + h, lse[h * BQ : (h + 1) * BQ, 0:1], logs)
            for pair in range(GROUP // 2):
                first = out[2 * pair * BQ : (2 * pair + 1) * BQ]
                second = out[(2 * pair + 1) * BQ : (2 * pair + 2) * BQ]
                both = jnp.where(lane < HEAD, pltpu.roll(first, HEAD, 1), second)
                column = (g * GROUP // 2 + pair) * LANES
                att_ref[at, column : column + LANES] = both.astype(BF16)
        lse_ref[at, :] = logs

    def run(ceiling):
        def q_loop(i, _):
            acc[...] = jnp.zeros_like(acc)
            count = meta_ref[1 + i]
            free = open_tiles(meta_ref, i)
            if ceiling:
                free = free * 0
                top[...] = jnp.full_like(top, 2 * MASKED)

                def top_loop(t, _):
                    spots = tile_pair(meta_ref, tiles, i, 2 * t)
                    bias = mask_bias(info_ref, seg_ref, i, spots)

                    def top_group(g, _):
                        s = masked(dot_tr(q_rows(i, g), key_pair(kv, g, spots)), bias)
                        top[g] = jnp.maximum(top[g], jnp.max(s, axis=1, keepdims=True))
                        return 0

                    lax.fori_loop(0, KV_HEADS, top_group, 0)
                    return 0

                lax.fori_loop(0, (count + 1) // 2, top_loop, 0)
            else:

                def open_loop(t, _):
                    spots = tile_pair(meta_ref, tiles, i, 2 * t)
                    for g in range(KV_HEADS):
                        fold(i, g, spots, None, False)
                    return 0

                lax.fori_loop(0, free // 2, open_loop, 0)

            def k_loop(t, _):
                spots = tile_pair(meta_ref, tiles, i, free + 2 * t)
                bias = mask_bias(info_ref, seg_ref, i, spots)
                if ceiling:

                    def group(g, _):
                        fold(i, g, spots, bias, True)
                        return 0

                    lax.fori_loop(0, KV_HEADS, group, 0)
                else:
                    for g in range(KV_HEADS):
                        fold(i, g, spots, bias, False)
                return 0

            lax.fori_loop(0, (count - free + 1) // 2, k_loop, 0)
            finish(i, ceiling)
            return 0

        lax.fori_loop(0, rows // BQ, q_loop, 0)

    bound = jnp.max(top_ref[...]) * jnp.max(k_tops[...].astype(F32))
    safe = bound < (SAFE_EXPONENT / SCALE2) ** 2

    @pl.when(safe)
    def _():
        run(False)

    @pl.when(jnp.logical_not(safe))
    def _():
        run(True)


def attention_forward(meta, q, top, kvs, info, seg):
    rows = q.shape[1]
    span = len(kvs)
    keys = span * rows
    tiles = keys // BK
    return pl.pallas_call(
        functools.partial(forward_kernel, tiles=tiles, span=span),
        out_shape=[
            jax.ShapeDtypeStruct((rows, D), BF16),
            jax.ShapeDtypeStruct((rows, LANES), F32),
        ],
        in_specs=[SMEM_SPACE] + [VMEM_SPACE] * 2 + [ANY_SPACE] * span + [VMEM_SPACE] * 2,
        out_specs=[VMEM_SPACE] * 2,
        scratch_shapes=[
            pltpu.VMEM((KV_HEADS, keys, LANES), BF16),
            pltpu.VMEM((KV_HEADS, keys, LANES), BF16),
            pltpu.VMEM((KV_HEADS, STACK, LANES), F32),
            pltpu.VMEM((KV_HEADS, STACK, LANES), F32),
            pltpu.VMEM((span, 16, LANES), BF16),
            pltpu.SemaphoreType.DMA((3 * span,)),
        ],
        compiler_params=params(52),
        cost_estimate=SMALL,
        name="attention_forward",
    )(meta, q, top, *kvs, info, seg)


def backward_kernel(
    meta_ref, q_ref, da_ref, att_ref, lse_ref, cos_ref, sin_ref, *refs, tiles, span, heads
):
    first_head, groups = heads
    kv_refs = refs[:span]
    info_ref, seg_ref, dq_ref, near_ref, far_ref, key, val, dkv, dq, qd, lifted, sems = refs[span:]
    rows = q_ref.shape[1]
    block = meta_ref[0]
    copies = gather_keys(block, kv_refs, key, sems, pl.ds(first_head, groups))
    for copy in copies:
        copy.start()

    def clear(n, _):
        dkv[:, pl.ds(n * BK, BK), :] = jnp.zeros((groups, BK, LANES), F32)
        return 0

    lax.fori_loop(0, key.shape[1] // BK, clear, 0)
    for copy in copies:
        copy.wait()
    split_keys(key, key, val)
    lane = lane_iota((BQ, LANES))
    left = lane < HEAD

    def lanes_of(column, first):
        out = jnp.zeros((BQ, LANES), F32)
        for k in range(3):
            top = column.astype(BF16).astype(F32)
            out = jnp.where(lane == first + k, top, out)
            column = column - top
        return out

    def q_loop(i, _):
        at = pl.ds(pl.multiple_of(i * BQ, BQ), BQ)
        dq[...] = jnp.zeros_like(dq)
        logs = lse_ref[at, :] * (-1.0 / SCALE2)
        for h in range(first_head * GROUP, (first_head + groups) * GROUP):
            g, r = h // GROUP - first_head, h % GROUP
            column = h // 2 * LANES
            da = da_ref[at, column : column + LANES].astype(F32)
            delta = da * att_ref[at, column : column + LANES].astype(F32)
            mine = left if h % 2 == 0 else jnp.logical_not(left)
            delta = jnp.sum(jnp.where(mine, delta, 0.0), axis=1, keepdims=True)
            if h % 2 == 0:
                da = pltpu.roll(da, HEAD, 1)
            q = q_ref[h, at, :]
            own = slice(r * BQ, (r + 1) * BQ)
            other = slice(STACK + r * BQ, STACK + (r + 1) * BQ)
            qd[g, own, :] = q
            qd[g, other, :] = jnp.where(left, 0.0, da).astype(BF16)
            lse = lanes_of(logs[:, h : h + 1], HEAD)
            lifted[g, own, :] = jnp.where(left, q.astype(F32), lse).astype(BF16)
            lifted[g, other, :] = jnp.where(left, lanes_of(-delta, 0), da).astype(BF16)

        def fold(g, spots, bias):
            keys = key_pair(key, g, spots)
            s = dot_tr(lifted[g, :STACK, :], keys)
            p = jnp.exp2(s * SCALE2 if bias is None else masked(s, bias))
            ds = (p * dot_tr(lifted[g, STACK:, :], key_pair(val, g, spots))).astype(BF16)
            p = p.astype(BF16)
            dq[g] += dot(ds, keys)
            moved = dot_cc(jnp.concatenate([ds, p], axis=0), qd[g])
            for n, (first, _) in enumerate(spots):
                dkv[g, pl.ds(first, BK), :] += moved[n * BK : (n + 1) * BK]

        count = meta_ref[1 + i]
        free = open_tiles(meta_ref, i)

        def open_loop(t, _):
            spots = tile_pair(meta_ref, tiles, i, 2 * t)
            for g in range(groups):
                fold(g, spots, None)
            return 0

        lax.fori_loop(0, free // 2, open_loop, 0)

        def k_loop(t, _):
            spots = tile_pair(meta_ref, tiles, i, free + 2 * t)
            bias = mask_bias(info_ref, seg_ref, i, spots)
            for g in range(groups):
                fold(g, spots, bias)
            return 0

        lax.fori_loop(0, (count - free + 1) // 2, k_loop, 0)
        cos = cos_ref[at, :]
        sin = sin_ref[at, :]
        low = (lane % HEAD) < HEAD // 2
        for g in range(groups):
            for pair in range(GROUP // 2):
                first = dq[g, 2 * pair * BQ : (2 * pair + 1) * BQ]
                second = dq[g, (2 * pair + 1) * BQ : (2 * pair + 2) * BQ]
                z = jnp.where(left, first, pltpu.roll(second, HEAD, 1)) * SCALE
                z = z * cos - half_turn(z, low) * sin
                column = (g * GROUP // 2 + pair) * LANES
                dq_ref[at, column : column + LANES] = z.astype(BF16)
        return 0

    lax.fori_loop(0, rows // BQ, q_loop, 0)
    factor = jnp.where(lane < HEAD, SCALE, 1.0)
    for e in range(span):
        target = near_ref if e % 2 == 0 else far_ref
        for half in range(2):
            first = first_row(block ^ e, half, rows, span)

            def leave(n, _):
                at = pl.ds(pl.multiple_of(half * (rows // 2) + n * BQ, BQ), BQ)
                source = pl.ds(pl.multiple_of(first + n * BQ, BQ), BQ)
                for g in range(groups):
                    target[e // 2, g, at, :] = (dkv[g, source, :] * factor).astype(BF16)
                return 0

            lax.fori_loop(0, rows // 2 // BQ, leave, 0)


def attention_backward(heads, meta, q, da, att, lse, cos, sin, kvs, info, seg):
    rows = q.shape[1]
    span = len(kvs)
    keys = span * rows
    tiles = keys // BK
    groups = heads[1]
    return pl.pallas_call(
        functools.partial(backward_kernel, tiles=tiles, span=span, heads=heads),
        out_shape=[
            jax.ShapeDtypeStruct((rows, groups * GROUP * HEAD), BF16),
            jax.ShapeDtypeStruct((span // 2, groups, rows, LANES), BF16),
            jax.ShapeDtypeStruct((span // 2, groups, rows, LANES), BF16),
        ],
        in_specs=[SMEM_SPACE] + [VMEM_SPACE] * 6 + [ANY_SPACE] * span + [VMEM_SPACE] * 2,
        out_specs=[VMEM_SPACE] * 3,
        scratch_shapes=[
            pltpu.VMEM((groups, keys, LANES), BF16),
            pltpu.VMEM((groups, keys, LANES), BF16),
            pltpu.VMEM((groups, keys, LANES), F32),
            pltpu.VMEM((groups, STACK, LANES), F32),
            pltpu.VMEM((groups, 2 * STACK, LANES), BF16),
            pltpu.VMEM((groups, 2 * STACK, LANES), BF16),
            pltpu.SemaphoreType.DMA((2 * span,)),
        ],
        compiler_params=params(56),
        cost_estimate=SMALL,
        name="attention_backward",
    )(meta, q, da, att, lse, cos, sin, *kvs, info, seg)


def middle_kernel(place_ref, x_ref, att_ref, gain_ref, *refs):
    piece_refs, (mid_ref, n_ref, w_ref, sems) = refs[:-4], refs[-4:]
    for copy in assembly(place_ref, piece_refs, w_ref, sems):
        copy.wait()
    mid_ref[...] = dot_tr(att_ref[...], w_ref[...])
    gain2 = gain_ref[1:2, :]

    def norm(i, _):
        at = pl.ds(pl.multiple_of(i * BQ, BQ), BQ)
        mid = x_ref[at, :].astype(F32) + mid_ref[at, :]
        scale = lax.rsqrt(jnp.mean(mid * mid, axis=1, keepdims=True) + EPSILON)
        mid_ref[at, :] = mid
        n_ref[at, :] = (mid * scale * gain2).astype(BF16)
        return 0

    lax.fori_loop(0, mid_ref.shape[0] // BQ, norm, 0)


def middle(x, att, gains, pieces, place):
    rows = x.shape[0]
    count = sum(p.shape[0] for p in pieces)
    return pl.pallas_call(
        middle_kernel,
        out_shape=[
            jax.ShapeDtypeStruct((rows, D), F32),
            jax.ShapeDtypeStruct((rows, D), BF16),
            jax.ShapeDtypeStruct((D, D), BF16),
        ],
        in_specs=[SMEM_SPACE] + [VMEM_SPACE] * 3 + [ANY_SPACE] * len(pieces),
        out_specs=[VMEM_SPACE] * 3,
        scratch_shapes=[pltpu.SemaphoreType.DMA((count,))],
        compiler_params=params(32),
        name="middle",
    )(place, x, att, gains, *pieces)


def feed_forward_kernel(
    n1_ref, n2_ref, og1_ref, og2_ref, wg_ref, wu_ref, wd_ref, *refs, later
):
    priors, refs = refs[: 2 * later], refs[2 * later :]
    own_ref, far_ref, dw_ref, n, og, nt, ogt, oacc, nacc, hid, dgate, dup = refs
    f = pl.program_id(0)
    part = pl.program_id(1)
    rows = n1_ref.shape[0]

    @pl.when((f == 0) & (part == 0))
    def _():
        n[:rows] = n1_ref[...]
        n[rows:] = n2_ref[...]
        og[:rows] = og1_ref[...]
        og[rows:] = og2_ref[...]
        nt[...] = n[...].T
        ogt[...] = og[...].T
        if later:
            for k, (prior, target) in enumerate(zip(priors, (own_ref, far_ref))):
                pltpu.sync_copy(prior, target)
                oacc[k * rows : (k + 1) * rows] = target[0].astype(F32)
                nacc[k * rows : (k + 1) * rows] = target[1].astype(F32)
        else:
            oacc[...] = jnp.zeros_like(oacc)
            nacc[...] = jnp.zeros_like(nacc)

    @pl.when(part == 0)
    def _():
        for k in range(2):
            at = slice(k * rows, (k + 1) * rows)
            gate = dot(n[at], wg_ref[...])
            up = dot(n[at], wu_ref[...])
            grad = dot(og[at], wd_ref[...])
            sig = jax.nn.sigmoid(gate)
            silu = gate * sig
            hid[at] = (silu * up).astype(BF16)
            dgate[at] = (grad * up * sig * (1.0 + gate * (1.0 - sig))).astype(BF16)
            dup[at] = (grad * silu).astype(BF16)
        dw_ref[...] = dot(nt[...], dgate[...]).astype(BF16)

    @pl.when(part == 1)
    def _():
        nacc[...] += dot_tr(dgate[...], wg_ref[...]) + dot_tr(dup[...], wu_ref[...])
        dw_ref[...] = dot(nt[...], dup[...]).astype(BF16)

    @pl.when(part == 2)
    def _():
        oacc[...] += dot_tr(hid[...], wd_ref[...])
        dw_ref[...] = dot(ogt[...], hid[...]).astype(BF16)

    @pl.when((f == pl.num_programs(0) - 1) & (part == 2))
    def _():
        own_ref[0] = oacc[:rows].astype(BF16)
        own_ref[1] = nacc[:rows].astype(BF16)
        far_ref[0] = oacc[rows:].astype(BF16)
        far_ref[1] = nacc[rows:].astype(BF16)


def feed_forward(steps, n_own, n_far, og_own, og_far, w, priors=()):
    rows = n_own.shape[0]
    block = FF_BLOCK
    whole = pl.BlockSpec((rows, D), lambda f, k: (0, 0), pipeline_mode=pl.Buffered(1))
    sides = pl.BlockSpec((2, rows, D), lambda f, k: (0, 0, 0))
    slab = [pl.BlockSpec((D, block), lambda f, k, m=m: (0, m * steps + f)) for m in range(3)]
    return pl.pallas_call(
        functools.partial(feed_forward_kernel, later=bool(priors)),
        grid=(steps, 3),
        in_specs=[whole] * 4 + slab + [ANY_SPACE] * len(priors),
        out_specs=[sides, sides, pl.BlockSpec((D, block), lambda f, k: (0, k * steps + f))],
        out_shape=[
            jax.ShapeDtypeStruct((2, rows, D), BF16),
            jax.ShapeDtypeStruct((2, rows, D), BF16),
            jax.ShapeDtypeStruct((D, 3 * steps * block), BF16),
        ],
        scratch_shapes=[
            pltpu.VMEM((2 * rows, D), BF16),
            pltpu.VMEM((2 * rows, D), BF16),
            pltpu.VMEM((D, 2 * rows), BF16),
            pltpu.VMEM((D, 2 * rows), BF16),
            pltpu.VMEM((2 * rows, D), F32),
            pltpu.VMEM((2 * rows, D), F32),
            pltpu.VMEM((2 * rows, block), BF16),
            pltpu.VMEM((2 * rows, block), BF16),
            pltpu.VMEM((2 * rows, block), BF16),
        ],
        compiler_params=params(62),
        cost_estimate=SMALL,
        name="feed_forward",
    )(n_own, n_far, og_own, og_far, w, w, w, *priors)


def turn_kernel(
    mid_ref, own_ref, got_ref, og_ref, gain_ref, w_ref, att_ref,
    out_ref, gm_ref, da_ref, dw_ref, dgain_ref, gmb,
):
    gain2 = gain_ref[1:2, :]

    def step(i, dgain):
        at = pl.ds(pl.multiple_of(i * BQ, BQ), BQ)
        mid = mid_ref[at, :]
        out = mid + (own_ref[0, at, :].astype(F32) + got_ref[0, at, :].astype(F32))
        out_ref[at, :] = out.astype(BF16)
        dn = own_ref[1, at, :].astype(F32) + got_ref[1, at, :].astype(F32)
        scale = lax.rsqrt(jnp.mean(mid * mid, axis=1, keepdims=True) + EPSILON)
        dgain = dgain + jnp.sum((dn * mid * scale).reshape(BQ // 8, 8, D), axis=0)
        q2 = dn * gain2
        mean = jnp.mean(q2 * mid, axis=1, keepdims=True)
        gm = og_ref[at, :].astype(F32) + scale * q2 - mid * (scale * scale * scale * mean)
        gm_ref[at, :] = gm
        gmb[at, :] = gm.astype(BF16)
        return dgain

    dgain = lax.fori_loop(0, mid_ref.shape[0] // BQ, step, jnp.zeros((8, D), F32))
    dgain_ref[...] = dgain
    da_ref[...] = dot(gmb[...], w_ref[...]).astype(BF16)
    dw_ref[...] = dot_cc(gmb[...], att_ref[...]).astype(BF16)


def turn(mid, own, got, og, gains, w, att):
    rows = mid.shape[0]
    return pl.pallas_call(
        turn_kernel,
        out_shape=[
            jax.ShapeDtypeStruct((rows, D), BF16),
            jax.ShapeDtypeStruct((rows, D), F32),
            jax.ShapeDtypeStruct((rows, D), BF16),
            jax.ShapeDtypeStruct((D, D), BF16),
            jax.ShapeDtypeStruct((8, D), F32),
        ],
        scratch_shapes=[pltpu.VMEM((rows, D), BF16)],
        compiler_params=params(56),
        name="turn",
    )(mid, own, got, og, gains, w, att)


def project_back_kernel(
    x_ref, n_ref, dqa_ref, dqb_ref, ka_refs, kb_refs, w_ref, dgain_ref,
    cos_ref, sin_ref, dn_ref, dw_ref, dz,
):
    rows = x_ref.shape[0]
    lane = lane_iota((BQ, LANES))
    low = (lane % HEAD) < HEAD // 2
    left = lane < HEAD
    first = dqa_ref.shape[1] // (GROUP * HEAD)

    def turn_back(i, _):
        at = pl.ds(pl.multiple_of(i * BQ, BQ), BQ)
        cos = cos_ref[at, :]
        sin = sin_ref[at, :]
        for g in range(KV_HEADS):
            refs, k, dq_ref = (ka_refs, g, dqa_ref) if g < first else (kb_refs, g - first, dqb_ref)
            z = sum(ref[k, at, :].astype(F32) for ref in refs)
            rot = z * cos - half_turn(z, low) * sin
            base = g * GROUP_COLS
            span = GROUP * HEAD
            dz[at, base : base + span] = dq_ref[at, k * span : (k + 1) * span]
            dz[at, base + span : base + span + LANES] = jnp.where(left, rot, z).astype(BF16)
        return 0

    lax.fori_loop(0, rows // BQ, turn_back, 0)
    dw_ref[:, :QKV] = dot_cc(n_ref[...], dz[...]).astype(BF16)
    dn_ref[...] = dot_tr(dz[...], w_ref[:, :QKV])

    def step(i, dgain):
        at = pl.ds(pl.multiple_of(i * BQ, BQ), BQ)
        x = x_ref[at, :].astype(F32)
        scale = lax.rsqrt(jnp.mean(x * x, axis=1, keepdims=True) + EPSILON)
        return dgain + jnp.sum((dn_ref[at, :] * x * scale).reshape(BQ // 8, 8, D), axis=0)

    dgain1 = lax.fori_loop(0, rows // BQ, step, jnp.zeros((8, D), F32))
    dgain1 = jnp.sum(dgain1, axis=0, keepdims=True)
    dgain2 = jnp.sum(dgain_ref[...], axis=0, keepdims=True)
    row = lax.broadcasted_iota(jnp.int32, (LANES, D), 0)
    both = jnp.where(row == 0, dgain1, jnp.where(row == 1, dgain2, 0.0))
    dw_ref[:, QKV:] = both.T.astype(BF16)


def project_back(x, n, dqs, pieces, w, dgain, cos, sin):
    rows = x.shape[0]

    def kernel(x_ref, n_ref, dqa_ref, dqb_ref, *refs):
        count = len(pieces[0])
        return project_back_kernel(
            x_ref, n_ref, dqa_ref, dqb_ref, refs[:count], refs[count : 2 * count],
            *refs[2 * count :],
        )

    return pl.pallas_call(
        kernel,
        out_shape=[
            jax.ShapeDtypeStruct((rows, D), F32),
            jax.ShapeDtypeStruct((D, QKV_PAD), BF16),
        ],
        scratch_shapes=[pltpu.VMEM((rows, QKV), BF16)],
        compiler_params=params(48),
        name="project_back",
    )(x, n, *dqs, *pieces[0], *pieces[1], w, dgain, cos, sin)


def input_grad_kernel(x_ref, gm_ref, dn_ref, gain_ref, in_ref):
    x = x_ref[...].astype(F32)
    scale = lax.rsqrt(jnp.mean(x * x, axis=1, keepdims=True) + EPSILON)
    q1 = dn_ref[...] * gain_ref[0:1, :]
    mean = jnp.mean(q1 * x, axis=1, keepdims=True)
    in_ref[...] = gm_ref[...] + scale * q1 - x * (scale * scale * scale * mean)


def input_gradient(x, gm, dn, gains):
    rows = x.shape[0]
    block = pl.BlockSpec((BQ, D), lambda i: (i, 0))
    return pl.pallas_call(
        input_grad_kernel,
        grid=(rows // BQ,),
        in_specs=[block] * 3 + [pl.BlockSpec((8, D), lambda i: (0, 0))],
        out_specs=block,
        out_shape=jax.ShapeDtypeStruct((rows, D), F32),
        compiler_params=params(32),
        cost_estimate=SMALL,
        name="input_gradient",
    )(x, gm, dn, gains)


def body(
    layer_in, out_grad, segment_ids, segment_parents, norm_gain1, w_query, w_key, w_value, w_output,
    norm_gain2, w_gate, w_up, w_down,
):
    size = lax.axis_size("fsdp")
    rows = layer_in.shape[0]
    span = TREE // rows
    shard = D // size
    me = lax.axis_index("fsdp")
    block = me % span
    tree = me // span
    core = me % 2

    def swap(v, bit):
        return lax.ppermute(v, "fsdp", [(i, i ^ bit) for i in range(size)])

    same_core = [list(range(c, size, 2)) for c in range(2)]

    trees = size // span
    chips = span // 2
    chip = block // 2

    def stage(*values):
        return lax.optimization_barrier(values)

    def half_columns(*halves):
        keep = jnp.where(core == 0, halves[0], halves[1])
        got = swap(jnp.where(core == 0, halves[1], halves[0]), 1)
        return jnp.where(
            core == 0, jnp.concatenate([keep, got], axis=0), jnp.concatenate([got, keep], axis=0)
        )

    def part(v, index, axis):
        return lax.dynamic_index_in_dim(v, index, axis, keepdims=False)

    def send_cores(grad):
        grad = grad.reshape(trees, chips, 2, shard, grad.shape[1])
        return part(grad, core, 2), swap(part(grad, 1 - core, 2), 1)

    def send_chips(total):
        return part(total, chip, 1), *(swap(part(total, chip ^ c, 1), 2 * c) for c in range(1, chips))

    def send_trees(total):
        if trees > 4:
            across = [list(range(k, size, span)) for k in range(span)]
            total = lax.psum_scatter(total, "fsdp", axis_index_groups=across)
            return (total.reshape(total.shape[-2:]),)
        return part(total, tree, 0), *(
            swap(part(total, tree ^ t, 0), span * t) for t in range(1, trees)
        )

    def halve(v, bit, axis, distance):
        return part(v, bit, axis), swap(part(v, 1 - bit, axis), distance)

    def trees_first(v):
        if trees != 4:
            return (v,)
        return halve(v.reshape(2, 2, *v.shape[1:]), tree // 2, 0, 2 * span)

    def trees_second(v):
        return halve(v, tree % 2, 0, span) if trees == 4 else send_trees(v)

    def add(terms):
        return sum((t.astype(F32) for t in terms[1:]), terms[0].astype(F32))

    def add16(terms):
        return add(terms).astype(BF16)

    def even_out(v):
        return jnp.concatenate([v[: rows // 2], swap(v[rows // 2 :], span - 1).astype(v.dtype)])

    turned = w_output.T
    grouped = [w_query.reshape(shard, KV_HEADS, GROUP * HEAD)]
    grouped += [w.reshape(shard, KV_HEADS, HEAD) for w in (w_key, w_value)]
    grouped = jnp.concatenate(grouped, axis=2).reshape(shard, QKV)
    gain_pair = jnp.stack([norm_gain1, norm_gain2], axis=1)
    gain_pair = jnp.pad(gain_pair, ((0, 0), (0, LANES - 2)))
    grouped = jnp.concatenate([grouped, gain_pair], axis=1)

    def columns(c):
        parts = [grouped[:, c * QKV_PAD // 2 : (c + 1) * QKV_PAD // 2]]
        first = c * HALF
        for k, count in enumerate(FF_STEPS):
            last = first + count * FF_BLOCK
            parts += [w[:, first:last] for w in (w_gate, w_up, down)]
            if k == 0:
                parts += [turned[:, c * D // 2 : (c + 1) * D // 2]]
            first = last
        return jnp.concatenate(parts, axis=1)

    down = w_down.T
    chip_rows = half_columns(columns(0), columns(1))
    first, ff_w = QKV_PAD // 2, []
    for k, count in enumerate(FF_STEPS):
        last = first + 3 * count * FF_BLOCK + (D // 2 if k == 0 else 0)
        ff_w += [
            lax.all_gather(
                chip_rows[:, first:last], "fsdp", tiled=True, axis_index_groups=same_core
            )
        ]
        first = last
    qkv_rows = chip_rows[:, : QKV_PAD // 2]
    if trees > 4:
        qkv_rows = lax.all_gather(qkv_rows, "fsdp", tiled=True, axis_index_groups=same_core)[None]
        qkv_pieces, order = [qkv_rows], jnp.zeros((1,), jnp.int32)
    else:
        qkv_rows = jnp.stack([qkv_rows] + [swap(qkv_rows, span * t) for t in range(1, trees)])
        qkv_pieces = [qkv_rows] + [swap(qkv_rows, 2 * c) for c in range(1, chips)]
        order = [(tree ^ t) * chips + (chip ^ c) for c in range(chips) for t in range(trees)]
        order = jnp.stack(order)
    qkv_place = jnp.stack([core] * len(qkv_pieces) + [1 - core] * len(qkv_pieces))
    qkv_place = jnp.concatenate([qkv_place, order, order])
    qkv_pieces = qkv_pieces + [swap(p, 1) for p in qkv_pieces]

    tree_seg = segment_ids
    bit = 1
    while bit < span:
        other = swap(tree_seg, bit)
        first = (me & bit) == 0
        tree_seg = jnp.concatenate(
            [jnp.where(first, tree_seg, other), jnp.where(first, other, tree_seg)], axis=0
        )
        bit *= 2
    layer_in, tree_seg = stage(layer_in, tree_seg)
    tokens_in = even_out(layer_in)
    seg_count = segment_parents.shape[0] * span // size
    seg_base = tree * seg_count
    tree_seg = tree_seg - seg_base
    starts = [first_row(block, half, rows, span) for half in range(2)]
    own_row = jnp.concatenate([n + jnp.arange(rows // 2, dtype=jnp.int32) for n in starts])
    own_seg = jnp.concatenate(
        [lax.dynamic_slice_in_dim(tree_seg, n, rows // 2) for n in starts]
    )
    ids = jnp.arange(seg_count, dtype=jnp.int32)
    parent = lax.dynamic_slice_in_dim(segment_parents, seg_base, seg_count) - seg_base

    def look(index, table):
        return jnp.sum(jnp.where(index[:, None] == ids[None, :], table[None, :], 0), axis=1)

    grand = look(parent, parent)
    lengths = jnp.sum((tree_seg[None, :] == ids[:, None]).astype(jnp.int32), axis=1)
    starts = jnp.sum(jnp.where(ids[None, :] < ids[:, None], lengths[None, :], 0), axis=1)
    depth = jnp.where(parent != ids, look(parent, lengths), 0)
    depth = depth + jnp.where(grand != parent, look(grand, lengths), 0)
    positions = (look(own_seg, depth - starts) + own_row).astype(F32)
    lane = jnp.arange(LANES, dtype=jnp.int32)
    inverse = jnp.exp((lane % 32).astype(F32) * (-2.0 * math.log(ROPE_BASE) / HEAD))
    angles = positions[:, None] * inverse[None, :]
    cos = jnp.cos(angles)
    sin = jnp.sin(angles) * jnp.where(lane % HEAD < HEAD // 2, -1.0, 1.0)[None, :]
    info = [own_seg, look(own_seg, parent), look(own_seg, grand), own_row]
    info = sum(jnp.where(lane[None, :] == c, v[:, None], 0) for c, v in enumerate(info))
    tiles = TREE // BK
    steps = rows // BQ
    tile_seg = tree_seg.reshape(tiles, BK)
    tile_first, tile_last = tile_seg[:, 0], tile_seg[:, -1]
    step_seg = own_seg.reshape(steps, BQ)

    def inside(s):
        return (tile_first[None, :] <= s[:, None]) & (s[:, None] <= tile_last[None, :])

    hit = inside(ids) | inside(parent) | inside(grand)
    here = (step_seg[:, :1] <= ids[None, :]) & (ids[None, :] <= step_seg[:, -1:])
    active = jnp.any(here[:, :, None] & hit[None, :, :], axis=1)
    tile_range = jnp.arange(tiles, dtype=jnp.int32)
    last_row = own_row.reshape(steps, BQ)[:, -1]
    active = active & (tile_range[None, :] * BK <= last_row[:, None])
    before = tile_range[:, None] < tile_range[None, :]
    place = jnp.sum((active[:, :, None] & before[None]).astype(jnp.int32), axis=1)
    barred = (ids[None, :] != ids[:, None]) & (ids[None, :] != parent[:, None])
    barred = barred & (ids[None, :] != grand[:, None])
    tile_has = (tile_first[:, None] <= ids[None, :]) & (ids[None, :] <= tile_last[:, None])
    barred = jnp.any(barred[:, None, :] & tile_has[None, :, :], axis=2)
    barred = jnp.any(here[:, :, None] & barred[None, :, :], axis=1)
    whole = active & ~barred & ((tile_range[None, :] + 1) * BK <= last_row[:, None] - BQ + 1)
    whole_count = jnp.sum(whole.astype(jnp.int32), axis=1)
    rank = jnp.sum((whole[:, :, None] & before[None]).astype(jnp.int32), axis=1)
    place = jnp.where(whole, rank, whole_count[:, None] + place - rank)
    chosen = active[:, :, None] & (place[:, :, None] == tile_range[None, None, :])
    listed = jnp.sum(jnp.where(chosen, tile_range[None, :, None], 0), axis=1)
    counts = jnp.sum(active.astype(jnp.int32), axis=1)
    counts = [jnp.pad(v, (0, BQ // 2 - steps)) for v in (counts, whole_count)]
    meta = jnp.concatenate([block[None], *counts, listed.reshape(steps * tiles)])
    seg_row = tree_seg[None, :]

    normed1, q, kv, gains, qkv_w, q_top = project(qkv_place, tokens_in, cos, sin, qkv_pieces)
    kvs = [kv, swap(kv, 1)]
    for c in range(1, chips):
        piece = swap(kv, 2 * c)
        kvs += [piece, swap(piece, 1)]
    out_grad, *kvs = stage(out_grad, *kvs)
    grads_in = even_out(out_grad)
    att, lse = attention_forward(meta, q, q_top, kvs, info, seg_row)
    att, grads_in = stage(att, grads_in)
    og_far = swap(grads_in, 1)
    att, ff_w[0] = stage(att, ff_w[0])
    out_w = ff_w[0][None, :, 3 * FF_STEPS[0] * FF_BLOCK :]
    out_place = jnp.stack([core, 1 - core, 0, 0])
    mid, normed2, out_w = middle(tokens_in, att, gains, [out_w, swap(out_w, 1)], out_place)
    normed2_far = swap(normed2, 1)
    tokens = (normed2, normed2_far, grads_in, og_far)
    *sums, ff_dw = feed_forward(FF_STEPS[0], *tokens, ff_w[0])
    ff_dw = lax.psum_scatter(
        ff_dw, "fsdp", scatter_dimension=0, tiled=True, axis_index_groups=same_core
    )
    ff_w[1], *sums = stage(ff_w[1], *sums)
    *sums, next_dw = feed_forward(FF_STEPS[1], *tokens, ff_w[1], sums)
    next_dw = send_chips(next_dw.reshape(trees, chips, 2 * shard, next_dw.shape[1]))
    own, far = sums
    layer_out, grad_mid, da, out_dw, dgain2 = turn(
        mid, own, swap(far, 1), grads_in, gains, out_w, att
    )

    def backward(n, meta):
        return attention_backward(
            HEAD_PARTS[n], meta, q, da, att, lse, cos, sin, kvs, info, seg_row
        )

    def meet(near, far):
        got = swap(far, 1)
        return [near[0], got[0]], [add16((near[c], got[c])) for c in range(1, chips)]

    chip_x, chip_y = chip % 2, chip // 2
    out_dw = send_cores(out_dw)
    layer_out = even_out(layer_out)
    dq_a, near, far = backward(0, meta)
    near, far, dq_a, layer_out, *values = stage(near, far, dq_a, layer_out, *out_dw, *next_dw)
    out_dw, next_dw = add16(values[:2]), add16(values[2:])
    pieces_a, both = meet(near, far)
    meta, out_dw, next_dw, *both = stage(meta, out_dw, next_dw, *both)
    both = [swap(v, 2 * c + 2) for c, v in enumerate(both)]
    out_dw = halve(out_dw.reshape(trees, 2, 2, shard, D), chip_x, 2, 2)
    next_dw = trees_first(next_dw)
    dq_b, near, far = backward(1, meta)
    near, far, dq_b, *values = stage(near, far, dq_b, *both, *out_dw, *next_dw)
    pieces_a += values[: len(both)]
    values = values[len(both) :]
    out_dw, next_dw = add16(values[:2]), add16(values[2:])
    pieces_b, both = meet(near, far)
    out_dw, next_dw, *both = stage(out_dw, next_dw, *both)
    pieces_b += [swap(v, 2 * c + 2) for c, v in enumerate(both)]
    out_dw = halve(out_dw, chip_y, 1, 4)
    next_dw = trees_second(next_dw)
    dn, qkv_dw = project_back(
        tokens_in, normed1, (dq_a, dq_b), (pieces_a, pieces_b), qkv_w, dgain2, cos, sin
    )
    qkv_dw = send_cores(qkv_dw)
    dn, *values = stage(dn, *out_dw, *next_dw, *qkv_dw)
    out_dw, values = add16(values[:2]), values[2:]
    next_dw, qkv_dw = add16(values[: len(next_dw)]), add16(values[len(next_dw) :])
    qkv_dw = send_chips(qkv_dw)
    ff_dw = jnp.concatenate([ff_dw, next_dw], axis=1).reshape(2, shard, -1)
    ff_dw = halve(ff_dw, core, 0, 1)
    out_dw = trees_first(out_dw)
    input_grad = input_gradient(tokens_in, grad_mid, dn, gains)
    input_grad, *values = stage(input_grad, *ff_dw, *out_dw, *qkv_dw)
    (keep, got), values = values[:2], values[2:]
    out_dw, qkv_dw = add16(values[: len(out_dw)]), add16(values[len(out_dw) :])
    out_dw, qkv_dw = trees_second(out_dw), send_trees(qkv_dw)
    travelled = swap(input_grad[rows // 2 :].astype(BF16), span - 1)
    input_grad = jnp.concatenate([input_grad[: rows // 2], travelled.astype(F32)])
    out_dw, qkv_dw = add(out_dw), add(qkv_dw)

    groups = qkv_dw[:, :QKV].reshape(shard, KV_HEADS, GROUP_COLS)
    grad_query = groups[:, :, : GROUP * HEAD].reshape(shard, HEADS * HEAD)
    grad_key = groups[:, :, GROUP * HEAD : GROUP * HEAD + HEAD].reshape(shard, KV_HEADS * HEAD)
    grad_value = groups[:, :, GROUP * HEAD + HEAD :].reshape(shard, KV_HEADS * HEAD)

    grads = [[], [], []]
    for c in range(2):
        half = jnp.where(core == c, keep, got).astype(F32)
        first = 0
        for steps in FF_STEPS:
            for grad in grads:
                last = first + steps * FF_BLOCK
                grad.append(half[:, first:last])
                first = last
    ff_grads = [jnp.concatenate(grad, axis=1) for grad in grads]
    return (
        layer_out,
        input_grad,
        qkv_dw[:, QKV],
        grad_query,
        grad_key,
        grad_value,
        out_dw.T,
        qkv_dw[:, QKV + 1],
        ff_grads[0],
        ff_grads[1],
        ff_grads[2].T,
    )


def solution(mesh):
    rows, cols, flat = P("fsdp", None), P(None, "fsdp"), P("fsdp")
    return jax.shard_map(
        body,
        mesh=mesh,
        in_specs=(rows, rows, flat, P(), flat, rows, rows, rows, cols, flat, rows, rows, cols),
        out_specs=(rows, rows, flat, rows, rows, rows, cols, flat, rows, rows, cols),
        check_vma=False,
    )
```

```python
import functools
import math

import jax
import jax.numpy as jnp
from jax import lax
from jax.experimental import pallas as pl
from jax.experimental.pallas import tpu as pltpu
from jax.sharding import PartitionSpec as P

HEADS = 20
KV_HEADS = 5
GROUP = HEADS // KV_HEADS
HEAD = 64
TREE = 5120
D = 1280
FF = 3584
HALF = FF // 2
LANES = 128
GROUP_COLS = GROUP * HEAD + 2 * HEAD
QKV = KV_HEADS * GROUP_COLS
QKV_PAD = QKV + LANES
BQ = 160
BK = 256
STACK = GROUP * BQ
FF_BLOCK = 256
FF_STEPS = (3, 4)
HEAD_PARTS = ((0, 3), (3, 2))

EPSILON = 1e-05
ROPE_BASE = 10000.0
MASKED = -1e30
SCALE = HEAD**-0.5
SCALE2 = SCALE * math.log2(math.e)
SAFE_EXPONENT = 60.0
FAR = 1 << 20

F32 = jnp.float32
BF16 = jnp.bfloat16
ROWS_BY_ROWS = (((1,), (1,)), ((), ()))
COLS_BY_COLS = (((0,), (0,)), ((), ()))
SMALL = pl.CostEstimate(flops=10**6, bytes_accessed=10**4, transcendentals=0)
VMEM_SPACE = pl.BlockSpec(memory_space=pltpu.VMEM)
SMEM_SPACE = pl.BlockSpec(memory_space=pltpu.SMEM)
ANY_SPACE = pl.BlockSpec(memory_space=pl.ANY)


def params(mib):
    return pltpu.CompilerParams(vmem_limit_bytes=mib * 2**20)


def lane_iota(shape):
    return lax.broadcasted_iota(jnp.int32, shape, len(shape) - 1)


def dot(a, b):
    return jnp.dot(a, b, preferred_element_type=F32)


def dot_tr(a, b):
    return lax.dot_general(a, b, ROWS_BY_ROWS, preferred_element_type=F32)


def dot_cc(a, b):
    return lax.dot_general(a, b, COLS_BY_COLS, preferred_element_type=F32)


def half_turn(z, low):
    return jnp.where(low, pltpu.roll(z, LANES - 32, 1), pltpu.roll(z, 32, 1))


def assembly(place_ref, piece_refs, w, sems):
    copies = []
    for e, ref in enumerate(piece_refs):
        parts, rows, cols = ref.shape
        col = pl.multiple_of(place_ref[e] * cols, LANES)
        for part in range(parts):
            k = len(copies)
            row = pl.multiple_of(place_ref[len(piece_refs) + k] * rows, 16)
            to = w.at[pl.ds(row, rows), pl.ds(col, cols)]
            copies.append(pltpu.make_async_copy(ref.at[part], to, sems.at[k]))
    for copy in copies:
        copy.start()
    return copies


def square_sums(rows):
    shape = (LANES, LANES)
    same = (lax.broadcasted_iota(jnp.int32, shape, 0) < HEAD) == (lane_iota(shape) < HEAD)
    same = jnp.where(same, 1.0, 0.0).astype(BF16)

    def squares(z):
        sums = dot((z * z).astype(BF16), same)
        return jnp.max(sums.reshape(rows // 8, 8, LANES), axis=0)

    return squares


def project_keys_kernel(place_ref, x_ref, cos_ref, sin_ref, *refs):
    piece_refs, (n_ref, kv_ref, gain_ref, w_ref, sems) = refs[:-5], refs[-5:]
    copies = assembly(place_ref, piece_refs, w_ref, sems)
    for copy in copies:
        copy.wait()
    gains = w_ref[:, QKV:].astype(F32).T
    gain_ref[...] = gains[:8, :]
    gain1 = gains[0:1, :]
    rows = x_ref.shape[0]

    def norm(i, _):
        at = pl.ds(i * BQ, BQ)
        x = x_ref[at, :].astype(F32)
        scale = lax.rsqrt(jnp.mean(x * x, axis=1, keepdims=True) + EPSILON)
        n_ref[at, :] = (x * scale * gain1).astype(BF16)
        return 0

    lax.fori_loop(0, rows // BQ, norm, 0)
    lane = lane_iota((rows, LANES))
    low = (lane % HEAD) < HEAD // 2
    left = lane < HEAD
    squares = square_sums(rows)
    tops = jnp.zeros((8, LANES), F32)
    columns = [w_ref[:, (g + 1) * GROUP_COLS - LANES : (g + 1) * GROUP_COLS] for g in range(KV_HEADS)]
    z = dot(n_ref[...], jnp.concatenate(columns, axis=1))
    for g in range(KV_HEADS):
        zk = z[:, g * LANES : (g + 1) * LANES]
        rot = zk * cos_ref[...] + half_turn(zk, low) * sin_ref[...]
        tops = jnp.maximum(tops, squares(rot))
        kv_ref[g, :rows] = jnp.where(left, rot, zk).astype(BF16)
    top = jnp.max(jnp.where(left[:8], tops, 0.0)) * 1.02
    kv_ref[:, rows:] = jnp.full((KV_HEADS, 16, LANES), top, F32).astype(BF16)


def project_keys(place, x, cos, sin, pieces):
    rows = x.shape[0]
    count = sum(p.shape[0] for p in pieces)
    return pl.pallas_call(
        project_keys_kernel,
        out_shape=[
            jax.ShapeDtypeStruct((rows, D), BF16),
            jax.ShapeDtypeStruct((KV_HEADS, rows + 16, LANES), BF16),
            jax.ShapeDtypeStruct((8, D), F32),
            jax.ShapeDtypeStruct((D, QKV_PAD), BF16),
        ],
        in_specs=[SMEM_SPACE] + [VMEM_SPACE] * 3 + [ANY_SPACE] * len(pieces),
        out_specs=[VMEM_SPACE] * 4,
        scratch_shapes=[pltpu.SemaphoreType.DMA((count,))],
        compiler_params=params(48),
        name="project_keys",
    )(place, x, cos, sin, *pieces)


def project_queries_kernel(n_ref, w_ref, cos_ref, sin_ref, q_ref, top_ref):
    rows = n_ref.shape[0]
    lane = lane_iota((rows, LANES))
    low = (lane % HEAD) < HEAD // 2
    left = lane < HEAD
    squares = square_sums(rows)
    tops = jnp.zeros((8, LANES), F32)
    for g in range(KV_HEADS):
        z = dot(n_ref[...], w_ref[:, g * GROUP_COLS : (g + 1) * GROUP_COLS - LANES])
        for pair in range(GROUP // 2):
            zp = z[:, pair * LANES : (pair + 1) * LANES]
            rot = zp * cos_ref[...] + half_turn(zp, low) * sin_ref[...]
            rot = rot.astype(BF16).astype(F32)
            tops = jnp.maximum(tops, squares(rot))
            head = g * GROUP + 2 * pair
            q_ref[head] = jnp.where(left, rot, 0.0).astype(BF16)
            q_ref[head + 1] = jnp.where(left, pltpu.roll(rot, HEAD, 1), 0.0).astype(BF16)
    top_ref[...] = tops


def project_queries(n, w, cos, sin):
    rows = n.shape[0]
    return pl.pallas_call(
        project_queries_kernel,
        out_shape=[
            jax.ShapeDtypeStruct((HEADS, rows, LANES), BF16),
            jax.ShapeDtypeStruct((8, LANES), F32),
        ],
        compiler_params=params(48),
        cost_estimate=SMALL,
        name="project_queries",
    )(n, w, cos, sin)


def first_row(device, half, rows, span):
    device = device ^ (span - 1) if half else device
    return pl.multiple_of(device * rows + half * (rows // 2), BQ)


def gather_keys(block, kv_refs, kv, sems, heads):
    rows, span = kv_refs[0].shape[1] - 16, len(kv_refs)
    copies = []
    for e, ref in enumerate(kv_refs):
        for half in range(2):
            source = ref.at[heads, pl.ds(half * (rows // 2), rows // 2), :]
            to = kv.at[:, pl.ds(first_row(block ^ e, half, rows, span), rows // 2), :]
            copies.append(pltpu.make_async_copy(source, to, sems.at[2 * e + half]))
    return copies


def tile_pair(meta_ref, tiles, i, k):
    spots = []
    count = meta_ref[1 + i]
    for k in (k, k + 1):
        first = pl.multiple_of(meta_ref[1 + BQ + i * tiles + jnp.minimum(k, count - 1)] * BK, BK)
        spots.append((first, jnp.where(k < count, first, FAR)))
    return spots


def open_tiles(meta_ref, i):
    return meta_ref[1 + BQ // 2 + i] // 2 * 2


def mask_bias(info_ref, seg_ref, i, spots):
    info = info_ref[pl.ds(i * BQ, BQ), :]
    own, parent, grand, row = (info[:, c : c + 1] for c in range(4))
    parts = []
    for first, name in spots:
        seg = seg_ref[:, pl.ds(first, BK)]
        key_row = lane_iota((1, BK)) + name
        ok = ((seg == own) | (seg == parent) | (seg == grand)) & (key_row <= row)
        parts.append(jnp.where(ok, 0.0, MASKED))
    return jnp.concatenate(parts, axis=1)


def key_pair(kv, g, spots):
    return jnp.concatenate([kv[g, pl.ds(first, BK), :] for first, _ in spots], axis=0)


def masked(s, bias):
    return (s.reshape(GROUP, BQ, 2 * BK) * SCALE2 + bias[None]).reshape(STACK, 2 * BK)


def split_keys(kv, first, second):
    left = lane_iota((BK, LANES)) < HEAD
    one = jnp.ones((BK, LANES), BF16)

    def step(n, _):
        at = pl.ds(pl.multiple_of(n * BK, BK), BK)
        for g in range(kv.shape[0]):
            v = kv[g, at, :]
            second[g, at, :] = jnp.where(left, one, v)
            if first is not None:
                first[g, at, :] = jnp.where(left, v, one)
        return 0

    lax.fori_loop(0, kv.shape[1] // BK, step, 0)


def forward_kernel(meta_ref, q_ref, top_ref, *refs, tiles, span):
    kv_refs = refs[:span]
    info_ref, seg_ref, att_ref, lse_ref, kv, val, acc, top, k_tops, sems = refs[span:]
    rows = q_ref.shape[1]
    copies = gather_keys(meta_ref[0], kv_refs, kv, sems, pl.ds(0, KV_HEADS))
    for e, ref in enumerate(kv_refs):
        source = ref.at[0, pl.ds(rows, 16), :]
        copies.append(pltpu.make_async_copy(source, k_tops.at[e], sems.at[2 * span + e]))
    for copy in copies:
        copy.start()
    for copy in copies:
        copy.wait()
    split_keys(kv, None, val)

    def q_rows(i, g):
        at = pl.ds(pl.multiple_of(i * BQ, BQ), BQ)
        return q_ref[pl.ds(g * GROUP, GROUP), at, :].reshape(STACK, LANES)

    def fold(i, g, spots, bias, ceiling):
        s = dot_tr(q_rows(i, g), key_pair(kv, g, spots))
        s = s * SCALE2 if bias is None else masked(s, bias)
        if ceiling:
            s = s - top[g, :, 0:1]
        acc[g] += dot(jnp.exp2(s).astype(BF16), key_pair(val, g, spots))

    def finish(i, ceiling):
        at = pl.ds(pl.multiple_of(i * BQ, BQ), BQ)
        lane = lane_iota((BQ, LANES))
        logs = jnp.zeros((BQ, LANES), F32)
        for g in range(KV_HEADS):
            sums = acc[g]
            lse = jnp.log2(sums)
            if ceiling:
                lse = lse + top[g, :, 0:1]
            out = sums * pltpu.roll(1.0 / sums, HEAD, 1)
            for h in range(GROUP):
                logs = jnp.where(lane == g * GROUP + h, lse[h * BQ : (h + 1) * BQ, 0:1], logs)
            for pair in range(GROUP // 2):
                first = out[2 * pair * BQ : (2 * pair + 1) * BQ]
                second = out[(2 * pair + 1) * BQ : (2 * pair + 2) * BQ]
                both = jnp.where(lane < HEAD, pltpu.roll(first, HEAD, 1), second)
                column = (g * GROUP // 2 + pair) * LANES
                att_ref[at, column : column + LANES] = both.astype(BF16)
        lse_ref[at, :] = logs

    def run(ceiling):
        def q_loop(i, _):
            acc[...] = jnp.zeros_like(acc)
            count = meta_ref[1 + i]
            free = open_tiles(meta_ref, i)
            if ceiling:
                free = free * 0
                top[...] = jnp.full_like(top, 2 * MASKED)

                def top_loop(t, _):
                    spots = tile_pair(meta_ref, tiles, i, 2 * t)
                    bias = mask_bias(info_ref, seg_ref, i, spots)

                    def top_group(g, _):
                        s = masked(dot_tr(q_rows(i, g), key_pair(kv, g, spots)), bias)
                        top[g] = jnp.maximum(top[g], jnp.max(s, axis=1, keepdims=True))
                        return 0

                    lax.fori_loop(0, KV_HEADS, top_group, 0)
                    return 0

                lax.fori_loop(0, (count + 1) // 2, top_loop, 0)
            else:

                def open_loop(t, _):
                    spots = tile_pair(meta_ref, tiles, i, 2 * t)
                    for g in range(KV_HEADS):
                        fold(i, g, spots, None, False)
                    return 0

                lax.fori_loop(0, free // 2, open_loop, 0)

            def k_loop(t, _):
                spots = tile_pair(meta_ref, tiles, i, free + 2 * t)
                bias = mask_bias(info_ref, seg_ref, i, spots)
                if ceiling:

                    def group(g, _):
                        fold(i, g, spots, bias, True)
                        return 0

                    lax.fori_loop(0, KV_HEADS, group, 0)
                else:
                    for g in range(KV_HEADS):
                        fold(i, g, spots, bias, False)
                return 0

            lax.fori_loop(0, (count - free + 1) // 2, k_loop, 0)
            finish(i, ceiling)
            return 0

        lax.fori_loop(0, rows // BQ, q_loop, 0)

    bound = jnp.max(top_ref[...]) * jnp.max(k_tops[...].astype(F32))
    safe = bound < (SAFE_EXPONENT / SCALE2) ** 2

    @pl.when(safe)
    def _():
        run(False)

    @pl.when(jnp.logical_not(safe))
    def _():
        run(True)


def attention_forward(meta, q, top, kvs, info, seg):
    rows = q.shape[1]
    span = len(kvs)
    keys = span * rows
    tiles = keys // BK
    return pl.pallas_call(
        functools.partial(forward_kernel, tiles=tiles, span=span),
        out_shape=[
            jax.ShapeDtypeStruct((rows, D), BF16),
            jax.ShapeDtypeStruct((rows, LANES), F32),
        ],
        in_specs=[SMEM_SPACE] + [VMEM_SPACE] * 2 + [ANY_SPACE] * span + [VMEM_SPACE] * 2,
        out_specs=[VMEM_SPACE] * 2,
        scratch_shapes=[
            pltpu.VMEM((KV_HEADS, keys, LANES), BF16),
            pltpu.VMEM((KV_HEADS, keys, LANES), BF16),
            pltpu.VMEM((KV_HEADS, STACK, LANES), F32),
            pltpu.VMEM((KV_HEADS, STACK, LANES), F32),
            pltpu.VMEM((span, 16, LANES), BF16),
            pltpu.SemaphoreType.DMA((3 * span,)),
        ],
        compiler_params=params(52),
        cost_estimate=SMALL,
        name="attention_forward",
    )(meta, q, top, *kvs, info, seg)


def backward_kernel(
    meta_ref, q_ref, da_ref, att_ref, lse_ref, cos_ref, sin_ref, *refs, tiles, span, heads
):
    first_head, groups = heads
    kv_refs = refs[:span]
    info_ref, seg_ref, dq_ref, near_ref, far_ref, key, val, dkv, dq, qd, lifted, sems = refs[span:]
    rows = q_ref.shape[1]
    block = meta_ref[0]
    copies = gather_keys(block, kv_refs, key, sems, pl.ds(first_head, groups))
    for copy in copies:
        copy.start()

    def clear(n, _):
        dkv[:, pl.ds(n * BK, BK), :] = jnp.zeros((groups, BK, LANES), F32)
        return 0

    lax.fori_loop(0, key.shape[1] // BK, clear, 0)
    for copy in copies:
        copy.wait()
    split_keys(key, key, val)
    lane = lane_iota((BQ, LANES))
    left = lane < HEAD

    def lanes_of(column, first):
        out = jnp.zeros((BQ, LANES), F32)
        for k in range(3):
            top = column.astype(BF16).astype(F32)
            out = jnp.where(lane == first + k, top, out)
            column = column - top
        return out

    def q_loop(i, _):
        at = pl.ds(pl.multiple_of(i * BQ, BQ), BQ)
        dq[...] = jnp.zeros_like(dq)
        logs = lse_ref[at, :] * (-1.0 / SCALE2)
        for h in range(first_head * GROUP, (first_head + groups) * GROUP):
            g, r = h // GROUP - first_head, h % GROUP
            column = h // 2 * LANES
            da = da_ref[at, column : column + LANES].astype(F32)
            delta = da * att_ref[at, column : column + LANES].astype(F32)
            mine = left if h % 2 == 0 else jnp.logical_not(left)
            delta = jnp.sum(jnp.where(mine, delta, 0.0), axis=1, keepdims=True)
            if h % 2 == 0:
                da = pltpu.roll(da, HEAD, 1)
            q = q_ref[h, at, :]
            own = slice(r * BQ, (r + 1) * BQ)
            other = slice(STACK + r * BQ, STACK + (r + 1) * BQ)
            qd[g, own, :] = q
            qd[g, other, :] = jnp.where(left, 0.0, da).astype(BF16)
            lse = lanes_of(logs[:, h : h + 1], HEAD)
            lifted[g, own, :] = jnp.where(left, q.astype(F32), lse).astype(BF16)
            lifted[g, other, :] = jnp.where(left, lanes_of(-delta, 0), da).astype(BF16)

        def fold(g, spots, bias):
            keys = key_pair(key, g, spots)
            s = dot_tr(lifted[g, :STACK, :], keys)
            p = jnp.exp2(s * SCALE2 if bias is None else masked(s, bias))
            ds = (p * dot_tr(lifted[g, STACK:, :], key_pair(val, g, spots))).astype(BF16)
            p = p.astype(BF16)
            dq[g] += dot(ds, keys)
            moved = dot_cc(jnp.concatenate([ds, p], axis=0), qd[g])
            for n, (first, _) in enumerate(spots):
                dkv[g, pl.ds(first, BK), :] += moved[n * BK : (n + 1) * BK]

        count = meta_ref[1 + i]
        free = open_tiles(meta_ref, i)

        def open_loop(t, _):
            spots = tile_pair(meta_ref, tiles, i, 2 * t)
            for g in range(groups):
                fold(g, spots, None)
            return 0

        lax.fori_loop(0, free // 2, open_loop, 0)

        def k_loop(t, _):
            spots = tile_pair(meta_ref, tiles, i, free + 2 * t)
            bias = mask_bias(info_ref, seg_ref, i, spots)
            for g in range(groups):
                fold(g, spots, bias)
            return 0

        lax.fori_loop(0, (count - free + 1) // 2, k_loop, 0)
        cos = cos_ref[at, :]
        sin = sin_ref[at, :]
        low = (lane % HEAD) < HEAD // 2
        for g in range(groups):
            for pair in range(GROUP // 2):
                first = dq[g, 2 * pair * BQ : (2 * pair + 1) * BQ]
                second = dq[g, (2 * pair + 1) * BQ : (2 * pair + 2) * BQ]
                z = jnp.where(left, first, pltpu.roll(second, HEAD, 1)) * SCALE
                z = z * cos - half_turn(z, low) * sin
                column = (g * GROUP // 2 + pair) * LANES
                dq_ref[at, column : column + LANES] = z.astype(BF16)
        return 0

    lax.fori_loop(0, rows // BQ, q_loop, 0)
    factor = jnp.where(lane < HEAD, SCALE, 1.0)
    for e in range(span):
        target = near_ref if e % 2 == 0 else far_ref
        for half in range(2):
            first = first_row(block ^ e, half, rows, span)

            def leave(n, _):
                at = pl.ds(pl.multiple_of(half * (rows // 2) + n * BQ, BQ), BQ)
                source = pl.ds(pl.multiple_of(first + n * BQ, BQ), BQ)
                for g in range(groups):
                    target[e // 2, g, at, :] = (dkv[g, source, :] * factor).astype(BF16)
                return 0

            lax.fori_loop(0, rows // 2 // BQ, leave, 0)


def attention_backward(heads, meta, q, da, att, lse, cos, sin, kvs, info, seg):
    rows = q.shape[1]
    span = len(kvs)
    keys = span * rows
    tiles = keys // BK
    groups = heads[1]
    return pl.pallas_call(
        functools.partial(backward_kernel, tiles=tiles, span=span, heads=heads),
        out_shape=[
            jax.ShapeDtypeStruct((rows, groups * GROUP * HEAD), BF16),
            jax.ShapeDtypeStruct((span // 2, groups, rows, LANES), BF16),
            jax.ShapeDtypeStruct((span // 2, groups, rows, LANES), BF16),
        ],
        in_specs=[SMEM_SPACE] + [VMEM_SPACE] * 6 + [ANY_SPACE] * span + [VMEM_SPACE] * 2,
        out_specs=[VMEM_SPACE] * 3,
        scratch_shapes=[
            pltpu.VMEM((groups, keys, LANES), BF16),
            pltpu.VMEM((groups, keys, LANES), BF16),
            pltpu.VMEM((groups, keys, LANES), F32),
            pltpu.VMEM((groups, STACK, LANES), F32),
            pltpu.VMEM((groups, 2 * STACK, LANES), BF16),
            pltpu.VMEM((groups, 2 * STACK, LANES), BF16),
            pltpu.SemaphoreType.DMA((2 * span,)),
        ],
        compiler_params=params(56),
        cost_estimate=SMALL,
        name="attention_backward",
    )(meta, q, da, att, lse, cos, sin, *kvs, info, seg)


def middle_kernel(place_ref, x_ref, att_ref, gain_ref, *refs):
    piece_refs, (mid_ref, n_ref, w_ref, sems) = refs[:-4], refs[-4:]
    for copy in assembly(place_ref, piece_refs, w_ref, sems):
        copy.wait()
    mid_ref[...] = dot_tr(att_ref[...], w_ref[...])
    gain2 = gain_ref[1:2, :]

    def norm(i, _):
        at = pl.ds(pl.multiple_of(i * BQ, BQ), BQ)
        mid = x_ref[at, :].astype(F32) + mid_ref[at, :]
        scale = lax.rsqrt(jnp.mean(mid * mid, axis=1, keepdims=True) + EPSILON)
        mid_ref[at, :] = mid
        n_ref[at, :] = (mid * scale * gain2).astype(BF16)
        return 0

    lax.fori_loop(0, mid_ref.shape[0] // BQ, norm, 0)


def middle(x, att, gains, pieces, place):
    rows = x.shape[0]
    count = sum(p.shape[0] for p in pieces)
    return pl.pallas_call(
        middle_kernel,
        out_shape=[
            jax.ShapeDtypeStruct((rows, D), F32),
            jax.ShapeDtypeStruct((rows, D), BF16),
            jax.ShapeDtypeStruct((D, D), BF16),
        ],
        in_specs=[SMEM_SPACE] + [VMEM_SPACE] * 3 + [ANY_SPACE] * len(pieces),
        out_specs=[VMEM_SPACE] * 3,
        scratch_shapes=[pltpu.SemaphoreType.DMA((count,))],
        compiler_params=params(32),
        name="middle",
    )(place, x, att, gains, *pieces)


def feed_forward_kernel(
    n1_ref, n2_ref, og1_ref, og2_ref, wg_ref, wu_ref, wd_ref, *refs, later
):
    priors, refs = refs[: 2 * later], refs[2 * later :]
    own_ref, far_ref, dw_ref, n, og, nt, ogt, oacc, nacc, hid, dgate, dup = refs
    f = pl.program_id(0)
    part = pl.program_id(1)
    rows = n1_ref.shape[0]

    @pl.when((f == 0) & (part == 0))
    def _():
        n[:rows] = n1_ref[...]
        n[rows:] = n2_ref[...]
        og[:rows] = og1_ref[...]
        og[rows:] = og2_ref[...]
        nt[...] = n[...].T
        ogt[...] = og[...].T
        if later:
            for k, (prior, target) in enumerate(zip(priors, (own_ref, far_ref))):
                pltpu.sync_copy(prior, target)
                oacc[k * rows : (k + 1) * rows] = target[0].astype(F32)
                nacc[k * rows : (k + 1) * rows] = target[1].astype(F32)
        else:
            oacc[...] = jnp.zeros_like(oacc)
            nacc[...] = jnp.zeros_like(nacc)

    @pl.when(part == 0)
    def _():
        for k in range(2):
            at = slice(k * rows, (k + 1) * rows)
            gate = dot(n[at], wg_ref[...])
            up = dot(n[at], wu_ref[...])
            grad = dot(og[at], wd_ref[...])
            sig = jax.nn.sigmoid(gate)
            silu = gate * sig
            hid[at] = (silu * up).astype(BF16)
            dgate[at] = (grad * up * sig * (1.0 + gate * (1.0 - sig))).astype(BF16)
            dup[at] = (grad * silu).astype(BF16)
        dw_ref[...] = dot(nt[...], dgate[...]).astype(BF16)

    @pl.when(part == 1)
    def _():
        nacc[...] += dot_tr(dgate[...], wg_ref[...]) + dot_tr(dup[...], wu_ref[...])
        dw_ref[...] = dot(nt[...], dup[...]).astype(BF16)

    @pl.when(part == 2)
    def _():
        oacc[...] += dot_tr(hid[...], wd_ref[...])
        dw_ref[...] = dot(ogt[...], hid[...]).astype(BF16)

    @pl.when((f == pl.num_programs(0) - 1) & (part == 2))
    def _():
        own_ref[0] = oacc[:rows].astype(BF16)
        own_ref[1] = nacc[:rows].astype(BF16)
        far_ref[0] = oacc[rows:].astype(BF16)
        far_ref[1] = nacc[rows:].astype(BF16)


def feed_forward(steps, n_own, n_far, og_own, og_far, w, priors=()):
    rows = n_own.shape[0]
    block = FF_BLOCK
    whole = pl.BlockSpec((rows, D), lambda f, k: (0, 0), pipeline_mode=pl.Buffered(1))
    sides = pl.BlockSpec((2, rows, D), lambda f, k: (0, 0, 0))
    slab = [pl.BlockSpec((D, block), lambda f, k, m=m: (0, m * steps + f)) for m in range(3)]
    return pl.pallas_call(
        functools.partial(feed_forward_kernel, later=bool(priors)),
        grid=(steps, 3),
        in_specs=[whole] * 4 + slab + [ANY_SPACE] * len(priors),
        out_specs=[sides, sides, pl.BlockSpec((D, block), lambda f, k: (0, k * steps + f))],
        out_shape=[
            jax.ShapeDtypeStruct((2, rows, D), BF16),
            jax.ShapeDtypeStruct((2, rows, D), BF16),
            jax.ShapeDtypeStruct((D, 3 * steps * block), BF16),
        ],
        scratch_shapes=[
            pltpu.VMEM((2 * rows, D), BF16),
            pltpu.VMEM((2 * rows, D), BF16),
            pltpu.VMEM((D, 2 * rows), BF16),
            pltpu.VMEM((D, 2 * rows), BF16),
            pltpu.VMEM((2 * rows, D), F32),
            pltpu.VMEM((2 * rows, D), F32),
            pltpu.VMEM((2 * rows, block), BF16),
            pltpu.VMEM((2 * rows, block), BF16),
            pltpu.VMEM((2 * rows, block), BF16),
        ],
        compiler_params=params(62),
        cost_estimate=SMALL,
        name="feed_forward",
    )(n_own, n_far, og_own, og_far, w, w, w, *priors)


def turn_kernel(
    mid_ref, own_ref, got_ref, og_ref, gain_ref, w_ref, att_ref,
    out_ref, gm_ref, da_ref, dw_ref, dgain_ref, gmb,
):
    gain2 = gain_ref[1:2, :]

    def step(i, dgain):
        at = pl.ds(pl.multiple_of(i * BQ, BQ), BQ)
        mid = mid_ref[at, :]
        out = mid + (own_ref[0, at, :].astype(F32) + got_ref[0, at, :].astype(F32))
        out_ref[at, :] = out.astype(BF16)
        dn = own_ref[1, at, :].astype(F32) + got_ref[1, at, :].astype(F32)
        scale = lax.rsqrt(jnp.mean(mid * mid, axis=1, keepdims=True) + EPSILON)
        dgain = dgain + jnp.sum((dn * mid * scale).reshape(BQ // 8, 8, D), axis=0)
        q2 = dn * gain2
        mean = jnp.mean(q2 * mid, axis=1, keepdims=True)
        gm = og_ref[at, :].astype(F32) + scale * q2 - mid * (scale * scale * scale * mean)
        gm_ref[at, :] = gm
        gmb[at, :] = gm.astype(BF16)
        return dgain

    dgain = lax.fori_loop(0, mid_ref.shape[0] // BQ, step, jnp.zeros((8, D), F32))
    dgain_ref[...] = dgain
    da_ref[...] = dot(gmb[...], w_ref[...]).astype(BF16)
    dw_ref[...] = dot_cc(gmb[...], att_ref[...]).astype(BF16)


def turn(mid, own, got, og, gains, w, att):
    rows = mid.shape[0]
    return pl.pallas_call(
        turn_kernel,
        out_shape=[
            jax.ShapeDtypeStruct((rows, D), BF16),
            jax.ShapeDtypeStruct((rows, D), F32),
            jax.ShapeDtypeStruct((rows, D), BF16),
            jax.ShapeDtypeStruct((D, D), BF16),
            jax.ShapeDtypeStruct((8, D), F32),
        ],
        scratch_shapes=[pltpu.VMEM((rows, D), BF16)],
        compiler_params=params(56),
        name="turn",
    )(mid, own, got, og, gains, w, att)


def project_back_kernel(
    x_ref, n_ref, dqa_ref, dqb_ref, ka_refs, kb_refs, w_ref, dgain_ref,
    cos_ref, sin_ref, dn_ref, dw_ref, dz,
):
    rows = x_ref.shape[0]
    lane = lane_iota((BQ, LANES))
    low = (lane % HEAD) < HEAD // 2
    left = lane < HEAD
    first = dqa_ref.shape[1] // (GROUP * HEAD)

    def turn_back(i, _):
        at = pl.ds(pl.multiple_of(i * BQ, BQ), BQ)
        cos = cos_ref[at, :]
        sin = sin_ref[at, :]
        for g in range(KV_HEADS):
            refs, k, dq_ref = (ka_refs, g, dqa_ref) if g < first else (kb_refs, g - first, dqb_ref)
            z = sum(ref[k, at, :].astype(F32) for ref in refs)
            rot = z * cos - half_turn(z, low) * sin
            base = g * GROUP_COLS
            span = GROUP * HEAD
            dz[at, base : base + span] = dq_ref[at, k * span : (k + 1) * span]
            dz[at, base + span : base + span + LANES] = jnp.where(left, rot, z).astype(BF16)
        return 0

    lax.fori_loop(0, rows // BQ, turn_back, 0)
    dw_ref[:, :QKV] = dot_cc(n_ref[...], dz[...]).astype(BF16)
    dn_ref[...] = dot_tr(dz[...], w_ref[:, :QKV])

    def step(i, dgain):
        at = pl.ds(pl.multiple_of(i * BQ, BQ), BQ)
        x = x_ref[at, :].astype(F32)
        scale = lax.rsqrt(jnp.mean(x * x, axis=1, keepdims=True) + EPSILON)
        return dgain + jnp.sum((dn_ref[at, :] * x * scale).reshape(BQ // 8, 8, D), axis=0)

    dgain1 = lax.fori_loop(0, rows // BQ, step, jnp.zeros((8, D), F32))
    dgain1 = jnp.sum(dgain1, axis=0, keepdims=True)
    dgain2 = jnp.sum(dgain_ref[...], axis=0, keepdims=True)
    row = lax.broadcasted_iota(jnp.int32, (LANES, D), 0)
    both = jnp.where(row == 0, dgain1, jnp.where(row == 1, dgain2, 0.0))
    dw_ref[:, QKV:] = both.T.astype(BF16)


def project_back(x, n, dqs, pieces, w, dgain, cos, sin):
    rows = x.shape[0]

    def kernel(x_ref, n_ref, dqa_ref, dqb_ref, *refs):
        count = len(pieces[0])
        return project_back_kernel(
            x_ref, n_ref, dqa_ref, dqb_ref, refs[:count], refs[count : 2 * count],
            *refs[2 * count :],
        )

    return pl.pallas_call(
        kernel,
        out_shape=[
            jax.ShapeDtypeStruct((rows, D), F32),
            jax.ShapeDtypeStruct((D, QKV_PAD), BF16),
        ],
        scratch_shapes=[pltpu.VMEM((rows, QKV), BF16)],
        compiler_params=params(48),
        name="project_back",
    )(x, n, *dqs, *pieces[0], *pieces[1], w, dgain, cos, sin)


def input_grad_kernel(x_ref, gm_ref, dn_ref, gain_ref, in_ref):
    x = x_ref[...].astype(F32)
    scale = lax.rsqrt(jnp.mean(x * x, axis=1, keepdims=True) + EPSILON)
    q1 = dn_ref[...] * gain_ref[0:1, :]
    mean = jnp.mean(q1 * x, axis=1, keepdims=True)
    in_ref[...] = gm_ref[...] + scale * q1 - x * (scale * scale * scale * mean)


def input_gradient(x, gm, dn, gains):
    rows = x.shape[0]
    block = pl.BlockSpec((BQ, D), lambda i: (i, 0))
    return pl.pallas_call(
        input_grad_kernel,
        grid=(rows // BQ,),
        in_specs=[block] * 3 + [pl.BlockSpec((8, D), lambda i: (0, 0))],
        out_specs=block,
        out_shape=jax.ShapeDtypeStruct((rows, D), F32),
        compiler_params=params(32),
        cost_estimate=SMALL,
        name="input_gradient",
    )(x, gm, dn, gains)


def body(
    layer_in, out_grad, segment_ids, segment_parents, norm_gain1, w_query, w_key, w_value, w_output,
    norm_gain2, w_gate, w_up, w_down,
):
    size = lax.axis_size("fsdp")
    rows = layer_in.shape[0]
    span = TREE // rows
    shard = D // size
    me = lax.axis_index("fsdp")
    block = me % span
    tree = me // span
    core = me % 2

    def swap(v, bit):
        return lax.ppermute(v, "fsdp", [(i, i ^ bit) for i in range(size)])

    same_core = [list(range(c, size, 2)) for c in range(2)]

    trees = size // span
    chips = span // 2
    chip = block // 2

    def stage(*values):
        return lax.optimization_barrier(values)

    def half_columns(*halves):
        keep = jnp.where(core == 0, halves[0], halves[1])
        got = swap(jnp.where(core == 0, halves[1], halves[0]), 1)
        return jnp.where(
            core == 0, jnp.concatenate([keep, got], axis=0), jnp.concatenate([got, keep], axis=0)
        )

    def part(v, index, axis):
        return lax.dynamic_index_in_dim(v, index, axis, keepdims=False)

    def send_cores(grad):
        grad = grad.reshape(trees, chips, 2, shard, grad.shape[1])
        return part(grad, core, 2), swap(part(grad, 1 - core, 2), 1)

    def send_chips(total):
        return part(total, chip, 1), *(swap(part(total, chip ^ c, 1), 2 * c) for c in range(1, chips))

    def send_trees(total):
        if trees > 4:
            across = [list(range(k, size, span)) for k in range(span)]
            total = lax.psum_scatter(total, "fsdp", axis_index_groups=across)
            return (total.reshape(total.shape[-2:]),)
        return part(total, tree, 0), *(
            swap(part(total, tree ^ t, 0), span * t) for t in range(1, trees)
        )

    def halve(v, bit, axis, distance):
        return part(v, bit, axis), swap(part(v, 1 - bit, axis), distance)

    def trees_first(v):
        if trees != 4:
            return (v,)
        return halve(v.reshape(2, 2, *v.shape[1:]), tree // 2, 0, 2 * span)

    def trees_second(v):
        return halve(v, tree % 2, 0, span) if trees == 4 else send_trees(v)

    def add(terms):
        return sum((t.astype(F32) for t in terms[1:]), terms[0].astype(F32))

    def add16(terms):
        return add(terms).astype(BF16)

    def even_out(v):
        return jnp.concatenate([v[: rows // 2], swap(v[rows // 2 :], span - 1).astype(v.dtype)])

    turned = w_output.T
    grouped = [w_query.reshape(shard, KV_HEADS, GROUP * HEAD)]
    grouped += [w.reshape(shard, KV_HEADS, HEAD) for w in (w_key, w_value)]
    grouped = jnp.concatenate(grouped, axis=2).reshape(shard, QKV)
    gain_pair = jnp.stack([norm_gain1, norm_gain2], axis=1)
    gain_pair = jnp.pad(gain_pair, ((0, 0), (0, LANES - 2)))
    grouped = jnp.concatenate([grouped, gain_pair], axis=1)

    def columns(c):
        parts = [grouped[:, c * QKV_PAD // 2 : (c + 1) * QKV_PAD // 2]]
        first = c * HALF
        for k, count in enumerate(FF_STEPS):
            last = first + count * FF_BLOCK
            parts += [w[:, first:last] for w in (w_gate, w_up, down)]
            if k == 0:
                parts += [turned[:, c * D // 2 : (c + 1) * D // 2]]
            first = last
        return jnp.concatenate(parts, axis=1)

    down = w_down.T
    chip_rows = half_columns(columns(0), columns(1))
    first, ff_w = QKV_PAD // 2, []
    for k, count in enumerate(FF_STEPS):
        last = first + 3 * count * FF_BLOCK + (D // 2 if k == 0 else 0)
        ff_w += [
            lax.all_gather(
                chip_rows[:, first:last], "fsdp", tiled=True, axis_index_groups=same_core
            )
        ]
        first = last
    qkv_rows = chip_rows[:, : QKV_PAD // 2]
    if trees > 4:
        qkv_rows = lax.all_gather(qkv_rows, "fsdp", tiled=True, axis_index_groups=same_core)[None]
        qkv_pieces, order = [qkv_rows], jnp.zeros((1,), jnp.int32)
    else:
        qkv_rows = jnp.stack([qkv_rows] + [swap(qkv_rows, span * t) for t in range(1, trees)])
        qkv_pieces = [qkv_rows] + [swap(qkv_rows, 2 * c) for c in range(1, chips)]
        order = [(tree ^ t) * chips + (chip ^ c) for c in range(chips) for t in range(trees)]
        order = jnp.stack(order)
    qkv_place = jnp.stack([core] * len(qkv_pieces) + [1 - core] * len(qkv_pieces))
    qkv_place = jnp.concatenate([qkv_place, order, order])
    qkv_pieces = qkv_pieces + [swap(p, 1) for p in qkv_pieces]

    tree_seg = segment_ids
    bit = 1
    while bit < span:
        other = swap(tree_seg, bit)
        first = (me & bit) == 0
        tree_seg = jnp.concatenate(
            [jnp.where(first, tree_seg, other), jnp.where(first, other, tree_seg)], axis=0
        )
        bit *= 2
    layer_in, tree_seg = stage(layer_in, tree_seg)
    tokens_in = even_out(layer_in)
    seg_count = segment_parents.shape[0] * span // size
    seg_base = tree * seg_count
    tree_seg = tree_seg - seg_base
    starts = [first_row(block, half, rows, span) for half in range(2)]
    own_row = jnp.concatenate([n + jnp.arange(rows // 2, dtype=jnp.int32) for n in starts])
    own_seg = jnp.concatenate(
        [lax.dynamic_slice_in_dim(tree_seg, n, rows // 2) for n in starts]
    )
    ids = jnp.arange(seg_count, dtype=jnp.int32)
    parent = lax.dynamic_slice_in_dim(segment_parents, seg_base, seg_count) - seg_base

    def look(index, table):
        return jnp.sum(jnp.where(index[:, None] == ids[None, :], table[None, :], 0), axis=1)

    grand = look(parent, parent)
    lengths = jnp.sum((tree_seg[None, :] == ids[:, None]).astype(jnp.int32), axis=1)
    starts = jnp.sum(jnp.where(ids[None, :] < ids[:, None], lengths[None, :], 0), axis=1)
    depth = jnp.where(parent != ids, look(parent, lengths), 0)
    depth = depth + jnp.where(grand != parent, look(grand, lengths), 0)
    positions = (look(own_seg, depth - starts) + own_row).astype(F32)
    lane = jnp.arange(LANES, dtype=jnp.int32)
    inverse = jnp.exp((lane % 32).astype(F32) * (-2.0 * math.log(ROPE_BASE) / HEAD))
    angles = positions[:, None] * inverse[None, :]
    cos = jnp.cos(angles)
    sin = jnp.sin(angles) * jnp.where(lane % HEAD < HEAD // 2, -1.0, 1.0)[None, :]
    info = [own_seg, look(own_seg, parent), look(own_seg, grand), own_row]
    info = sum(jnp.where(lane[None, :] == c, v[:, None], 0) for c, v in enumerate(info))
    tiles = TREE // BK
    steps = rows // BQ
    tile_seg = tree_seg.reshape(tiles, BK)
    tile_first, tile_last = tile_seg[:, 0], tile_seg[:, -1]
    step_seg = own_seg.reshape(steps, BQ)

    def inside(s):
        return (tile_first[None, :] <= s[:, None]) & (s[:, None] <= tile_last[None, :])

    hit = inside(ids) | inside(parent) | inside(grand)
    here = (step_seg[:, :1] <= ids[None, :]) & (ids[None, :] <= step_seg[:, -1:])
    active = jnp.any(here[:, :, None] & hit[None, :, :], axis=1)
    tile_range = jnp.arange(tiles, dtype=jnp.int32)
    last_row = own_row.reshape(steps, BQ)[:, -1]
    active = active & (tile_range[None, :] * BK <= last_row[:, None])
    before = tile_range[:, None] < tile_range[None, :]
    place = jnp.sum((active[:, :, None] & before[None]).astype(jnp.int32), axis=1)
    barred = (ids[None, :] != ids[:, None]) & (ids[None, :] != parent[:, None])
    barred = barred & (ids[None, :] != grand[:, None])
    tile_has = (tile_first[:, None] <= ids[None, :]) & (ids[None, :] <= tile_last[:, None])
    barred = jnp.any(barred[:, None, :] & tile_has[None, :, :], axis=2)
    barred = jnp.any(here[:, :, None] & barred[None, :, :], axis=1)
    whole = active & ~barred & ((tile_range[None, :] + 1) * BK <= last_row[:, None] - BQ + 1)
    whole_count = jnp.sum(whole.astype(jnp.int32), axis=1)
    rank = jnp.sum((whole[:, :, None] & before[None]).astype(jnp.int32), axis=1)
    place = jnp.where(whole, rank, whole_count[:, None] + place - rank)
    chosen = active[:, :, None] & (place[:, :, None] == tile_range[None, None, :])
    listed = jnp.sum(jnp.where(chosen, tile_range[None, :, None], 0), axis=1)
    counts = jnp.sum(active.astype(jnp.int32), axis=1)
    counts = [jnp.pad(v, (0, BQ // 2 - steps)) for v in (counts, whole_count)]
    meta = jnp.concatenate([block[None], *counts, listed.reshape(steps * tiles)])
    seg_row = tree_seg[None, :]

    normed1, kv, gains, qkv_w = project_keys(qkv_place, tokens_in, cos, sin, qkv_pieces)
    kv_near = swap(kv, 1)
    kv_far = [swap(kv, 2 * c) for c in range(1, chips)]
    q, q_top = project_queries(normed1, qkv_w, cos, sin)
    q, kv_near, *kv_far = stage(q, kv_near, *kv_far)
    kvs = [kv, kv_near]
    for piece in kv_far:
        kvs += [piece, swap(piece, 1)]
    out_grad, q, *kvs = stage(out_grad, q, *kvs)
    grads_in = even_out(out_grad)
    att, lse = attention_forward(meta, q, q_top, kvs, info, seg_row)
    att, grads_in = stage(att, grads_in)
    og_far = swap(grads_in, 1)
    att, ff_w[0] = stage(att, ff_w[0])
    out_w = ff_w[0][None, :, 3 * FF_STEPS[0] * FF_BLOCK :]
    out_place = jnp.stack([core, 1 - core, 0, 0])
    mid, normed2, out_w = middle(tokens_in, att, gains, [out_w, swap(out_w, 1)], out_place)
    normed2_far = swap(normed2, 1)
    tokens = (normed2, normed2_far, grads_in, og_far)
    *sums, next_dw = feed_forward(FF_STEPS[0], *tokens, ff_w[0])
    next_dw = send_chips(next_dw.reshape(trees, chips, 2 * shard, next_dw.shape[1]))
    ff_w[1], *sums = stage(ff_w[1], *sums)
    *sums, ff_dw = feed_forward(FF_STEPS[1], *tokens, ff_w[1], sums)
    ff_dw = lax.psum_scatter(
        ff_dw, "fsdp", scatter_dimension=0, tiled=True, axis_index_groups=same_core
    )
    own, far = sums
    layer_out, grad_mid, da, out_dw, dgain2 = turn(
        mid, own, swap(far, 1), grads_in, gains, out_w, att
    )

    def backward(n, meta):
        return attention_backward(
            HEAD_PARTS[n], meta, q, da, att, lse, cos, sin, kvs, info, seg_row
        )

    def meet(near, far):
        got = swap(far, 1)
        return [near[0], got[0]], [add16((near[c], got[c])) for c in range(1, chips)]

    chip_x, chip_y = chip % 2, chip // 2
    out_dw = send_cores(out_dw)
    layer_out = even_out(layer_out)
    dq_a, near, far = backward(0, meta)
    near, far, dq_a, layer_out, *values = stage(near, far, dq_a, layer_out, *out_dw, *next_dw)
    out_dw, next_dw = add16(values[:2]), add16(values[2:])
    pieces_a, both = meet(near, far)
    meta, out_dw, next_dw, *both = stage(meta, out_dw, next_dw, *both)
    both = [swap(v, 2 * c + 2) for c, v in enumerate(both)]
    out_dw = halve(out_dw.reshape(trees, 2, 2, shard, D), chip_x, 2, 2)
    next_dw = trees_first(next_dw)
    dq_b, near, far = backward(1, meta)
    near, far, dq_b, *values = stage(near, far, dq_b, *both, *out_dw, *next_dw)
    pieces_a += values[: len(both)]
    values = values[len(both) :]
    out_dw, next_dw = add16(values[:2]), add16(values[2:])
    pieces_b, both = meet(near, far)
    out_dw, next_dw, *both = stage(out_dw, next_dw, *both)
    pieces_b += [swap(v, 2 * c + 2) for c, v in enumerate(both)]
    out_dw = halve(out_dw, chip_y, 1, 4)
    next_dw = trees_second(next_dw)
    dn, qkv_dw = project_back(
        tokens_in, normed1, (dq_a, dq_b), (pieces_a, pieces_b), qkv_w, dgain2, cos, sin
    )
    qkv_dw = send_cores(qkv_dw)
    dn, *values = stage(dn, *out_dw, *next_dw, *qkv_dw)
    out_dw, values = add16(values[:2]), values[2:]
    next_dw, qkv_dw = add16(values[: len(next_dw)]), add16(values[len(next_dw) :])
    qkv_dw = send_chips(qkv_dw)
    ff_dw = jnp.concatenate([next_dw, ff_dw], axis=1).reshape(2, shard, -1)
    ff_dw = halve(ff_dw, core, 0, 1)
    out_dw = trees_first(out_dw)
    input_grad = input_gradient(tokens_in, grad_mid, dn, gains)
    input_grad, *values = stage(input_grad, *ff_dw, *out_dw, *qkv_dw)
    (keep, got), values = values[:2], values[2:]
    out_dw, qkv_dw = add16(values[: len(out_dw)]), add16(values[len(out_dw) :])
    out_dw, qkv_dw = trees_second(out_dw), send_trees(qkv_dw)
    travelled = swap(input_grad[rows // 2 :].astype(BF16), span - 1)
    input_grad = jnp.concatenate([input_grad[: rows // 2], travelled.astype(F32)])
    out_dw, qkv_dw = add(out_dw), add(qkv_dw)

    groups = qkv_dw[:, :QKV].reshape(shard, KV_HEADS, GROUP_COLS)
    grad_query = groups[:, :, : GROUP * HEAD].reshape(shard, HEADS * HEAD)
    grad_key = groups[:, :, GROUP * HEAD : GROUP * HEAD + HEAD].reshape(shard, KV_HEADS * HEAD)
    grad_value = groups[:, :, GROUP * HEAD + HEAD :].reshape(shard, KV_HEADS * HEAD)

    grads = [[], [], []]
    for c in range(2):
        half = jnp.where(core == c, keep, got).astype(F32)
        first = 0
        for steps in FF_STEPS:
            for grad in grads:
                last = first + steps * FF_BLOCK
                grad.append(half[:, first:last])
                first = last
    ff_grads = [jnp.concatenate(grad, axis=1) for grad in grads]
    return (
        layer_out,
        input_grad,
        qkv_dw[:, QKV],
        grad_query,
        grad_key,
        grad_value,
        out_dw.T,
        qkv_dw[:, QKV + 1],
        ff_grads[0],
        ff_grads[1],
        ff_grads[2].T,
    )


def solution(mesh):
    rows, cols, flat = P("fsdp", None), P(None, "fsdp"), P("fsdp")
    return jax.shard_map(
        body,
        mesh=mesh,
        in_specs=(rows, rows, flat, P(), flat, rows, rows, rows, cols, flat, rows, rows, cols),
        out_specs=(rows, rows, flat, rows, rows, rows, cols, flat, rows, rows, cols),
        check_vma=False,
    )
```

```python
import functools
import math

import jax
import jax.numpy as jnp
from jax import lax
from jax.experimental import pallas as pl
from jax.experimental.pallas import tpu as pltpu
from jax.sharding import PartitionSpec as P

HEADS = 20
KV_HEADS = 5
GROUP = HEADS // KV_HEADS
HEAD = 64
TREE = 5120
D = 1280
FF = 3584
HALF = FF // 2
LANES = 128
GROUP_COLS = GROUP * HEAD + 2 * HEAD
QKV = KV_HEADS * GROUP_COLS
QKV_PAD = QKV + LANES
BQ = 160
BK = 256
STACK = GROUP * BQ
FF_BLOCK = 256
FF_STEPS = (3, 4)
HEAD_PARTS = ((0, 3), (3, 2))

EPSILON = 1e-05
ROPE_BASE = 10000.0
MASKED = -1e30
SCALE = HEAD**-0.5
SCALE2 = SCALE * math.log2(math.e)
SAFE_EXPONENT = 60.0
FAR = 1 << 20

F32 = jnp.float32
BF16 = jnp.bfloat16
ROWS_BY_ROWS = (((1,), (1,)), ((), ()))
COLS_BY_COLS = (((0,), (0,)), ((), ()))
SMALL = pl.CostEstimate(flops=10**6, bytes_accessed=10**4, transcendentals=0)
VMEM_SPACE = pl.BlockSpec(memory_space=pltpu.VMEM)
SMEM_SPACE = pl.BlockSpec(memory_space=pltpu.SMEM)
ANY_SPACE = pl.BlockSpec(memory_space=pl.ANY)


def params(mib):
    return pltpu.CompilerParams(vmem_limit_bytes=mib * 2**20)


def lane_iota(shape):
    return lax.broadcasted_iota(jnp.int32, shape, len(shape) - 1)


def dot(a, b):
    return jnp.dot(a, b, preferred_element_type=F32)


def dot_tr(a, b):
    return lax.dot_general(a, b, ROWS_BY_ROWS, preferred_element_type=F32)


def dot_cc(a, b):
    return lax.dot_general(a, b, COLS_BY_COLS, preferred_element_type=F32)


def half_turn(z, low):
    return jnp.where(low, pltpu.roll(z, LANES - 32, 1), pltpu.roll(z, 32, 1))


def assembly(place_ref, piece_refs, w, sems):
    copies = []
    for e, ref in enumerate(piece_refs):
        parts, rows, cols = ref.shape
        col = pl.multiple_of(place_ref[e] * cols, LANES)
        for part in range(parts):
            k = len(copies)
            row = pl.multiple_of(place_ref[len(piece_refs) + k] * rows, 16)
            to = w.at[pl.ds(row, rows), pl.ds(col, cols)]
            copies.append(pltpu.make_async_copy(ref.at[part], to, sems.at[k]))
    for copy in copies:
        copy.start()
    return copies


def square_sums(rows):
    shape = (LANES, LANES)
    same = (lax.broadcasted_iota(jnp.int32, shape, 0) < HEAD) == (lane_iota(shape) < HEAD)
    same = jnp.where(same, 1.0, 0.0).astype(BF16)

    def squares(z):
        sums = dot((z * z).astype(BF16), same)
        return jnp.max(sums.reshape(rows // 8, 8, LANES), axis=0)

    return squares


def project_keys_kernel(place_ref, x_ref, cos_ref, sin_ref, *refs):
    piece_refs, (n_ref, kv_ref, gain_ref, w_ref, sems) = refs[:-5], refs[-5:]
    copies = assembly(place_ref, piece_refs, w_ref, sems)
    for copy in copies:
        copy.wait()
    gains = w_ref[:, QKV:].astype(F32).T
    gain_ref[...] = gains[:8, :]
    gain1 = gains[0:1, :]
    rows = x_ref.shape[0]

    def norm(i, _):
        at = pl.ds(i * BQ, BQ)
        x = x_ref[at, :].astype(F32)
        scale = lax.rsqrt(jnp.mean(x * x, axis=1, keepdims=True) + EPSILON)
        n_ref[at, :] = (x * scale * gain1).astype(BF16)
        return 0

    lax.fori_loop(0, rows // BQ, norm, 0)
    lane = lane_iota((rows, LANES))
    low = (lane % HEAD) < HEAD // 2
    left = lane < HEAD
    squares = square_sums(rows)
    tops = jnp.zeros((8, LANES), F32)
    columns = [w_ref[:, (g + 1) * GROUP_COLS - LANES : (g + 1) * GROUP_COLS] for g in range(KV_HEADS)]
    z = dot(n_ref[...], jnp.concatenate(columns, axis=1))
    for g in range(KV_HEADS):
        zk = z[:, g * LANES : (g + 1) * LANES]
        rot = zk * cos_ref[...] + half_turn(zk, low) * sin_ref[...]
        tops = jnp.maximum(tops, squares(rot))
        kv_ref[g, :rows] = jnp.where(left, rot, zk).astype(BF16)
    top = jnp.max(jnp.where(left[:8], tops, 0.0)) * 1.02
    kv_ref[:, rows:] = jnp.full((KV_HEADS, 16, LANES), top, F32).astype(BF16)


def project_keys(place, x, cos, sin, pieces):
    rows = x.shape[0]
    count = sum(p.shape[0] for p in pieces)
    return pl.pallas_call(
        project_keys_kernel,
        out_shape=[
            jax.ShapeDtypeStruct((rows, D), BF16),
            jax.ShapeDtypeStruct((KV_HEADS, rows + 16, LANES), BF16),
            jax.ShapeDtypeStruct((8, D), F32),
            jax.ShapeDtypeStruct((D, QKV_PAD), BF16),
        ],
        in_specs=[SMEM_SPACE] + [VMEM_SPACE] * 3 + [ANY_SPACE] * len(pieces),
        out_specs=[VMEM_SPACE] * 4,
        scratch_shapes=[pltpu.SemaphoreType.DMA((count,))],
        compiler_params=params(48),
        name="project_keys",
    )(place, x, cos, sin, *pieces)


def project_queries_kernel(n_ref, w_ref, cos_ref, sin_ref, q_ref, top_ref):
    rows = n_ref.shape[0]
    lane = lane_iota((rows, LANES))
    low = (lane % HEAD) < HEAD // 2
    left = lane < HEAD
    squares = square_sums(rows)
    tops = jnp.zeros((8, LANES), F32)
    for g in range(KV_HEADS):
        z = dot(n_ref[...], w_ref[:, g * GROUP_COLS : (g + 1) * GROUP_COLS - LANES])
        for pair in range(GROUP // 2):
            zp = z[:, pair * LANES : (pair + 1) * LANES]
            rot = zp * cos_ref[...] + half_turn(zp, low) * sin_ref[...]
            rot = rot.astype(BF16).astype(F32)
            tops = jnp.maximum(tops, squares(rot))
            head = g * GROUP + 2 * pair
            q_ref[head] = jnp.where(left, rot, 0.0).astype(BF16)
            q_ref[head + 1] = jnp.where(left, pltpu.roll(rot, HEAD, 1), 0.0).astype(BF16)
    top_ref[...] = tops


def project_queries(n, w, cos, sin):
    rows = n.shape[0]
    return pl.pallas_call(
        project_queries_kernel,
        out_shape=[
            jax.ShapeDtypeStruct((HEADS, rows, LANES), BF16),
            jax.ShapeDtypeStruct((8, LANES), F32),
        ],
        compiler_params=params(48),
        cost_estimate=SMALL,
        name="project_queries",
    )(n, w, cos, sin)


def first_row(device, half, rows, span):
    device = device ^ (span - 1) if half else device
    return pl.multiple_of(device * rows + half * (rows // 2), BQ)


def gather_keys(block, kv_refs, kv, sems, heads):
    rows, span = kv_refs[0].shape[1] - 16, len(kv_refs)
    copies = []
    for e, ref in enumerate(kv_refs):
        for half in range(2):
            source = ref.at[heads, pl.ds(half * (rows // 2), rows // 2), :]
            to = kv.at[:, pl.ds(first_row(block ^ e, half, rows, span), rows // 2), :]
            copies.append(pltpu.make_async_copy(source, to, sems.at[2 * e + half]))
    return copies


def tile_pair(meta_ref, tiles, i, k):
    spots = []
    count = meta_ref[1 + i]
    for k in (k, k + 1):
        first = pl.multiple_of(meta_ref[1 + BQ + i * tiles + jnp.minimum(k, count - 1)] * BK, BK)
        spots.append((first, jnp.where(k < count, first, FAR)))
    return spots


def open_tiles(meta_ref, i):
    return meta_ref[1 + BQ // 2 + i] // 2 * 2


def mask_bias(info_ref, seg_ref, i, spots):
    info = info_ref[pl.ds(i * BQ, BQ), :]
    own, parent, grand, row = (info[:, c : c + 1] for c in range(4))
    parts = []
    for first, name in spots:
        seg = seg_ref[:, pl.ds(first, BK)]
        key_row = lane_iota((1, BK)) + name
        ok = ((seg == own) | (seg == parent) | (seg == grand)) & (key_row <= row)
        parts.append(jnp.where(ok, 0.0, MASKED))
    return jnp.concatenate(parts, axis=1)


def key_pair(kv, g, spots):
    return jnp.concatenate([kv[g, pl.ds(first, BK), :] for first, _ in spots], axis=0)


def masked(s, bias):
    return (s.reshape(GROUP, BQ, 2 * BK) * SCALE2 + bias[None]).reshape(STACK, 2 * BK)


def split_keys(kv, first, second):
    left = lane_iota((BK, LANES)) < HEAD
    one = jnp.ones((BK, LANES), BF16)

    def step(n, _):
        at = pl.ds(pl.multiple_of(n * BK, BK), BK)
        for g in range(kv.shape[0]):
            v = kv[g, at, :]
            second[g, at, :] = jnp.where(left, one, v)
            if first is not None:
                first[g, at, :] = jnp.where(left, v, one)
        return 0

    lax.fori_loop(0, kv.shape[1] // BK, step, 0)


def forward_kernel(meta_ref, q_ref, top_ref, *refs, tiles, span):
    kv_refs = refs[:span]
    info_ref, seg_ref, att_ref, lse_ref, kv, val, acc, top, k_tops, sems = refs[span:]
    rows = q_ref.shape[1]
    copies = gather_keys(meta_ref[0], kv_refs, kv, sems, pl.ds(0, KV_HEADS))
    for e, ref in enumerate(kv_refs):
        source = ref.at[0, pl.ds(rows, 16), :]
        copies.append(pltpu.make_async_copy(source, k_tops.at[e], sems.at[2 * span + e]))
    for copy in copies:
        copy.start()
    for copy in copies:
        copy.wait()
    split_keys(kv, None, val)

    def q_rows(i, g):
        at = pl.ds(pl.multiple_of(i * BQ, BQ), BQ)
        return q_ref[pl.ds(g * GROUP, GROUP), at, :].reshape(STACK, LANES)

    def fold(i, g, spots, bias, ceiling):
        s = dot_tr(q_rows(i, g), key_pair(kv, g, spots))
        s = s * SCALE2 if bias is None else masked(s, bias)
        if ceiling:
            s = s - top[g, :, 0:1]
        acc[g] += dot(jnp.exp2(s).astype(BF16), key_pair(val, g, spots))

    def finish(i, ceiling):
        at = pl.ds(pl.multiple_of(i * BQ, BQ), BQ)
        lane = lane_iota((BQ, LANES))
        logs = jnp.zeros((BQ, LANES), F32)
        for g in range(KV_HEADS):
            sums = acc[g]
            lse = jnp.log2(sums)
            if ceiling:
                lse = lse + top[g, :, 0:1]
            out = sums * pltpu.roll(1.0 / sums, HEAD, 1)
            for h in range(GROUP):
                logs = jnp.where(lane == g * GROUP + h, lse[h * BQ : (h + 1) * BQ, 0:1], logs)
            for pair in range(GROUP // 2):
                first = out[2 * pair * BQ : (2 * pair + 1) * BQ]
                second = out[(2 * pair + 1) * BQ : (2 * pair + 2) * BQ]
                both = jnp.where(lane < HEAD, pltpu.roll(first, HEAD, 1), second)
                column = (g * GROUP // 2 + pair) * LANES
                att_ref[at, column : column + LANES] = both.astype(BF16)
        lse_ref[at, :] = logs

    def run(ceiling):
        def q_loop(i, _):
            acc[...] = jnp.zeros_like(acc)
            count = meta_ref[1 + i]
            free = open_tiles(meta_ref, i)
            if ceiling:
                free = free * 0
                top[...] = jnp.full_like(top, 2 * MASKED)

                def top_loop(t, _):
                    spots = tile_pair(meta_ref, tiles, i, 2 * t)
                    bias = mask_bias(info_ref, seg_ref, i, spots)

                    def top_group(g, _):
                        s = masked(dot_tr(q_rows(i, g), key_pair(kv, g, spots)), bias)
                        top[g] = jnp.maximum(top[g], jnp.max(s, axis=1, keepdims=True))
                        return 0

                    lax.fori_loop(0, KV_HEADS, top_group, 0)
                    return 0

                lax.fori_loop(0, (count + 1) // 2, top_loop, 0)
            else:

                def open_loop(t, _):
                    spots = tile_pair(meta_ref, tiles, i, 2 * t)
                    for g in range(KV_HEADS):
                        fold(i, g, spots, None, False)
                    return 0

                lax.fori_loop(0, free // 2, open_loop, 0)

            def k_loop(t, _):
                spots = tile_pair(meta_ref, tiles, i, free + 2 * t)
                bias = mask_bias(info_ref, seg_ref, i, spots)
                if ceiling:

                    def group(g, _):
                        fold(i, g, spots, bias, True)
                        return 0

                    lax.fori_loop(0, KV_HEADS, group, 0)
                else:
                    for g in range(KV_HEADS):
                        fold(i, g, spots, bias, False)
                return 0

            lax.fori_loop(0, (count - free + 1) // 2, k_loop, 0)
            finish(i, ceiling)
            return 0

        lax.fori_loop(0, rows // BQ, q_loop, 0)

    bound = jnp.max(top_ref[...]) * jnp.max(k_tops[...].astype(F32))
    safe = bound < (SAFE_EXPONENT / SCALE2) ** 2

    @pl.when(safe)
    def _():
        run(False)

    @pl.when(jnp.logical_not(safe))
    def _():
        run(True)


def attention_forward(meta, q, top, kvs, info, seg):
    rows = q.shape[1]
    span = len(kvs)
    keys = span * rows
    tiles = keys // BK
    return pl.pallas_call(
        functools.partial(forward_kernel, tiles=tiles, span=span),
        out_shape=[
            jax.ShapeDtypeStruct((rows, D), BF16),
            jax.ShapeDtypeStruct((rows, LANES), F32),
        ],
        in_specs=[SMEM_SPACE] + [VMEM_SPACE] * 2 + [ANY_SPACE] * span + [VMEM_SPACE] * 2,
        out_specs=[VMEM_SPACE] * 2,
        scratch_shapes=[
            pltpu.VMEM((KV_HEADS, keys, LANES), BF16),
            pltpu.VMEM((KV_HEADS, keys, LANES), BF16),
            pltpu.VMEM((KV_HEADS, STACK, LANES), F32),
            pltpu.VMEM((KV_HEADS, STACK, LANES), F32),
            pltpu.VMEM((span, 16, LANES), BF16),
            pltpu.SemaphoreType.DMA((3 * span,)),
        ],
        compiler_params=params(52),
        cost_estimate=SMALL,
        name="attention_forward",
    )(meta, q, top, *kvs, info, seg)


def backward_kernel(
    meta_ref, q_ref, da_ref, att_ref, lse_ref, cos_ref, sin_ref, *refs, tiles, span, heads
):
    first_head, groups = heads
    kv_refs = refs[:span]
    info_ref, seg_ref, dq_ref, near_ref, far_ref, key, val, dkv, dq, qd, lifted, sems = refs[span:]
    rows = q_ref.shape[1]
    block = meta_ref[0]
    copies = gather_keys(block, kv_refs, key, sems, pl.ds(first_head, groups))
    for copy in copies:
        copy.start()

    def clear(n, _):
        dkv[:, pl.ds(n * BK, BK), :] = jnp.zeros((groups, BK, LANES), F32)
        return 0

    lax.fori_loop(0, key.shape[1] // BK, clear, 0)
    for copy in copies:
        copy.wait()
    split_keys(key, key, val)
    lane = lane_iota((BQ, LANES))
    left = lane < HEAD

    def lanes_of(column, first):
        out = jnp.zeros((BQ, LANES), F32)
        for k in range(3):
            top = column.astype(BF16).astype(F32)
            out = jnp.where(lane == first + k, top, out)
            column = column - top
        return out

    def q_loop(i, _):
        at = pl.ds(pl.multiple_of(i * BQ, BQ), BQ)
        dq[...] = jnp.zeros_like(dq)
        logs = lse_ref[at, :] * (-1.0 / SCALE2)
        for h in range(first_head * GROUP, (first_head + groups) * GROUP):
            g, r = h // GROUP - first_head, h % GROUP
            column = h // 2 * LANES
            da = da_ref[at, column : column + LANES].astype(F32)
            delta = da * att_ref[at, column : column + LANES].astype(F32)
            mine = left if h % 2 == 0 else jnp.logical_not(left)
            delta = jnp.sum(jnp.where(mine, delta, 0.0), axis=1, keepdims=True)
            if h % 2 == 0:
                da = pltpu.roll(da, HEAD, 1)
            q = q_ref[h, at, :]
            own = slice(r * BQ, (r + 1) * BQ)
            other = slice(STACK + r * BQ, STACK + (r + 1) * BQ)
            qd[g, own, :] = q
            qd[g, other, :] = jnp.where(left, 0.0, da).astype(BF16)
            lse = lanes_of(logs[:, h : h + 1], HEAD)
            lifted[g, own, :] = jnp.where(left, q.astype(F32), lse).astype(BF16)
            lifted[g, other, :] = jnp.where(left, lanes_of(-delta, 0), da).astype(BF16)

        def fold(g, spots, bias):
            keys = key_pair(key, g, spots)
            s = dot_tr(lifted[g, :STACK, :], keys)
            p = jnp.exp2(s * SCALE2 if bias is None else masked(s, bias))
            ds = (p * dot_tr(lifted[g, STACK:, :], key_pair(val, g, spots))).astype(BF16)
            p = p.astype(BF16)
            dq[g] += dot(ds, keys)
            moved = dot_cc(jnp.concatenate([ds, p], axis=0), qd[g])
            for n, (first, _) in enumerate(spots):
                dkv[g, pl.ds(first, BK), :] += moved[n * BK : (n + 1) * BK]

        count = meta_ref[1 + i]
        free = open_tiles(meta_ref, i)

        def open_loop(t, _):
            spots = tile_pair(meta_ref, tiles, i, 2 * t)
            for g in range(groups):
                fold(g, spots, None)
            return 0

        lax.fori_loop(0, free // 2, open_loop, 0)

        def k_loop(t, _):
            spots = tile_pair(meta_ref, tiles, i, free + 2 * t)
            bias = mask_bias(info_ref, seg_ref, i, spots)
            for g in range(groups):
                fold(g, spots, bias)
            return 0

        lax.fori_loop(0, (count - free + 1) // 2, k_loop, 0)
        cos = cos_ref[at, :]
        sin = sin_ref[at, :]
        low = (lane % HEAD) < HEAD // 2
        for g in range(groups):
            for pair in range(GROUP // 2):
                first = dq[g, 2 * pair * BQ : (2 * pair + 1) * BQ]
                second = dq[g, (2 * pair + 1) * BQ : (2 * pair + 2) * BQ]
                z = jnp.where(left, first, pltpu.roll(second, HEAD, 1)) * SCALE
                z = z * cos - half_turn(z, low) * sin
                column = (g * GROUP // 2 + pair) * LANES
                dq_ref[at, column : column + LANES] = z.astype(BF16)
        return 0

    lax.fori_loop(0, rows // BQ, q_loop, 0)
    factor = jnp.where(lane < HEAD, SCALE, 1.0)
    for e in range(span):
        target = near_ref if e % 2 == 0 else far_ref
        for half in range(2):
            first = first_row(block ^ e, half, rows, span)

            def leave(n, _):
                at = pl.ds(pl.multiple_of(half * (rows // 2) + n * BQ, BQ), BQ)
                source = pl.ds(pl.multiple_of(first + n * BQ, BQ), BQ)
                for g in range(groups):
                    target[e // 2, g, at, :] = (dkv[g, source, :] * factor).astype(BF16)
                return 0

            lax.fori_loop(0, rows // 2 // BQ, leave, 0)


def attention_backward(heads, meta, q, da, att, lse, cos, sin, kvs, info, seg):
    rows = q.shape[1]
    span = len(kvs)
    keys = span * rows
    tiles = keys // BK
    groups = heads[1]
    return pl.pallas_call(
        functools.partial(backward_kernel, tiles=tiles, span=span, heads=heads),
        out_shape=[
            jax.ShapeDtypeStruct((rows, groups * GROUP * HEAD), BF16),
            jax.ShapeDtypeStruct((span // 2, groups, rows, LANES), BF16),
            jax.ShapeDtypeStruct((span // 2, groups, rows, LANES), BF16),
        ],
        in_specs=[SMEM_SPACE] + [VMEM_SPACE] * 6 + [ANY_SPACE] * span + [VMEM_SPACE] * 2,
        out_specs=[VMEM_SPACE] * 3,
        scratch_shapes=[
            pltpu.VMEM((groups, keys, LANES), BF16),
            pltpu.VMEM((groups, keys, LANES), BF16),
            pltpu.VMEM((groups, keys, LANES), F32),
            pltpu.VMEM((groups, STACK, LANES), F32),
            pltpu.VMEM((groups, 2 * STACK, LANES), BF16),
            pltpu.VMEM((groups, 2 * STACK, LANES), BF16),
            pltpu.SemaphoreType.DMA((2 * span,)),
        ],
        compiler_params=params(56),
        cost_estimate=SMALL,
        name="attention_backward",
    )(meta, q, da, att, lse, cos, sin, *kvs, info, seg)


def middle_kernel(place_ref, x_ref, att_ref, gain_ref, *refs):
    piece_refs, (mid_ref, n_ref, w_ref, sems) = refs[:-4], refs[-4:]
    for copy in assembly(place_ref, piece_refs, w_ref, sems):
        copy.wait()
    mid_ref[...] = dot_tr(att_ref[...], w_ref[...])
    gain2 = gain_ref[1:2, :]

    def norm(i, _):
        at = pl.ds(pl.multiple_of(i * BQ, BQ), BQ)
        mid = x_ref[at, :].astype(F32) + mid_ref[at, :]
        scale = lax.rsqrt(jnp.mean(mid * mid, axis=1, keepdims=True) + EPSILON)
        mid_ref[at, :] = mid
        n_ref[at, :] = (mid * scale * gain2).astype(BF16)
        return 0

    lax.fori_loop(0, mid_ref.shape[0] // BQ, norm, 0)


def middle(x, att, gains, pieces, place):
    rows = x.shape[0]
    count = sum(p.shape[0] for p in pieces)
    return pl.pallas_call(
        middle_kernel,
        out_shape=[
            jax.ShapeDtypeStruct((rows, D), F32),
            jax.ShapeDtypeStruct((rows, D), BF16),
            jax.ShapeDtypeStruct((D, D), BF16),
        ],
        in_specs=[SMEM_SPACE] + [VMEM_SPACE] * 3 + [ANY_SPACE] * len(pieces),
        out_specs=[VMEM_SPACE] * 3,
        scratch_shapes=[pltpu.SemaphoreType.DMA((count,))],
        compiler_params=params(32),
        name="middle",
    )(place, x, att, gains, *pieces)


def feed_forward_kernel(
    n1_ref, n2_ref, og1_ref, og2_ref, wg_ref, wu_ref, wd_ref, *refs, later
):
    priors, refs = refs[: 2 * later], refs[2 * later :]
    own_ref, far_ref, dw_ref, nt, ogt, oacc, nacc, hid, dgate, dup, sems = refs
    f = pl.program_id(0)
    part = pl.program_id(1)
    rows = n1_ref.shape[0]
    copies = [
        pltpu.make_async_copy(prior, target, sems.at[k])
        for k, (prior, target) in enumerate(zip(priors, (own_ref, far_ref)))
    ]

    @pl.when((f == 0) & (part == 0))
    def _():
        for copy in copies:
            copy.start()
        nt[:, :rows] = n1_ref[...].T
        nt[:, rows:] = n2_ref[...].T
        ogt[:, :rows] = og1_ref[...].T
        ogt[:, rows:] = og2_ref[...].T
        oacc[...] = jnp.zeros_like(oacc)
        nacc[...] = jnp.zeros_like(nacc)

    @pl.when(part == 0)
    def _():
        for k, (n_ref, og_ref) in enumerate(((n1_ref, og1_ref), (n2_ref, og2_ref))):
            at = slice(k * rows, (k + 1) * rows)
            gate = dot(n_ref[...], wg_ref[...])
            up = dot(n_ref[...], wu_ref[...])
            grad = dot(og_ref[...], wd_ref[...])
            sig = jax.nn.sigmoid(gate)
            silu = gate * sig
            hid[at] = (silu * up).astype(BF16)
            dgate[at] = (grad * up * sig * (1.0 + gate * (1.0 - sig))).astype(BF16)
            dup[at] = (grad * silu).astype(BF16)
        dw_ref[...] = dot(nt[...], dgate[...]).astype(BF16)

    @pl.when(part == 1)
    def _():
        nacc[...] += dot_tr(dgate[...], wg_ref[...]) + dot_tr(dup[...], wu_ref[...])
        dw_ref[...] = dot(nt[...], dup[...]).astype(BF16)

    @pl.when(part == 2)
    def _():
        oacc[...] += dot_tr(hid[...], wd_ref[...])
        dw_ref[...] = dot(ogt[...], hid[...]).astype(BF16)

    @pl.when((f == pl.num_programs(0) - 1) & (part == 2))
    def _():
        for copy in copies:
            copy.wait()
        for k, target in enumerate((own_ref, far_ref)):
            for side, acc in enumerate((oacc, nacc)):
                total = acc[k * rows : (k + 1) * rows]
                if later:
                    total = total + target[side].astype(F32)
                target[side] = total.astype(BF16)


def feed_forward(steps, n_own, n_far, og_own, og_far, w, priors=()):
    rows = n_own.shape[0]
    block = FF_BLOCK
    whole = pl.BlockSpec((rows, D), lambda f, k: (0, 0), pipeline_mode=pl.Buffered(1))
    sides = pl.BlockSpec((2, rows, D), lambda f, k: (0, 0, 0))
    slab = [pl.BlockSpec((D, block), lambda f, k, m=m: (0, m * steps + f)) for m in range(3)]
    return pl.pallas_call(
        functools.partial(feed_forward_kernel, later=bool(priors)),
        grid=(steps, 3),
        in_specs=[whole] * 4 + slab + [ANY_SPACE] * len(priors),
        out_specs=[sides, sides, pl.BlockSpec((D, block), lambda f, k: (0, k * steps + f))],
        out_shape=[
            jax.ShapeDtypeStruct((2, rows, D), BF16),
            jax.ShapeDtypeStruct((2, rows, D), BF16),
            jax.ShapeDtypeStruct((D, 3 * steps * block), BF16),
        ],
        scratch_shapes=[
            pltpu.VMEM((D, 2 * rows), BF16),
            pltpu.VMEM((D, 2 * rows), BF16),
            pltpu.VMEM((2 * rows, D), F32),
            pltpu.VMEM((2 * rows, D), F32),
            pltpu.VMEM((2 * rows, block), BF16),
            pltpu.VMEM((2 * rows, block), BF16),
            pltpu.VMEM((2 * rows, block), BF16),
            pltpu.SemaphoreType.DMA((2,)),
        ],
        compiler_params=params(62),
        cost_estimate=SMALL,
        name="feed_forward",
    )(n_own, n_far, og_own, og_far, w, w, w, *priors)


def turn_kernel(
    mid_ref, own_ref, got_ref, og_ref, gain_ref, w_ref, att_ref,
    out_ref, gm_ref, da_ref, dw_ref, dgain_ref, gmb,
):
    gain2 = gain_ref[1:2, :]

    def step(i, dgain):
        at = pl.ds(pl.multiple_of(i * BQ, BQ), BQ)
        mid = mid_ref[at, :]
        out = mid + (own_ref[0, at, :].astype(F32) + got_ref[0, at, :].astype(F32))
        out_ref[at, :] = out.astype(BF16)
        dn = own_ref[1, at, :].astype(F32) + got_ref[1, at, :].astype(F32)
        scale = lax.rsqrt(jnp.mean(mid * mid, axis=1, keepdims=True) + EPSILON)
        dgain = dgain + jnp.sum((dn * mid * scale).reshape(BQ // 8, 8, D), axis=0)
        q2 = dn * gain2
        mean = jnp.mean(q2 * mid, axis=1, keepdims=True)
        gm = og_ref[at, :].astype(F32) + scale * q2 - mid * (scale * scale * scale * mean)
        gm_ref[at, :] = gm
        gmb[at, :] = gm.astype(BF16)
        return dgain

    dgain = lax.fori_loop(0, mid_ref.shape[0] // BQ, step, jnp.zeros((8, D), F32))
    dgain_ref[...] = dgain
    da_ref[...] = dot(gmb[...], w_ref[...]).astype(BF16)
    dw_ref[...] = dot_cc(gmb[...], att_ref[...]).astype(BF16)


def turn(mid, own, got, og, gains, w, att):
    rows = mid.shape[0]
    return pl.pallas_call(
        turn_kernel,
        out_shape=[
            jax.ShapeDtypeStruct((rows, D), BF16),
            jax.ShapeDtypeStruct((rows, D), F32),
            jax.ShapeDtypeStruct((rows, D), BF16),
            jax.ShapeDtypeStruct((D, D), BF16),
            jax.ShapeDtypeStruct((8, D), F32),
        ],
        scratch_shapes=[pltpu.VMEM((rows, D), BF16)],
        compiler_params=params(56),
        name="turn",
    )(mid, own, got, og, gains, w, att)


def project_back_kernel(
    x_ref, n_ref, dqa_ref, dqb_ref, ka_refs, kb_refs, w_ref, dgain_ref,
    cos_ref, sin_ref, dn_ref, dw_ref, dz,
):
    rows = x_ref.shape[0]
    lane = lane_iota((BQ, LANES))
    low = (lane % HEAD) < HEAD // 2
    left = lane < HEAD
    first = dqa_ref.shape[1] // (GROUP * HEAD)

    def turn_back(i, _):
        at = pl.ds(pl.multiple_of(i * BQ, BQ), BQ)
        cos = cos_ref[at, :]
        sin = sin_ref[at, :]
        for g in range(KV_HEADS):
            refs, k, dq_ref = (ka_refs, g, dqa_ref) if g < first else (kb_refs, g - first, dqb_ref)
            z = sum(ref[k, at, :].astype(F32) for ref in refs)
            rot = z * cos - half_turn(z, low) * sin
            base = g * GROUP_COLS
            span = GROUP * HEAD
            dz[at, base : base + span] = dq_ref[at, k * span : (k + 1) * span]
            dz[at, base + span : base + span + LANES] = jnp.where(left, rot, z).astype(BF16)
        return 0

    lax.fori_loop(0, rows // BQ, turn_back, 0)
    dw_ref[:, :QKV] = dot_cc(n_ref[...], dz[...]).astype(BF16)
    dn_ref[...] = dot_tr(dz[...], w_ref[:, :QKV])

    def step(i, dgain):
        at = pl.ds(pl.multiple_of(i * BQ, BQ), BQ)
        x = x_ref[at, :].astype(F32)
        scale = lax.rsqrt(jnp.mean(x * x, axis=1, keepdims=True) + EPSILON)
        return dgain + jnp.sum((dn_ref[at, :] * x * scale).reshape(BQ // 8, 8, D), axis=0)

    dgain1 = lax.fori_loop(0, rows // BQ, step, jnp.zeros((8, D), F32))
    dgain1 = jnp.sum(dgain1, axis=0, keepdims=True)
    dgain2 = jnp.sum(dgain_ref[...], axis=0, keepdims=True)
    row = lax.broadcasted_iota(jnp.int32, (LANES, D), 0)
    both = jnp.where(row == 0, dgain1, jnp.where(row == 1, dgain2, 0.0))
    dw_ref[:, QKV:] = both.T.astype(BF16)


def project_back(x, n, dqs, pieces, w, dgain, cos, sin):
    rows = x.shape[0]

    def kernel(x_ref, n_ref, dqa_ref, dqb_ref, *refs):
        count = len(pieces[0])
        return project_back_kernel(
            x_ref, n_ref, dqa_ref, dqb_ref, refs[:count], refs[count : 2 * count],
            *refs[2 * count :],
        )

    return pl.pallas_call(
        kernel,
        out_shape=[
            jax.ShapeDtypeStruct((rows, D), F32),
            jax.ShapeDtypeStruct((D, QKV_PAD), BF16),
        ],
        scratch_shapes=[pltpu.VMEM((rows, QKV), BF16)],
        compiler_params=params(48),
        name="project_back",
    )(x, n, *dqs, *pieces[0], *pieces[1], w, dgain, cos, sin)


def input_grad_kernel(x_ref, gm_ref, dn_ref, gain_ref, in_ref):
    x = x_ref[...].astype(F32)
    scale = lax.rsqrt(jnp.mean(x * x, axis=1, keepdims=True) + EPSILON)
    q1 = dn_ref[...] * gain_ref[0:1, :]
    mean = jnp.mean(q1 * x, axis=1, keepdims=True)
    in_ref[...] = gm_ref[...] + scale * q1 - x * (scale * scale * scale * mean)


def input_gradient(x, gm, dn, gains):
    rows = x.shape[0]
    block = pl.BlockSpec((BQ, D), lambda i: (i, 0))
    return pl.pallas_call(
        input_grad_kernel,
        grid=(rows // BQ,),
        in_specs=[block] * 3 + [pl.BlockSpec((8, D), lambda i: (0, 0))],
        out_specs=block,
        out_shape=jax.ShapeDtypeStruct((rows, D), F32),
        compiler_params=params(32),
        cost_estimate=SMALL,
        name="input_gradient",
    )(x, gm, dn, gains)


def body(
    layer_in, out_grad, segment_ids, segment_parents, norm_gain1, w_query, w_key, w_value, w_output,
    norm_gain2, w_gate, w_up, w_down,
):
    size = lax.axis_size("fsdp")
    rows = layer_in.shape[0]
    span = TREE // rows
    shard = D // size
    me = lax.axis_index("fsdp")
    block = me % span
    tree = me // span
    core = me % 2

    def swap(v, bit):
        return lax.ppermute(v, "fsdp", [(i, i ^ bit) for i in range(size)])

    same_core = [list(range(c, size, 2)) for c in range(2)]

    trees = size // span
    chips = span // 2
    chip = block // 2

    def stage(*values):
        return lax.optimization_barrier(values)

    def half_columns(*halves):
        keep = jnp.where(core == 0, halves[0], halves[1])
        got = swap(jnp.where(core == 0, halves[1], halves[0]), 1)
        return jnp.where(
            core == 0, jnp.concatenate([keep, got], axis=0), jnp.concatenate([got, keep], axis=0)
        )

    def part(v, index, axis):
        return lax.dynamic_index_in_dim(v, index, axis, keepdims=False)

    def send_cores(grad):
        grad = grad.reshape(trees, chips, 2, shard, grad.shape[1])
        return part(grad, core, 2), swap(part(grad, 1 - core, 2), 1)

    def send_chips(total):
        return part(total, chip, 1), *(swap(part(total, chip ^ c, 1), 2 * c) for c in range(1, chips))

    def send_trees(total):
        if trees > 4:
            across = [list(range(k, size, span)) for k in range(span)]
            total = lax.psum_scatter(total, "fsdp", axis_index_groups=across)
            return (total.reshape(total.shape[-2:]),)
        return part(total, tree, 0), *(
            swap(part(total, tree ^ t, 0), span * t) for t in range(1, trees)
        )

    def halve(v, bit, axis, distance):
        return part(v, bit, axis), swap(part(v, 1 - bit, axis), distance)

    def trees_first(v):
        if trees != 4:
            return (v,)
        return halve(v.reshape(2, 2, *v.shape[1:]), tree // 2, 0, 2 * span)

    def trees_second(v):
        return halve(v, tree % 2, 0, span) if trees == 4 else send_trees(v)

    def add(terms):
        return sum((t.astype(F32) for t in terms[1:]), terms[0].astype(F32))

    def add16(terms):
        return add(terms).astype(BF16)

    def even_out(v):
        return jnp.concatenate([v[: rows // 2], swap(v[rows // 2 :], span - 1).astype(v.dtype)])

    turned = w_output.T
    grouped = [w_query.reshape(shard, KV_HEADS, GROUP * HEAD)]
    grouped += [w.reshape(shard, KV_HEADS, HEAD) for w in (w_key, w_value)]
    grouped = jnp.concatenate(grouped, axis=2).reshape(shard, QKV)
    gain_pair = jnp.stack([norm_gain1, norm_gain2], axis=1)
    gain_pair = jnp.pad(gain_pair, ((0, 0), (0, LANES - 2)))
    grouped = jnp.concatenate([grouped, gain_pair], axis=1)

    def columns(c):
        parts = [grouped[:, c * QKV_PAD // 2 : (c + 1) * QKV_PAD // 2]]
        first = c * HALF
        for k, count in enumerate(FF_STEPS):
            last = first + count * FF_BLOCK
            parts += [w[:, first:last] for w in (w_gate, w_up, down)]
            if k == 0:
                parts += [turned[:, c * D // 2 : (c + 1) * D // 2]]
            first = last
        return jnp.concatenate(parts, axis=1)

    down = w_down.T
    chip_rows = half_columns(columns(0), columns(1))
    first, ff_w = QKV_PAD // 2, []
    for k, count in enumerate(FF_STEPS):
        last = first + 3 * count * FF_BLOCK + (D // 2 if k == 0 else 0)
        ff_w += [
            lax.all_gather(
                chip_rows[:, first:last], "fsdp", tiled=True, axis_index_groups=same_core
            )
        ]
        first = last
    qkv_rows = chip_rows[:, : QKV_PAD // 2]
    if trees > 4:
        qkv_rows = lax.all_gather(qkv_rows, "fsdp", tiled=True, axis_index_groups=same_core)[None]
        qkv_pieces, order = [qkv_rows], jnp.zeros((1,), jnp.int32)
    else:
        qkv_rows = jnp.stack([qkv_rows] + [swap(qkv_rows, span * t) for t in range(1, trees)])
        qkv_pieces = [qkv_rows] + [swap(qkv_rows, 2 * c) for c in range(1, chips)]
        order = [(tree ^ t) * chips + (chip ^ c) for c in range(chips) for t in range(trees)]
        order = jnp.stack(order)
    qkv_place = jnp.stack([core] * len(qkv_pieces) + [1 - core] * len(qkv_pieces))
    qkv_place = jnp.concatenate([qkv_place, order, order])
    qkv_pieces = qkv_pieces + [swap(p, 1) for p in qkv_pieces]

    tree_seg = segment_ids
    bit = 1
    while bit < span:
        other = swap(tree_seg, bit)
        first = (me & bit) == 0
        tree_seg = jnp.concatenate(
            [jnp.where(first, tree_seg, other), jnp.where(first, other, tree_seg)], axis=0
        )
        bit *= 2
    layer_in, tree_seg = stage(layer_in, tree_seg)
    tokens_in = even_out(layer_in)
    seg_count = segment_parents.shape[0] * span // size
    seg_base = tree * seg_count
    tree_seg = tree_seg - seg_base
    starts = [first_row(block, half, rows, span) for half in range(2)]
    own_row = jnp.concatenate([n + jnp.arange(rows // 2, dtype=jnp.int32) for n in starts])
    own_seg = jnp.concatenate(
        [lax.dynamic_slice_in_dim(tree_seg, n, rows // 2) for n in starts]
    )
    ids = jnp.arange(seg_count, dtype=jnp.int32)
    parent = lax.dynamic_slice_in_dim(segment_parents, seg_base, seg_count) - seg_base

    def look(index, table):
        return jnp.sum(jnp.where(index[:, None] == ids[None, :], table[None, :], 0), axis=1)

    grand = look(parent, parent)
    lengths = jnp.sum((tree_seg[None, :] == ids[:, None]).astype(jnp.int32), axis=1)
    starts = jnp.sum(jnp.where(ids[None, :] < ids[:, None], lengths[None, :], 0), axis=1)
    depth = jnp.where(parent != ids, look(parent, lengths), 0)
    depth = depth + jnp.where(grand != parent, look(grand, lengths), 0)
    positions = (look(own_seg, depth - starts) + own_row).astype(F32)
    lane = jnp.arange(LANES, dtype=jnp.int32)
    inverse = jnp.exp((lane % 32).astype(F32) * (-2.0 * math.log(ROPE_BASE) / HEAD))
    angles = positions[:, None] * inverse[None, :]
    cos = jnp.cos(angles)
    sin = jnp.sin(angles) * jnp.where(lane % HEAD < HEAD // 2, -1.0, 1.0)[None, :]
    info = [own_seg, look(own_seg, parent), look(own_seg, grand), own_row]
    info = sum(jnp.where(lane[None, :] == c, v[:, None], 0) for c, v in enumerate(info))
    tiles = TREE // BK
    steps = rows // BQ
    tile_seg = tree_seg.reshape(tiles, BK)
    tile_first, tile_last = tile_seg[:, 0], tile_seg[:, -1]
    step_seg = own_seg.reshape(steps, BQ)

    def inside(s):
        return (tile_first[None, :] <= s[:, None]) & (s[:, None] <= tile_last[None, :])

    hit = inside(ids) | inside(parent) | inside(grand)
    here = (step_seg[:, :1] <= ids[None, :]) & (ids[None, :] <= step_seg[:, -1:])
    active = jnp.any(here[:, :, None] & hit[None, :, :], axis=1)
    tile_range = jnp.arange(tiles, dtype=jnp.int32)
    last_row = own_row.reshape(steps, BQ)[:, -1]
    active = active & (tile_range[None, :] * BK <= last_row[:, None])
    before = tile_range[:, None] < tile_range[None, :]
    place = jnp.sum((active[:, :, None] & before[None]).astype(jnp.int32), axis=1)
    barred = (ids[None, :] != ids[:, None]) & (ids[None, :] != parent[:, None])
    barred = barred & (ids[None, :] != grand[:, None])
    tile_has = (tile_first[:, None] <= ids[None, :]) & (ids[None, :] <= tile_last[:, None])
    barred = jnp.any(barred[:, None, :] & tile_has[None, :, :], axis=2)
    barred = jnp.any(here[:, :, None] & barred[None, :, :], axis=1)
    whole = active & ~barred & ((tile_range[None, :] + 1) * BK <= last_row[:, None] - BQ + 1)
    whole_count = jnp.sum(whole.astype(jnp.int32), axis=1)
    rank = jnp.sum((whole[:, :, None] & before[None]).astype(jnp.int32), axis=1)
    place = jnp.where(whole, rank, whole_count[:, None] + place - rank)
    chosen = active[:, :, None] & (place[:, :, None] == tile_range[None, None, :])
    listed = jnp.sum(jnp.where(chosen, tile_range[None, :, None], 0), axis=1)
    counts = jnp.sum(active.astype(jnp.int32), axis=1)
    counts = [jnp.pad(v, (0, BQ // 2 - steps)) for v in (counts, whole_count)]
    meta = jnp.concatenate([block[None], *counts, listed.reshape(steps * tiles)])
    seg_row = tree_seg[None, :]

    normed1, kv, gains, qkv_w = project_keys(qkv_place, tokens_in, cos, sin, qkv_pieces)
    kv_near = swap(kv, 1)
    kv_far = [swap(kv, 2 * c) for c in range(1, chips)]
    q, q_top = project_queries(normed1, qkv_w, cos, sin)
    q, kv_near, *kv_far = stage(q, kv_near, *kv_far)
    kvs = [kv, kv_near]
    for piece in kv_far:
        kvs += [piece, swap(piece, 1)]
    out_grad, q, *kvs = stage(out_grad, q, *kvs)
    grads_in = even_out(out_grad)
    att, lse = attention_forward(meta, q, q_top, kvs, info, seg_row)
    att, grads_in = stage(att, grads_in)
    og_far = swap(grads_in, 1)
    att, ff_w[0] = stage(att, ff_w[0])
    out_w = ff_w[0][None, :, 3 * FF_STEPS[0] * FF_BLOCK :]
    out_place = jnp.stack([core, 1 - core, 0, 0])
    mid, normed2, out_w = middle(tokens_in, att, gains, [out_w, swap(out_w, 1)], out_place)
    normed2_far = swap(normed2, 1)
    tokens = (normed2, normed2_far, grads_in, og_far)
    *sums, next_dw = feed_forward(FF_STEPS[0], *tokens, ff_w[0])
    next_dw = send_chips(next_dw.reshape(trees, chips, 2 * shard, next_dw.shape[1]))
    ff_w[1], *sums = stage(ff_w[1], *sums)
    *sums, ff_dw = feed_forward(FF_STEPS[1], *tokens, ff_w[1], sums)
    ff_dw = lax.psum_scatter(
        ff_dw, "fsdp", scatter_dimension=0, tiled=True, axis_index_groups=same_core
    )
    own, far = sums
    layer_out, grad_mid, da, out_dw, dgain2 = turn(
        mid, own, swap(far, 1), grads_in, gains, out_w, att
    )

    def backward(n, meta):
        return attention_backward(
            HEAD_PARTS[n], meta, q, da, att, lse, cos, sin, kvs, info, seg_row
        )

    def meet(near, far):
        got = swap(far, 1)
        return [near[0], got[0]], [add16((near[c], got[c])) for c in range(1, chips)]

    chip_x, chip_y = chip % 2, chip // 2
    out_dw = send_cores(out_dw)
    layer_out = even_out(layer_out)
    dq_a, near, far = backward(0, meta)
    near, far, dq_a, layer_out, *values = stage(near, far, dq_a, layer_out, *out_dw, *next_dw)
    out_dw, next_dw = add16(values[:2]), add16(values[2:])
    pieces_a, both = meet(near, far)
    meta, out_dw, next_dw, *both = stage(meta, out_dw, next_dw, *both)
    both = [swap(v, 2 * c + 2) for c, v in enumerate(both)]
    out_dw = halve(out_dw.reshape(trees, 2, 2, shard, D), chip_x, 2, 2)
    next_dw = trees_first(next_dw)
    dq_b, near, far = backward(1, meta)
    near, far, dq_b, *values = stage(near, far, dq_b, *both, *out_dw, *next_dw)
    pieces_a += values[: len(both)]
    values = values[len(both) :]
    out_dw, next_dw = add16(values[:2]), add16(values[2:])
    pieces_b, both = meet(near, far)
    out_dw, next_dw, *both = stage(out_dw, next_dw, *both)
    pieces_b += [swap(v, 2 * c + 2) for c, v in enumerate(both)]
    out_dw = halve(out_dw, chip_y, 1, 4)
    next_dw = trees_second(next_dw)
    pieces_b[-1], *next_dw = stage(pieces_b[-1], *next_dw)
    dn, qkv_dw = project_back(
        tokens_in, normed1, (dq_a, dq_b), (pieces_a, pieces_b), qkv_w, dgain2, cos, sin
    )
    qkv_dw = send_cores(qkv_dw)
    dn, *values = stage(dn, *out_dw, *next_dw, *qkv_dw)
    out_dw, values = add16(values[:2]), values[2:]
    next_dw, qkv_dw = add16(values[: len(next_dw)]), add16(values[len(next_dw) :])
    qkv_dw = send_chips(qkv_dw)
    ff_dw = jnp.concatenate([next_dw, ff_dw], axis=1).reshape(2, shard, -1)
    ff_dw = halve(ff_dw, core, 0, 1)
    out_dw = trees_first(out_dw)
    input_grad = input_gradient(tokens_in, grad_mid, dn, gains)
    input_grad, *values = stage(input_grad, *ff_dw, *out_dw, *qkv_dw)
    (keep, got), values = values[:2], values[2:]
    out_dw, qkv_dw = add16(values[: len(out_dw)]), add16(values[len(out_dw) :])
    out_dw, qkv_dw = trees_second(out_dw), send_trees(qkv_dw)
    travelled = swap(input_grad[rows // 2 :].astype(BF16), span - 1)
    input_grad = jnp.concatenate([input_grad[: rows // 2], travelled.astype(F32)])
    out_dw, qkv_dw = add(out_dw), add(qkv_dw)

    groups = qkv_dw[:, :QKV].reshape(shard, KV_HEADS, GROUP_COLS)
    grad_query = groups[:, :, : GROUP * HEAD].reshape(shard, HEADS * HEAD)
    grad_key = groups[:, :, GROUP * HEAD : GROUP * HEAD + HEAD].reshape(shard, KV_HEADS * HEAD)
    grad_value = groups[:, :, GROUP * HEAD + HEAD :].reshape(shard, KV_HEADS * HEAD)

    grads = [[], [], []]
    for c in range(2):
        half = jnp.where(core == c, keep, got).astype(F32)
        first = 0
        for steps in FF_STEPS:
            for grad in grads:
                last = first + steps * FF_BLOCK
                grad.append(half[:, first:last])
                first = last
    ff_grads = [jnp.concatenate(grad, axis=1) for grad in grads]
    return (
        layer_out,
        input_grad,
        qkv_dw[:, QKV],
        grad_query,
        grad_key,
        grad_value,
        out_dw.T,
        qkv_dw[:, QKV + 1],
        ff_grads[0],
        ff_grads[1],
        ff_grads[2].T,
    )


def solution(mesh):
    rows, cols, flat = P("fsdp", None), P(None, "fsdp"), P("fsdp")
    return jax.shard_map(
        body,
        mesh=mesh,
        in_specs=(rows, rows, flat, P(), flat, rows, rows, rows, cols, flat, rows, rows, cols),
        out_specs=(rows, rows, flat, rows, rows, rows, cols, flat, rows, rows, cols),
        check_vma=False,
    )
```
